32 devices in a mesh: dp: 8 (over z, x), tensor: 4 (over y, core).
Axes of the slice: x: 2, y: 2, z: 4, core: 2. Of those that a mesh axis runs over, the one named last changes fastest.
Arguments:
- latent_tokens: bfloat16 [8, 1024, 1152], P('dp', None, 'tensor'), may hold values from -6 to 6
- timesteps: int32 [8], P('dp'), may hold values from 0 to 999, as said below
- labels: int32 [8], P('dp'), may hold values from 0 to 999
- class_table: bfloat16 [1000, 1152], replicated, may hold values from -6 to 6
- ada_weight: bfloat16 [1152, 6, 1152], P(None, None, 'tensor'), may hold values from -0.1875 to 0.1875
- ada_bias: bfloat16 [6, 1152], P(None, 'tensor'), may hold values from -4 to 4
- query_key_value_weight: bfloat16 [1152, 3, 1152], P(None, None, 'tensor'), may hold values from -0.1875 to 0.1875
- gate_weight: bfloat16 [1152, 16], P(None, 'tensor'), may hold values from -0.1875 to 0.1875
- gate_bias: bfloat16 [16], P('tensor'), may hold values from 1 to 7
- conv_weight: bfloat16 [3, 3, 1152], P(None, None, 'tensor'), may hold values from -5 to 5
- out_weight: bfloat16 [1152, 1152], P('tensor'), may hold values from -0.0014648438 to 0.0014648438
- up_weight: bfloat16 [1152, 4608], P(None, 'tensor'), may hold values from -0.23570226 to 0.23570226
- down_weight: bfloat16 [4608, 1152], P('tensor'), may hold values from -0.09375 to 0.09375
- cotangent: bfloat16 [8, 1024, 1152], P('dp', None, 'tensor'), may hold values from -6 to 6
Outputs:
- layer_out: bfloat16 [8, 1024, 1152], P('dp', None, 'tensor')
- grad_tokens: float32 [8, 1024, 1152], P('dp', None, 'tensor')
- grad_class: float32 [1000, 1152], P(None, 'dp')
- grad_ada_w: float32 [1152, 6, 1152], P('dp', None, 'tensor')
- grad_ada_b: float32 [6, 1152], P(None, 'tensor')
- grad_qkv: float32 [1152, 3, 1152], P('dp', None, 'tensor')
- grad_gate_w: float32 [1152, 16], P('dp', 'tensor')
- grad_gate_b: float32 [16], P('tensor')
- grad_conv: float32 [3, 3, 1152], P(None, None, 'tensor')
- grad_out_w: float32 [1152, 1152], P('tensor', 'dp')
- grad_up: float32 [1152, 4608], P('dp', 'tensor')
- grad_down: float32 [4608, 1152], P('tensor', 'dp')
The draws below stay inside these ranges and needn't reach their ends.
Inputs may be any that keep to these rules, and one draw needn't show every extreme that they name: `timesteps`: timesteps per latent, smaller ones more common; every draw holds both ends of the range.
All inputs are finite; a program needn't handle non-finite values.
Results may differ from the reference program's by a relative error of at most 0.012.
The reference program's roundings to bfloat16 on the way count: a program that leaves them out, or rounds other values in their place, can miss the bound.
Values may be sent and summed in bfloat16 or wider, within the bound.
A program may use at most 192 MiB of HBM per device.

```python
import math
import jax
import jax.numpy as jnp
from jax import lax

MODEL_DIM = 1152
H = 16
HD = 72
FF = 4608
NCLASS = 1000
NSTEPS = 1000
GRID = 32
CH = 64
LATENTS = 8


def draw_timesteps(key, part):
    key = jax.random.fold_in(key, 11)
    key_one, key_two, key_three, key_four = jax.random.split(key, 4)
    uniform_one = jax.random.randint(key_one, (LATENTS,), 0, NSTEPS)
    uniform_two = jax.random.randint(key_two, (LATENTS,), 0, NSTEPS)
    skewed = jnp.minimum(uniform_one, uniform_two)
    top_at = jax.random.randint(key_three, (), 0, LATENTS)
    bottom_at = (top_at + 1 + jax.random.randint(key_four, (), 0, LATENTS - 1)) % LATENTS
    positions = jnp.arange(LATENTS)
    skewed = jnp.where(positions == top_at, NSTEPS - 1, skewed)
    return jnp.where(positions == bottom_at, 0, skewed).astype(jnp.int32)


def draw_up_weight(key, part):
    key = jax.random.fold_in(key, 23)
    noise_key, column_key = jax.random.split(key)
    column_part = jnp.clip(jax.random.normal(column_key, (1, FF), jnp.float32), -4.0, 4.0)
    entries = jnp.clip(jax.random.normal(noise_key, (MODEL_DIM, FF), jnp.float32), -6.0, 6.0)
    strength = 0.5
    return ((entries + strength * column_part) * MODEL_DIM ** (-0.5)).astype(jnp.bfloat16)


def set_ends(values, own_key, low, high):
    longest = values.shape.index(max(values.shape))
    spots = []
    for shift in (0, 1):
        where = [jax.random.randint(jax.random.fold_in(own_key, axis), (), 0, length) for axis, length in enumerate(values.shape)]
        where[longest] = (where[longest] + shift) % values.shape[longest]
        spots.append(tuple(where))
    return values.at[spots[0]].set(low).at[spots[1]].set(high)


def steps_of(key, dims, shards, smallest, largest):
    level = 1.0
    for dim, shards_of in shards:
        draws = jax.random.uniform(jax.random.fold_in(jax.random.fold_in(key, 6), dim), (shards_of,), jnp.float32, smallest / len(shards), largest / len(shards))
        level = level * jnp.repeat(jnp.exp(draws), dims[dim] // shards_of).reshape((-1,) + (1,) * (len(dims) - 1 - dim))
    return level


def bell_draw(stream_key, extent, spread, bound, pieces=(), held_as=jnp.bfloat16):
    values = jax.random.normal(stream_key, extent, jnp.float32) * spread
    if len(pieces) > 0:
        values = steps_of(stream_key, extent, pieces, -0.22, 0.18) * values
    return jnp.clip(values, min=-bound, max=bound).astype(held_as)


def setup_inputs(seed: int = 0) -> dict:
    splits = jax.random.split(jax.random.key(seed), 15)
    latent_tokens = bell_draw(splits[0], (LATENTS, GRID * GRID, MODEL_DIM), 1.0, 6.0, ((0, 8), (2, 4)))
    timesteps = draw_timesteps(jax.random.fold_in(splits[14], 71), 0)
    labels = set_ends(jax.random.randint(splits[2], (LATENTS,), 0, NCLASS), jax.random.fold_in(splits[2], 1), 0, NCLASS - 1).astype(jnp.int32)
    class_table = bell_draw(splits[3], (NCLASS, MODEL_DIM), 1.0, 6.0)
    ada_weight = bell_draw(splits[4], (MODEL_DIM, 6, MODEL_DIM), MODEL_DIM ** -0.5, 0.1875, ((2, 4),))
    ada_bias = bell_draw(splits[5], (6, MODEL_DIM), 0.3, 4.0, ((1, 4),))
    query_key_value_weight = bell_draw(splits[6], (MODEL_DIM, 3, MODEL_DIM), MODEL_DIM ** -0.5, 0.1875, ((2, 4),))
    gate_weight = bell_draw(splits[7], (MODEL_DIM, H), MODEL_DIM ** -0.5, 0.1875, ((1, 4),))
    gate_bias = jnp.clip(1.0 + 6.0 * jax.random.uniform(splits[8], (H,), jnp.float32) ** steps_of(splits[8], (H,), ((0, 4),), -0.2, 0.2), 1.0, 7.0).astype(jnp.bfloat16)
    conv_weight = bell_draw(splits[9], (3, 3, MODEL_DIM), 0.35, 5.0, ((2, 4),))
    out_weight = bell_draw(splits[10], (MODEL_DIM, MODEL_DIM), (16 * MODEL_DIM * GRID * GRID) ** -0.5, 0.0014648438, ((0, 4),))
    up_weight = draw_up_weight(jax.random.fold_in(splits[14], 71), 0)
    down_weight = bell_draw(splits[12], (FF, MODEL_DIM), FF ** -0.5, 0.09375, ((0, 4),))
    cotangent = bell_draw(splits[13], (LATENTS, GRID * GRID, MODEL_DIM), 1.0, 6.0, ((0, 8), (2, 4)))
    return dict(latent_tokens=latent_tokens, timesteps=timesteps, labels=labels, class_table=class_table, ada_weight=ada_weight, ada_bias=ada_bias, query_key_value_weight=query_key_value_weight, gate_weight=gate_weight, gate_bias=gate_bias, conv_weight=conv_weight, out_weight=out_weight, up_weight=up_weight, down_weight=down_weight, cotangent=cotangent)


TOP_PRECISION = lax.Precision.HIGHEST
norm_eps = 1e-06

@jax.custom_vjp
def reduced_input(v):
    return lax.optimization_barrier(v.astype(jnp.bfloat16)).astype(jnp.float32)

@jax.custom_vjp
def reduced_gradient(v):
    return v

def low_keep(v):
    return (reduced_input(v), None)

def low_pass(kept, grad):
    return (grad,)

def back_keep(v):
    return (v, None)

def back_low(kept, grad):
    return (reduced_input(grad),)
reduced_input.defvjp(low_keep, low_pass)
reduced_gradient.defvjp(back_keep, back_low)

def embed_time(time_steps, model_width):
    half_width = model_width // 2
    frequency = jnp.exp(-math.log(10000.0) * jnp.arange(half_width, dtype=jnp.float32) / half_width)
    angles = time_steps.astype(jnp.float32)[:, None] * frequency[None, :]
    return jnp.concatenate([jnp.cos(angles), jnp.sin(angles)], axis=1)

def normalize(rows, shift_row, scale_row):
    mean_row = lax.optimization_barrier(jnp.mean(rows, axis=-1, keepdims=True))
    var_row = lax.optimization_barrier(jnp.mean(rows * rows, axis=-1, keepdims=True)) - mean_row * mean_row
    return (rows - mean_row) * lax.rsqrt(var_row + norm_eps) * (1.0 + scale_row) + shift_row

def span_pass(running_state, block):
    query_matrix, key_matrix, value_matrix, log_forget = block
    block_len = log_forget.shape[1]
    decay_factors = jnp.cumsum(log_forget, axis=1)
    causal_mask = (jnp.arange(block_len)[:, None] >= jnp.arange(block_len)[None, :])[None]
    decay_gap = jnp.where(causal_mask, decay_factors[:, :, None] - decay_factors[:, None, :], 0.0)
    score_matrix = jnp.einsum('mkd,mld->mkl', query_matrix, key_matrix, precision=TOP_PRECISION)
    weighted_values = jnp.where(causal_mask, jnp.exp(decay_gap), 0.0) * score_matrix
    within_block_part = jnp.einsum('dps,dsh->dph', weighted_values, value_matrix, precision=TOP_PRECISION)
    across_block_part = jnp.einsum('ugm,ump->ugp', query_matrix * jnp.exp(decay_factors)[:, :, None], running_state, precision=TOP_PRECISION)
    final_decay = decay_factors[:, -1:]
    carried = key_matrix * jnp.exp(final_decay - decay_factors)[:, :, None]
    running_state = running_state * jnp.exp(final_decay)[:, :, None] + jnp.einsum('nje,njf->nef', carried, value_matrix, precision=TOP_PRECISION)
    return (running_state, within_block_part + across_block_part)

def gated_scan(query_matrix, key_matrix, value_matrix, log_forget, span):
    latents, length, head_count, head_dim = query_matrix.shape
    blocks = length // span

    def arrange(array):
        return array.reshape(latents, blocks, span, head_count, head_dim).transpose(1, 0, 3, 2, 4).reshape(blocks, latents * head_count, span, head_dim)
    log_blocks = log_forget.reshape(latents, blocks, span, head_count).transpose(1, 0, 3, 2).reshape(blocks, latents * head_count, span)
    initial = jnp.zeros((latents * head_count, head_dim, head_dim), query_matrix.dtype)
    _, results = lax.scan(jax.checkpoint(span_pass), initial, (arrange(query_matrix), arrange(key_matrix), arrange(value_matrix), log_blocks))
    results = results.reshape(blocks, latents, head_count, span, head_dim).transpose(1, 0, 3, 2, 4)
    return results.reshape(latents, length, head_count * head_dim)

def depthwise(field, kernel, grid_side):
    latents = field.shape[0]
    channels = field.shape[2]
    image = field.reshape(latents, grid_side, grid_side, channels)
    padded = jnp.pad(image, ((0, 0), (1, 1), (1, 1), (0, 0)))
    summed = jnp.zeros_like(image)
    for row_off in range(3):
        for col_off in range(3):
            summed = summed + padded[:, row_off:row_off + grid_side, col_off:col_off + grid_side, :] * kernel[row_off, col_off]
    return summed.reshape(latents, grid_side * grid_side, channels)

def forward(tokens, time_steps, label_rows, class_table, ada_weight, ada_bias, query_key_value_weight, gate_weight, gate_bias, conv_weight, out_weight, up_weight, down_weight):
    group_size = tokens.shape[0]
    length = GRID * GRID
    onehot = (label_rows[:, None] == jnp.arange(NCLASS, dtype=jnp.int32)[None, :]).astype(jnp.float32)
    cond = jnp.dot(onehot, class_table, precision=TOP_PRECISION) + embed_time(time_steps, MODEL_DIM)
    silu_cond = reduced_input(jax.nn.silu(cond))
    mods = reduced_gradient(jnp.dot(silu_cond, ada_weight.reshape(MODEL_DIM, 6 * MODEL_DIM), precision=TOP_PRECISION).reshape(group_size, 6, MODEL_DIM) + ada_bias[None])
    first_normalized = reduced_input(normalize(tokens, mods[:, 0:1], mods[:, 1:2]))
    projected_rows = reduced_gradient(reduced_input(jnp.einsum('rhp,pi->rhi', first_normalized, query_key_value_weight.reshape(MODEL_DIM, 3 * MODEL_DIM), precision=TOP_PRECISION)))
    query_matrix = projected_rows[..., :MODEL_DIM].reshape(group_size, length, H, HD) * HD ** (-0.5)
    key_matrix = projected_rows[..., MODEL_DIM:2 * MODEL_DIM].reshape(group_size, length, H, HD)
    value_matrix = projected_rows[..., 2 * MODEL_DIM:].reshape(group_size, length, H, HD)
    forget_logit = reduced_gradient(jnp.einsum('gld,dh->glh', first_normalized, gate_weight, precision=TOP_PRECISION) + gate_bias)
    log_forget = jax.nn.log_sigmoid(forget_logit)
    recurrent = gated_scan(query_matrix, key_matrix, value_matrix, log_forget, CH)
    mixer_out = reduced_input(depthwise(recurrent, conv_weight, GRID))
    attn_out = reduced_gradient(jnp.einsum('gld,de->gle', mixer_out, out_weight, precision=TOP_PRECISION))
    after_attn = tokens + mods[:, 2:3] * attn_out
    normed_two = reduced_input(normalize(after_attn, mods[:, 3:4], mods[:, 4:5]))
    up_rows = reduced_gradient(jnp.einsum('gld,df->glf', normed_two, up_weight, precision=TOP_PRECISION))
    act = reduced_input(jax.nn.gelu(up_rows, approximate=True))
    mlp_out = reduced_gradient(jnp.einsum('glf,fd->gld', act, down_weight, precision=TOP_PRECISION))
    return after_attn + mods[:, 5:6] * mlp_out

def reference(latent_tokens, timesteps, labels, class_table, ada_weight, ada_bias, query_key_value_weight, gate_weight, gate_bias, conv_weight, out_weight, up_weight, down_weight, cotangent):
    weights = tuple((weight_item.astype(jnp.float32) for weight_item in (class_table, ada_weight, ada_bias, query_key_value_weight, gate_weight, gate_bias, conv_weight, out_weight, up_weight, down_weight)))
    group_size = math.gcd(LATENTS, 4)
    group_count = LATENTS // group_size

    def regroup(array):
        return array.reshape((group_count, group_size) + array.shape[1:])

    def one_group(totals, batch):
        tokens_in, steps_in, labels_in, grads_in = batch

        def local_forward(tokens_arg, *params):
            return forward(tokens_arg, steps_in, labels_in, *params)
        output, pull = jax.vjp(local_forward, tokens_in.astype(jnp.float32), *weights)
        grads = pull(grads_in.astype(jnp.float32))
        totals = tuple((total_part + new_part for total_part, new_part in zip(totals, grads[1:])))
        return (totals, (output.astype(jnp.bfloat16), grads[0]))
    initial = tuple((jnp.zeros_like(weight_item) for weight_item in weights))
    totals, (outputs, grad_rows) = lax.scan(one_group, initial, (regroup(latent_tokens), regroup(timesteps), regroup(labels), regroup(cotangent)))
    shape_full = (LATENTS, GRID * GRID, MODEL_DIM)
    return (outputs.reshape(shape_full), grad_rows.reshape(shape_full), totals[0], totals[1], totals[2], totals[3], totals[4], totals[5], totals[6], totals[7], totals[8], totals[9])
```

```python
from functools import partial
import math

import jax
import jax.numpy as jnp
from jax import lax
from jax.sharding import PartitionSpec as P

MODEL_DIM = 1152
HD = 72
NCLASS = 1000
GRID = 32
CH = 64


TOP_PRECISION = lax.Precision.HIGHEST
norm_eps = 1e-06


def embed_time(time_steps, model_width):
    half_width = model_width // 2
    frequency = jnp.exp(-math.log(10000.0) * jnp.arange(half_width, dtype=jnp.float32) / half_width)
    angles = time_steps.astype(jnp.float32)[:, None] * frequency[None, :]
    return jnp.concatenate([jnp.cos(angles), jnp.sin(angles)], axis=1)


def span_pass(running_state, block):
    query_matrix, key_matrix, value_matrix, log_forget = block
    block_len = log_forget.shape[1]
    decay_factors = jnp.cumsum(log_forget, axis=1)
    causal_mask = (jnp.arange(block_len)[:, None] >= jnp.arange(block_len)[None, :])[None]
    decay_gap = jnp.where(causal_mask, decay_factors[:, :, None] - decay_factors[:, None, :], 0.0)
    score_matrix = jnp.einsum("mkd,mld->mkl", query_matrix, key_matrix, precision=TOP_PRECISION)
    weighted_values = jnp.where(causal_mask, jnp.exp(decay_gap), 0.0) * score_matrix
    within_block_part = jnp.einsum(
        "dps,dsh->dph", weighted_values, value_matrix, precision=TOP_PRECISION
    )
    across_block_part = jnp.einsum(
        "ugm,ump->ugp",
        query_matrix * jnp.exp(decay_factors)[:, :, None],
        running_state,
        precision=TOP_PRECISION,
    )
    final_decay = decay_factors[:, -1:]
    carried = key_matrix * jnp.exp(final_decay - decay_factors)[:, :, None]
    running_state = running_state * jnp.exp(final_decay)[:, :, None] + jnp.einsum(
        "nje,njf->nef", carried, value_matrix, precision=TOP_PRECISION
    )
    return (running_state, within_block_part + across_block_part)


def gated_scan(query_matrix, key_matrix, value_matrix, log_forget, span):
    latents, length, head_count, head_dim = query_matrix.shape
    blocks = length // span

    def arrange(array):
        return (
            array.reshape(latents, blocks, span, head_count, head_dim)
            .transpose(1, 0, 3, 2, 4)
            .reshape(blocks, latents * head_count, span, head_dim)
        )

    log_blocks = (
        log_forget.reshape(latents, blocks, span, head_count)
        .transpose(1, 0, 3, 2)
        .reshape(blocks, latents * head_count, span)
    )
    initial = jnp.zeros((latents * head_count, head_dim, head_dim), query_matrix.dtype)
    _, results = lax.scan(
        jax.checkpoint(span_pass),
        initial,
        (arrange(query_matrix), arrange(key_matrix), arrange(value_matrix), log_blocks),
    )
    results = results.reshape(blocks, latents, head_count, span, head_dim).transpose(1, 0, 3, 2, 4)
    return results.reshape(latents, length, head_count * head_dim)


def depthwise(field, kernel, grid_side):
    latents = field.shape[0]
    channels = field.shape[2]
    image = field.reshape(latents, grid_side, grid_side, channels)
    padded = jnp.pad(image, ((0, 0), (1, 1), (1, 1), (0, 0)))
    summed = jnp.zeros_like(image)
    for row_off in range(3):
        for col_off in range(3):
            summed = (
                summed
                + padded[:, row_off : row_off + grid_side, col_off : col_off + grid_side, :]
                * kernel[row_off, col_off]
            )
    return summed.reshape(latents, grid_side * grid_side, channels)


def mixer_rows(query_matrix, key_matrix, value_matrix, log_forget, kernel, span, grid_side):
    recurrent = gated_scan(query_matrix, key_matrix, value_matrix, log_forget, span)
    return depthwise(recurrent, kernel, grid_side)


def tanh_gelu(inputs):
    return jax.nn.gelu(inputs, approximate=True)


def moments(rows, model_width):
    totals = lax.psum((jnp.sum(rows, axis=-1), jnp.sum(rows * rows, axis=-1)), "tensor")
    mean_row = totals[0][..., None] / model_width
    var_row = totals[1][..., None] / model_width - mean_row * mean_row
    return (mean_row, lax.rsqrt(var_row + norm_eps))


def share_rows(local_rows):
    return lax.all_gather(local_rows, "tensor", axis=2, tiled=True)


def branch_total(partial_rows):
    return lax.psum_scatter(partial_rows, "tensor", scatter_dimension=1, tiled=True)


def spread_grads(local_grads):
    return lax.all_gather(local_grads, "tensor", axis=2, tiled=True)


def input_total(partial_rows):
    return lax.psum_scatter(partial_rows, "tensor", scatter_dimension=1, tiled=True)


def norm_back(grad_normed, normalized, inv_std, scale_row, model_width):
    scaled = grad_normed * (1.0 + scale_row)
    totals = lax.psum((jnp.sum(scaled, axis=-1), jnp.sum(scaled * normalized, axis=-1)), "tensor")
    return inv_std * (
        scaled
        - totals[0][..., None] / model_width
        - normalized * totals[1][..., None] / model_width
    )


def shards(
    latent_tokens,
    timesteps,
    labels,
    class_table,
    ada_weight,
    ada_bias,
    query_key_value_weight,
    gate_weight,
    gate_bias,
    conv_weight,
    out_weight,
    up_weight,
    down_weight,
    cotangent,
):
    latents, length, part_width = latent_tokens.shape
    row_count = latents * length
    heads_here = gate_weight.shape[1]
    onehot = labels[:, None] == jnp.arange(NCLASS, dtype=jnp.int32)[None, :]
    cond = jnp.dot(
        onehot.astype(jnp.bfloat16), class_table, preferred_element_type=jnp.float32
    ) + embed_time(timesteps, MODEL_DIM)
    silu_value, silu_pull = jax.vjp(jax.nn.silu, cond)
    silu_cond = silu_value.astype(jnp.bfloat16)
    ada_flat = ada_weight.reshape(MODEL_DIM, 6 * part_width)
    mods = (
        jnp.dot(silu_cond, ada_flat, preferred_element_type=jnp.float32).reshape(
            latents, 6, part_width
        )
        + ada_bias.astype(jnp.float32)[None]
    )
    shift_one = mods[:, 0:1]
    scale_one = mods[:, 1:2]
    gate_one = mods[:, 2:3]
    shift_two = mods[:, 3:4]
    scale_two = mods[:, 4:5]
    gate_two = mods[:, 5:6]
    tokens_value = latent_tokens.astype(jnp.float32)
    mean_one, std_inv_one = moments(tokens_value, MODEL_DIM)
    unit_one = (tokens_value - mean_one) * std_inv_one
    first_normalized = share_rows((unit_one * (1.0 + scale_one) + shift_one).astype(jnp.bfloat16))
    rows_one = first_normalized.reshape(row_count, MODEL_DIM)
    qkv_flat = query_key_value_weight.reshape(MODEL_DIM, 3 * part_width)
    projected_rows = jnp.dot(rows_one, qkv_flat, preferred_element_type=jnp.float32).astype(
        jnp.bfloat16
    )
    forget_logit = jnp.dot(
        rows_one, gate_weight, preferred_element_type=jnp.float32
    ) + gate_bias.astype(jnp.float32)

    def head_view(columns):
        return columns.astype(jnp.float32).reshape(latents, length, heads_here, HD)

    query_matrix = head_view(projected_rows[:, :part_width]) * HD ** (-0.5)
    key_matrix = head_view(projected_rows[:, part_width : 2 * part_width])
    value_matrix = head_view(projected_rows[:, 2 * part_width :])
    log_forget = jax.nn.log_sigmoid(forget_logit).reshape(latents, length, heads_here)
    mixed_out, mixer_pull = jax.vjp(
        partial(mixer_rows, span=CH, grid_side=GRID),
        query_matrix,
        key_matrix,
        value_matrix,
        log_forget,
        conv_weight.astype(jnp.float32),
    )
    mixer_low = mixed_out.reshape(row_count, part_width).astype(jnp.bfloat16)
    attn_out = branch_total(
        jnp.dot(mixer_low, out_weight, preferred_element_type=jnp.float32)
    ).reshape(latents, length, part_width)
    after_attn = tokens_value + gate_one * attn_out
    mean_two, std_inv_two = moments(after_attn, MODEL_DIM)
    unit_two = (after_attn - mean_two) * std_inv_two
    normed_two = share_rows((unit_two * (1.0 + scale_two) + shift_two).astype(jnp.bfloat16))
    rows_two = normed_two.reshape(row_count, MODEL_DIM)
    up_rows = jnp.dot(rows_two, up_weight, preferred_element_type=jnp.float32)
    act_rows, gelu_pull = jax.vjp(tanh_gelu, up_rows)
    act_low = act_rows.astype(jnp.bfloat16)
    mlp_out = branch_total(
        jnp.dot(act_low, down_weight, preferred_element_type=jnp.float32)
    ).reshape(latents, length, part_width)
    layer_out = (after_attn + gate_two * mlp_out).astype(jnp.bfloat16)
    grad_result = cotangent.astype(jnp.float32)
    grad_gate_two = jnp.sum(grad_result * mlp_out, axis=1)
    grad_mlp = spread_grads((grad_result * gate_two).astype(jnp.bfloat16)).reshape(
        row_count, MODEL_DIM
    )
    grad_down = jnp.einsum("rf,rd->fd", act_low, grad_mlp, preferred_element_type=jnp.float32)
    grad_act = jnp.einsum("rd,fd->rf", grad_mlp, down_weight, preferred_element_type=jnp.float32)
    grad_up_rows = gelu_pull(grad_act)[0].astype(jnp.bfloat16)
    grad_up = jnp.einsum("rd,rf->df", rows_two, grad_up_rows, preferred_element_type=jnp.float32)
    grad_normed_two = input_total(
        jnp.einsum("rf,df->rd", grad_up_rows, up_weight, preferred_element_type=jnp.float32)
    ).reshape(latents, length, part_width)
    grad_shift_two = jnp.sum(grad_normed_two, axis=1)
    grad_scale_two = jnp.sum(grad_normed_two * unit_two, axis=1)
    grad_after = grad_result + norm_back(
        grad_normed_two, unit_two, std_inv_two, scale_two, MODEL_DIM
    )
    grad_gate_one = jnp.sum(grad_after * attn_out, axis=1)
    grad_attn = spread_grads((grad_after * gate_one).astype(jnp.bfloat16)).reshape(
        row_count, MODEL_DIM
    )
    grad_out_w = jnp.einsum("rp,rd->pd", mixer_low, grad_attn, preferred_element_type=jnp.float32)
    grad_mixed = jnp.einsum(
        "rd,pd->rp", grad_attn, out_weight, preferred_element_type=jnp.float32
    ).reshape(latents, length, part_width)
    grad_query, grad_key, grad_value, grad_log, grad_conv = mixer_pull(grad_mixed)
    grad_projected = (
        jnp.concatenate([grad_query * HD ** (-0.5), grad_key, grad_value], axis=2)
        .reshape(row_count, 3 * part_width)
        .astype(jnp.bfloat16)
    )
    grad_forget = (grad_log.reshape(row_count, heads_here) * jax.nn.sigmoid(-forget_logit)).astype(
        jnp.bfloat16
    )
    grad_qkv = jnp.einsum(
        "rd,rc->dc", rows_one, grad_projected, preferred_element_type=jnp.float32
    ).reshape(MODEL_DIM, 3, part_width)
    grad_gate_w = jnp.einsum("rd,rh->dh", rows_one, grad_forget, preferred_element_type=jnp.float32)
    grad_gate_b = jnp.sum(grad_forget.astype(jnp.float32), axis=0)
    grad_normed_one = input_total(
        jnp.einsum("rc,dc->rd", grad_projected, qkv_flat, preferred_element_type=jnp.float32)
        + jnp.einsum("rh,dh->rd", grad_forget, gate_weight, preferred_element_type=jnp.float32)
    ).reshape(latents, length, part_width)
    grad_shift_one = jnp.sum(grad_normed_one, axis=1)
    grad_scale_one = jnp.sum(grad_normed_one * unit_one, axis=1)
    grad_tokens = grad_after + norm_back(
        grad_normed_one, unit_one, std_inv_one, scale_one, MODEL_DIM
    )
    grad_mods = jnp.stack(
        [
            grad_shift_one,
            grad_scale_one,
            grad_gate_one,
            grad_shift_two,
            grad_scale_two,
            grad_gate_two,
        ],
        axis=1,
    ).astype(jnp.bfloat16)
    mods_flat = grad_mods.reshape(latents, 6 * part_width)
    grad_silu = jnp.einsum("bc,dc->bd", mods_flat, ada_flat, preferred_element_type=jnp.float32)
    shard_count = lax.psum(1, "dp")
    shard_at = lax.axis_index("dp")
    own_width = MODEL_DIM // shard_count
    small = jnp.concatenate(
        [
            mods_flat.astype(jnp.float32).reshape(latents * 6 * part_width),
            lax.psum(grad_silu, "tensor").reshape(latents * MODEL_DIM),
            cond.reshape(latents * MODEL_DIM),
            grad_gate_w.reshape(MODEL_DIM * heads_here),
            grad_gate_b,
            grad_conv.reshape(9 * part_width),
        ]
    )
    every = lax.all_gather(small, "dp", axis=0, tiled=False)
    every_labels = lax.all_gather(labels, "dp", axis=0, tiled=True)
    all_latents = every_labels.shape[0]
    sizes = [
        latents * 6 * part_width,
        latents * MODEL_DIM,
        latents * MODEL_DIM,
        MODEL_DIM * heads_here,
        heads_here,
        9 * part_width,
    ]
    starts = [sum(sizes[:index]) for index in range(len(sizes) + 1)]
    every_mods, every_silu, every_cond, every_gate_w, every_gate_b, every_conv = (
        every[:, low:high] for low, high in zip(starts[:-1], starts[1:])
    )
    every_mods = every_mods.reshape(all_latents, 6 * part_width)
    grad_ada_b = jnp.sum(every_mods, axis=0).reshape(6, part_width)
    grad_gate_b = jnp.sum(every_gate_b, axis=0)
    grad_conv = jnp.sum(every_conv, axis=0).reshape(3, 3, part_width)

    def own_columns(rows):
        rows = rows.reshape(all_latents, MODEL_DIM)
        return lax.dynamic_slice_in_dim(rows, shard_at * own_width, own_width, axis=1)

    own_silu, own_pull = jax.vjp(jax.nn.silu, own_columns(every_cond))
    own_cond = own_pull(own_columns(every_silu))[0]
    grad_ada_w = jnp.einsum(
        "bd,bc->dc",
        own_silu.astype(jnp.bfloat16),
        every_mods.astype(jnp.bfloat16),
        preferred_element_type=jnp.float32,
    ).reshape(own_width, 6, part_width)
    every_onehot = every_labels[:, None] == jnp.arange(NCLASS, dtype=jnp.int32)[None, :]
    grad_class = jnp.dot(every_onehot.astype(jnp.float32).T, own_cond, precision=TOP_PRECISION)
    own_gate_w = lax.dynamic_slice_in_dim(
        every_gate_w.reshape(shard_count, MODEL_DIM, heads_here), shard_at * own_width, own_width, axis=1
    )
    grad_gate_w = jnp.sum(own_gate_w, axis=0)

    def dp_total(partial, axis):
        low = partial.astype(jnp.bfloat16)
        return lax.psum_scatter(low, "dp", scatter_dimension=axis, tiled=True).astype(jnp.float32)

    grad_qkv, grad_out_w, grad_up, grad_down = (
        dp_total(grad_qkv, 0),
        dp_total(grad_out_w, 1),
        dp_total(grad_up, 0),
        dp_total(grad_down, 1),
    )
    return (
        layer_out,
        grad_tokens,
        grad_class,
        grad_ada_w,
        grad_ada_b,
        grad_qkv,
        grad_gate_w,
        grad_gate_b,
        grad_conv,
        grad_out_w,
        grad_up,
        grad_down,
    )


def solution(mesh):
    in_specs = (
        P("dp", None, "tensor"),
        P("dp"),
        P("dp"),
        P(),
        P(None, None, "tensor"),
        P(None, "tensor"),
        P(None, None, "tensor"),
        P(None, "tensor"),
        P("tensor"),
        P(None, None, "tensor"),
        P("tensor", None),
        P(None, "tensor"),
        P("tensor", None),
        P("dp", None, "tensor"),
    )
    out_specs = (
        P("dp", None, "tensor"),
        P("dp", None, "tensor"),
        P(None, "dp"),
        P("dp", None, "tensor"),
        P(None, "tensor"),
        P("dp", None, "tensor"),
        P("dp", "tensor"),
        P("tensor"),
        P(None, None, "tensor"),
        P("tensor", "dp"),
        P("dp", "tensor"),
        P("tensor", "dp"),
    )
    return jax.shard_map(shards, mesh=mesh, in_specs=in_specs, out_specs=out_specs, check_vma=False)
```

```python
import functools
import math

import jax
import jax.numpy as jnp
from jax import lax
from jax.experimental import pallas as pl
from jax.experimental.pallas import tpu as pltpu
from jax.sharding import PartitionSpec as P

MODEL_DIM = 1152
HD = 72
NCLASS = 1000
GRID = 32


TOP_PRECISION = lax.Precision.HIGHEST
norm_eps = 1e-06


def embed_time(time_steps, model_width):
    half_width = model_width // 2
    frequency = jnp.exp(-math.log(10000.0) * jnp.arange(half_width, dtype=jnp.float32) / half_width)
    angles = time_steps.astype(jnp.float32)[:, None] * frequency[None, :]
    return jnp.concatenate([jnp.cos(angles), jnp.sin(angles)], axis=1)


SPAN = 256

TN = (((0,), (0,)), ((), ()))
NT = (((1,), (1,)), ((), ()))
NN = (((1,), (0,)), ((), ()))
NTT = (((0,), (1,)), ((), ()))


def mm(left, right, form):
    return lax.dot_general(left, right, form, preferred_element_type=jnp.float32)


def low(values):
    return values.astype(jnp.bfloat16)


def shifted(rows, offset):
    length = rows.shape[1]
    return pltpu.roll(rows, (-offset) % length, 1)


def edge_masks(length):
    token = lax.broadcasted_iota(jnp.int32, (1, length), 1)
    column = lax.rem(token, GRID)
    return column > 0, column < GRID - 1, token >= GRID, token < length - GRID


def neighbours(rows, masks):
    left_ok, right_ok, _, _ = masks
    return (
        jnp.where(left_ok, shifted(rows, -1), 0.0),
        rows,
        jnp.where(right_ok, shifted(rows, 1), 0.0),
    )


def running_sum(rows, span, reverse=False, exclusive=False):
    length = rows.shape[1]
    place = lax.rem(lax.broadcasted_iota(jnp.int32, (1, length), 1), span)
    total = rows
    step = 1
    if exclusive:
        total = (
            jnp.where(place < span - 1, shifted(total, 1), 0.0)
            if reverse
            else jnp.where(place >= 1, shifted(total, -1), 0.0)
        )
    while step < span:
        if reverse:
            total = total + jnp.where(place < span - step, shifted(total, step), 0.0)
        else:
            total = total + jnp.where(place >= step, shifted(total, -step), 0.0)
        step *= 2
    return total


def log_sigmoid(logit):
    return jnp.minimum(logit, 0.0) - jnp.log(1.0 + jnp.exp(-jnp.abs(logit)))


def conv_rows(rows, taps, masks, adjoint):
    _, _, up_ok, down_ok = masks
    left, middle, right = neighbours(rows, masks)
    parts = []
    for row in range(3):
        if adjoint:
            weights = [taps[:, 3 * (2 - row) + 2 - col : 3 * (2 - row) + 3 - col] for col in range(3)]
        else:
            weights = [taps[:, 3 * row + col : 3 * row + col + 1] for col in range(3)]
        parts.append(left * weights[0] + middle * weights[1] + right * weights[2])
    above = jnp.where(up_ok, shifted(parts[0], -GRID), 0.0)
    below = jnp.where(down_ok, shifted(parts[2], GRID), 0.0)
    return above + parts[1] + below


def decay_block(row, column):
    span = row.shape[1]
    key_at = lax.broadcasted_iota(jnp.int32, (span, span), 0)
    query_at = lax.broadcasted_iota(jnp.int32, (span, span), 1)
    return jnp.where(query_at >= key_at, jnp.exp(jnp.minimum(row - column, 0.0)), 0.0)


def mixer_kernel(heads, proj_ref, logit_ref, taps_ref, mixed_ref, rec_ref, states_ref, wide, cum_ref, col_ref):
    part, length = rec_ref.shape
    spans = length // SPAN
    log_forget = log_sigmoid(logit_ref[...])
    cum = running_sum(log_forget, SPAN)
    cum_ref[...] = cum
    col_ref[...] = jnp.transpose(cum)
    wide[...] = proj_ref[...].astype(jnp.float32)
    scale = HD ** (-0.5)

    def one_span(at, states):
        lanes = pl.ds(pl.multiple_of(at * SPAN, SPAN), SPAN)
        after = []
        for head in range(heads):
            at_rows = [pl.ds(kind * part + head * HD, HD) for kind in range(3)]
            query, key, value = (wide[rows, lanes] for rows in at_rows)
            row = cum_ref[head : head + 1, lanes]
            column = col_ref[lanes, head : head + 1]
            last = row[:, SPAN - 1 : SPAN]
            state = states[head]
            states_ref[at, head] = state
            weights = decay_block(row, column) * mm(low(key), low(query), TN)
            out = mm(low(value), low(weights), NN)
            out = out + mm(low(state), low(query * jnp.exp(row)), NN)
            rec_ref[pl.ds(head * HD, HD), lanes] = out * scale
            carried = low(key * jnp.exp(last - row))
            after.append(state * jnp.exp(last) + mm(low(value), carried, NT))
        return tuple(after)

    lax.fori_loop(0, spans, one_span, tuple(jnp.zeros((HD, HD), jnp.float32) for _ in range(heads)))
    masks = edge_masks(length)

    def one_group(at, carry):
        rows = pl.ds(pl.multiple_of(at * 16, 16), 16)
        mixed_ref[rows, :] = low(conv_rows(rec_ref[rows, :], taps_ref[rows, :], masks, False))
        return carry

    lax.fori_loop(0, part // 16, one_group, 0)


def mixer(proj, logit, taps, heads):
    part = proj.shape[0] // 3
    length = proj.shape[1]
    spans = length // SPAN
    return pl.pallas_call(
        functools.partial(mixer_kernel, heads),
        out_shape=(
            jax.ShapeDtypeStruct((part, length), jnp.bfloat16),
            jax.ShapeDtypeStruct((part, length), jnp.float32),
            jax.ShapeDtypeStruct((spans, heads, HD, HD), jnp.float32),
        ),
        in_specs=[pl.BlockSpec(memory_space=pltpu.VMEM)] * 3,
        out_specs=[pl.BlockSpec(memory_space=pltpu.VMEM)] * 3,
        scratch_shapes=[
            pltpu.VMEM((3 * part, length), jnp.float32),
            pltpu.VMEM((8, length), jnp.float32),
            pltpu.VMEM((length, 8), jnp.float32),
        ],
        compiler_params=pltpu.CompilerParams(vmem_limit_bytes=56 * 2**20),
        name="mixer",
    )(proj, logit, taps)


def back_kernel(
    heads, proj_ref, logit_ref, taps_ref, rec_ref, states_ref, grad_ref,
    gproj_ref, gforget_ref, gtaps_ref, wide, gwide, cum_ref, col_ref, grec_ref, rows_ref,
):
    part, length = rec_ref.shape
    spans = length // SPAN
    logit = logit_ref[...]
    cum = running_sum(log_sigmoid(logit), SPAN)
    cum_ref[...] = cum
    col_ref[...] = jnp.transpose(cum)
    wide[...] = proj_ref[...].astype(jnp.float32)
    masks = edge_masks(length)
    scale = HD ** (-0.5)
    lane = lax.broadcasted_iota(jnp.int32, (16, 16), 1)

    def one_group(at, carry):
        rows = pl.ds(pl.multiple_of(at * 16, 16), 16)
        grad = grad_ref[rows, :].astype(jnp.float32)
        grec_ref[rows, :] = conv_rows(grad, taps_ref[rows, :], masks, True) * scale
        moved = neighbours(rec_ref[rows, :], masks)
        _, _, up_ok, down_ok = masks
        grads = (
            jnp.where(down_ok, shifted(grad, GRID), 0.0),
            grad,
            jnp.where(up_ok, shifted(grad, -GRID), 0.0),
        )
        result = jnp.zeros((16, 16), jnp.float32)
        for row in range(3):
            for col in range(3):
                one = jnp.sum(moved[col] * grads[row], axis=1, keepdims=True)
                result = jnp.where(lane == 3 * row + col, one, result)
        gtaps_ref[rows, :] = result
        return carry

    lax.fori_loop(0, part // 16, one_group, 0)
    rows_ref[...] = jnp.zeros_like(rows_ref)
    key_at = lax.broadcasted_iota(jnp.int32, (SPAN, SPAN), 0)
    query_at = lax.broadcasted_iota(jnp.int32, (SPAN, SPAN), 1)
    later = low(jnp.where(key_at >= query_at, 1.0, 0.0))

    def one_span(step, back_states):
        at = spans - 1 - step
        lanes = pl.ds(pl.multiple_of(at * SPAN, SPAN), SPAN)
        after = []
        for head in range(heads):
            at_rows = [pl.ds(kind * part + head * HD, HD) for kind in range(3)]
            query, key, value = (wide[rows, lanes] for rows in at_rows)
            grad = low(grec_ref[pl.ds(head * HD, HD), lanes])
            row = cum_ref[head : head + 1, lanes]
            column = col_ref[lanes, head : head + 1]
            last = row[:, SPAN - 1 : SPAN]
            state = states_ref[at, head]
            back = back_states[head]
            decay = decay_block(row, column)
            score = mm(low(key), low(query), TN)
            weights = decay * score
            grad_weights = mm(low(value), grad, TN)
            grad_score = grad_weights * decay
            product = low(grad_weights * weights)
            grad_score = low(grad_score)
            in_decay = jnp.exp(row)
            out_decay = jnp.exp(last - row)
            query_in = mm(low(state), grad, TN) * in_decay
            key_out = mm(low(back), low(value), TN) * out_decay
            gwide[at_rows[0], lanes] = mm(low(key), grad_score, NN) + query_in
            gwide[at_rows[1], lanes] = mm(low(query), grad_score, NT) + key_out
            carried = low(key * out_decay)
            gwide[at_rows[2], lanes] = mm(grad, low(weights), NT) + mm(low(back), carried, NN)
            inside = mm(product, later, NN)
            inside = jnp.sum(jnp.where(key_at < query_at, inside, 0.0), axis=0, keepdims=True)
            span_decay = jnp.exp(last)
            across = jnp.sum(back * state, keepdims=True) * span_decay
            rows_ref[0, head : head + 1, lanes] = jnp.sum(query * query_in, axis=0, keepdims=True)
            rows_ref[1, head : head + 1, lanes] = jnp.sum(key * key_out, axis=0, keepdims=True)
            rows_ref[2, head : head + 1, lanes] = inside + across
            after.append(back * span_decay + mm(grad, low(query * in_decay), NT))
        return tuple(after)

    lax.fori_loop(0, spans, one_span, tuple(jnp.zeros((HD, HD), jnp.float32) for _ in range(heads)))
    grad_log = (
        running_sum(rows_ref[0], SPAN, reverse=True)
        + running_sum(rows_ref[1], SPAN, exclusive=True)
        + rows_ref[2]
    )
    gforget_ref[...] = low(grad_log / (1.0 + jnp.exp(logit)))
    gproj_ref[...] = low(gwide[...])


def mixer_back(proj, logit, taps, rec, states, grad, heads):
    part = proj.shape[0] // 3
    length = proj.shape[1]
    return pl.pallas_call(
        functools.partial(back_kernel, heads),
        out_shape=(
            jax.ShapeDtypeStruct((3 * part, length), jnp.bfloat16),
            jax.ShapeDtypeStruct((8, length), jnp.bfloat16),
            jax.ShapeDtypeStruct((part, 16), jnp.float32),
        ),
        in_specs=[pl.BlockSpec(memory_space=pltpu.VMEM)] * 6,
        out_specs=[pl.BlockSpec(memory_space=pltpu.VMEM)] * 3,
        scratch_shapes=[
            pltpu.VMEM((3 * part, length), jnp.float32),
            pltpu.VMEM((3 * part, length), jnp.float32),
            pltpu.VMEM((8, length), jnp.float32),
            pltpu.VMEM((length, 8), jnp.float32),
            pltpu.VMEM((part, length), jnp.float32),
            pltpu.VMEM((3, 8, length), jnp.float32),
        ],
        compiler_params=pltpu.CompilerParams(vmem_limit_bytes=56 * 2**20),
        name="mixer_back",
    )(proj, logit, taps, rec, states, grad)


def tanh_gelu(inputs):
    return jax.nn.gelu(inputs, approximate=True)


def moments(rows, model_width):
    totals = lax.psum((jnp.sum(rows, axis=-1), jnp.sum(rows * rows, axis=-1)), "tensor")
    mean_row = totals[0][..., None] / model_width
    var_row = totals[1][..., None] / model_width - mean_row * mean_row
    return (mean_row, lax.rsqrt(var_row + norm_eps))


def share_rows(local_rows):
    return lax.all_gather(local_rows, "tensor", axis=2, tiled=True)


def branch_total(partial_rows):
    return lax.psum_scatter(partial_rows, "tensor", scatter_dimension=1, tiled=True)


def spread_grads(local_grads):
    return lax.all_gather(local_grads, "tensor", axis=2, tiled=True)


def input_total(partial_rows):
    return lax.psum_scatter(partial_rows, "tensor", scatter_dimension=1, tiled=True)


def norm_back(grad_normed, normalized, inv_std, scale_row, model_width):
    scaled = grad_normed * (1.0 + scale_row)
    totals = lax.psum((jnp.sum(scaled, axis=-1), jnp.sum(scaled * normalized, axis=-1)), "tensor")
    return inv_std * (
        scaled
        - totals[0][..., None] / model_width
        - normalized * totals[1][..., None] / model_width
    )


def shards(
    latent_tokens,
    timesteps,
    labels,
    class_table,
    ada_weight,
    ada_bias,
    query_key_value_weight,
    gate_weight,
    gate_bias,
    conv_weight,
    out_weight,
    up_weight,
    down_weight,
    cotangent,
):
    latents, length, part_width = latent_tokens.shape
    row_count = latents * length
    heads_here = gate_weight.shape[1]
    onehot = labels[:, None] == jnp.arange(NCLASS, dtype=jnp.int32)[None, :]
    cond = jnp.dot(
        onehot.astype(jnp.bfloat16), class_table, preferred_element_type=jnp.float32
    ) + embed_time(timesteps, MODEL_DIM)
    silu_value, silu_pull = jax.vjp(jax.nn.silu, cond)
    silu_cond = silu_value.astype(jnp.bfloat16)
    ada_flat = ada_weight.reshape(MODEL_DIM, 6 * part_width)
    mods = (
        jnp.dot(silu_cond, ada_flat, preferred_element_type=jnp.float32).reshape(
            latents, 6, part_width
        )
        + ada_bias.astype(jnp.float32)[None]
    )
    shift_one = mods[:, 0:1]
    scale_one = mods[:, 1:2]
    gate_one = mods[:, 2:3]
    shift_two = mods[:, 3:4]
    scale_two = mods[:, 4:5]
    gate_two = mods[:, 5:6]
    tokens_value = latent_tokens.astype(jnp.float32)
    mean_one, std_inv_one = moments(tokens_value, MODEL_DIM)
    unit_one = (tokens_value - mean_one) * std_inv_one
    first_normalized = share_rows((unit_one * (1.0 + scale_one) + shift_one).astype(jnp.bfloat16))
    rows_one = first_normalized.reshape(row_count, MODEL_DIM)
    qkv_flat = query_key_value_weight.reshape(MODEL_DIM, 3 * part_width)
    projected = low(mm(qkv_flat, rows_one, NTT))
    forget_logit = mm(gate_weight, rows_one, NTT) + gate_bias.astype(jnp.float32)[:, None]
    forget_logit = jnp.pad(forget_logit, ((0, 8 - heads_here), (0, 0)))
    taps = jnp.pad(conv_weight.astype(jnp.float32).reshape(9, part_width).T, ((0, 0), (0, 7)))
    mixed_low, recurrent, states = mixer(projected, forget_logit, taps, heads_here)
    attn_out = branch_total(
        mm(mixed_low, out_weight, TN)
    ).reshape(latents, length, part_width)
    after_attn = tokens_value + gate_one * attn_out
    mean_two, std_inv_two = moments(after_attn, MODEL_DIM)
    unit_two = (after_attn - mean_two) * std_inv_two
    normed_two = share_rows((unit_two * (1.0 + scale_two) + shift_two).astype(jnp.bfloat16))
    rows_two = normed_two.reshape(row_count, MODEL_DIM)
    up_rows = jnp.dot(rows_two, up_weight, preferred_element_type=jnp.float32)
    act_rows, gelu_pull = jax.vjp(tanh_gelu, up_rows)
    act_low = act_rows.astype(jnp.bfloat16)
    mlp_out = branch_total(
        jnp.dot(act_low, down_weight, preferred_element_type=jnp.float32)
    ).reshape(latents, length, part_width)
    layer_out = (after_attn + gate_two * mlp_out).astype(jnp.bfloat16)
    grad_result = cotangent.astype(jnp.float32)
    grad_gate_two = jnp.sum(grad_result * mlp_out, axis=1)
    grad_mlp = spread_grads((grad_result * gate_two).astype(jnp.bfloat16)).reshape(
        row_count, MODEL_DIM
    )
    grad_down = jnp.einsum("rf,rd->fd", act_low, grad_mlp, preferred_element_type=jnp.float32)
    grad_act = jnp.einsum("rd,fd->rf", grad_mlp, down_weight, preferred_element_type=jnp.float32)
    grad_up_rows = gelu_pull(grad_act)[0].astype(jnp.bfloat16)
    grad_up = jnp.einsum("rd,rf->df", rows_two, grad_up_rows, preferred_element_type=jnp.float32)
    grad_normed_two = input_total(
        jnp.einsum("rf,df->rd", grad_up_rows, up_weight, preferred_element_type=jnp.float32)
    ).reshape(latents, length, part_width)
    grad_shift_two = jnp.sum(grad_normed_two, axis=1)
    grad_scale_two = jnp.sum(grad_normed_two * unit_two, axis=1)
    grad_after = grad_result + norm_back(
        grad_normed_two, unit_two, std_inv_two, scale_two, MODEL_DIM
    )
    grad_gate_one = jnp.sum(grad_after * attn_out, axis=1)
    grad_attn = spread_grads((grad_after * gate_one).astype(jnp.bfloat16)).reshape(
        row_count, MODEL_DIM
    )
    grad_out_w = mm(mixed_low, grad_attn, NN)
    grad_mixed = mm(out_weight, grad_attn, NT)
    grad_projected, grad_forget, grad_taps = mixer_back(
        projected, forget_logit, taps, recurrent, states, grad_mixed, heads_here
    )
    grad_forget = grad_forget[:heads_here]
    grad_conv = grad_taps[:, :9].T
    grad_qkv = mm(rows_one, grad_projected, NTT).reshape(MODEL_DIM, 3, part_width)
    grad_gate_w = mm(rows_one, grad_forget, NTT)
    grad_gate_b = jnp.sum(grad_forget.astype(jnp.float32), axis=1)
    grad_normed_one = input_total(
        mm(grad_projected, qkv_flat, NTT) + mm(grad_forget, gate_weight, NTT)
    ).reshape(latents, length, part_width)
    grad_shift_one = jnp.sum(grad_normed_one, axis=1)
    grad_scale_one = jnp.sum(grad_normed_one * unit_one, axis=1)
    grad_tokens = grad_after + norm_back(
        grad_normed_one, unit_one, std_inv_one, scale_one, MODEL_DIM
    )
    grad_mods = jnp.stack(
        [
            grad_shift_one,
            grad_scale_one,
            grad_gate_one,
            grad_shift_two,
            grad_scale_two,
            grad_gate_two,
        ],
        axis=1,
    ).astype(jnp.bfloat16)
    mods_flat = grad_mods.reshape(latents, 6 * part_width)
    grad_silu = jnp.einsum("bc,dc->bd", mods_flat, ada_flat, preferred_element_type=jnp.float32)
    shard_count = lax.psum(1, "dp")
    shard_at = lax.axis_index("dp")
    own_width = MODEL_DIM // shard_count
    small = jnp.concatenate(
        [
            mods_flat.astype(jnp.float32).reshape(latents * 6 * part_width),
            lax.psum(grad_silu, "tensor").reshape(latents * MODEL_DIM),
            cond.reshape(latents * MODEL_DIM),
            grad_gate_w.reshape(MODEL_DIM * heads_here),
            grad_gate_b,
            grad_conv.reshape(9 * part_width),
        ]
    )
    every = lax.all_gather(small, "dp", axis=0, tiled=False)
    every_labels = lax.all_gather(labels, "dp", axis=0, tiled=True)
    all_latents = every_labels.shape[0]
    sizes = [
        latents * 6 * part_width,
        latents * MODEL_DIM,
        latents * MODEL_DIM,
        MODEL_DIM * heads_here,
        heads_here,
        9 * part_width,
    ]
    starts = [sum(sizes[:index]) for index in range(len(sizes) + 1)]
    every_mods, every_silu, every_cond, every_gate_w, every_gate_b, every_conv = (
        every[:, low:high] for low, high in zip(starts[:-1], starts[1:])
    )
    every_mods = every_mods.reshape(all_latents, 6 * part_width)
    grad_ada_b = jnp.sum(every_mods, axis=0).reshape(6, part_width)
    grad_gate_b = jnp.sum(every_gate_b, axis=0)
    grad_conv = jnp.sum(every_conv, axis=0).reshape(3, 3, part_width)

    def own_columns(rows):
        rows = rows.reshape(all_latents, MODEL_DIM)
        return lax.dynamic_slice_in_dim(rows, shard_at * own_width, own_width, axis=1)

    own_silu, own_pull = jax.vjp(jax.nn.silu, own_columns(every_cond))
    own_cond = own_pull(own_columns(every_silu))[0]
    grad_ada_w = jnp.einsum(
        "bd,bc->dc",
        own_silu.astype(jnp.bfloat16),
        every_mods.astype(jnp.bfloat16),
        preferred_element_type=jnp.float32,
    ).reshape(own_width, 6, part_width)
    every_onehot = every_labels[:, None] == jnp.arange(NCLASS, dtype=jnp.int32)[None, :]
    grad_class = jnp.dot(every_onehot.astype(jnp.float32).T, own_cond, precision=TOP_PRECISION)
    own_gate_w = lax.dynamic_slice_in_dim(
        every_gate_w.reshape(shard_count, MODEL_DIM, heads_here), shard_at * own_width, own_width, axis=1
    )
    grad_gate_w = jnp.sum(own_gate_w, axis=0)

    def dp_total(partial, axis):
        low = partial.astype(jnp.bfloat16)
        return lax.psum_scatter(low, "dp", scatter_dimension=axis, tiled=True).astype(jnp.float32)

    grad_qkv, grad_out_w, grad_up, grad_down = (
        dp_total(grad_qkv, 0),
        dp_total(grad_out_w, 1),
        dp_total(grad_up, 0),
        dp_total(grad_down, 1),
    )
    return (
        layer_out,
        grad_tokens,
        grad_class,
        grad_ada_w,
        grad_ada_b,
        grad_qkv,
        grad_gate_w,
        grad_gate_b,
        grad_conv,
        grad_out_w,
        grad_up,
        grad_down,
    )


def solution(mesh):
    in_specs = (
        P("dp", None, "tensor"),
        P("dp"),
        P("dp"),
        P(),
        P(None, None, "tensor"),
        P(None, "tensor"),
        P(None, None, "tensor"),
        P(None, "tensor"),
        P("tensor"),
        P(None, None, "tensor"),
        P("tensor", None),
        P(None, "tensor"),
        P("tensor", None),
        P("dp", None, "tensor"),
    )
    out_specs = (
        P("dp", None, "tensor"),
        P("dp", None, "tensor"),
        P(None, "dp"),
        P("dp", None, "tensor"),
        P(None, "tensor"),
        P("dp", None, "tensor"),
        P("dp", "tensor"),
        P("tensor"),
        P(None, None, "tensor"),
        P("tensor", "dp"),
        P("dp", "tensor"),
        P("tensor", "dp"),
    )
    return jax.shard_map(shards, mesh=mesh, in_specs=in_specs, out_specs=out_specs, check_vma=False)
```

```python
import functools
import math

import jax
import jax.numpy as jnp
from jax import lax
from jax.experimental import pallas as pl
from jax.experimental.pallas import tpu as pltpu
from jax.sharding import PartitionSpec as P

MODEL_DIM = 1152
HD = 72
NCLASS = 1000
GRID = 32


TOP_PRECISION = lax.Precision.HIGHEST
norm_eps = 1e-06


def embed_time(time_steps, model_width):
    half_width = model_width // 2
    frequency = jnp.exp(-math.log(10000.0) * jnp.arange(half_width, dtype=jnp.float32) / half_width)
    angles = time_steps.astype(jnp.float32)[:, None] * frequency[None, :]
    return jnp.concatenate([jnp.cos(angles), jnp.sin(angles)], axis=1)


SPAN = 256

TN = (((0,), (0,)), ((), ()))
NT = (((1,), (1,)), ((), ()))
NN = (((1,), (0,)), ((), ()))


def mm(left, right, form):
    return lax.dot_general(left, right, form, preferred_element_type=jnp.float32)


def low(values):
    return values.astype(jnp.bfloat16)


def shifted(rows, offset):
    length = rows.shape[1]
    return pltpu.roll(rows, (-offset) % length, 1)


def edge_masks(length):
    token = lax.broadcasted_iota(jnp.int32, (1, length), 1)
    column = lax.rem(token, GRID)
    return column > 0, column < GRID - 1, token >= GRID, token < length - GRID


def neighbours(rows, masks):
    left_ok, right_ok, _, _ = masks
    return (
        jnp.where(left_ok, shifted(rows, -1), 0.0),
        rows,
        jnp.where(right_ok, shifted(rows, 1), 0.0),
    )


def running_sum(rows, span, reverse=False, exclusive=False):
    length = rows.shape[1]
    place = lax.rem(lax.broadcasted_iota(jnp.int32, (1, length), 1), span)
    total = rows
    step = 1
    if exclusive:
        total = (
            jnp.where(place < span - 1, shifted(total, 1), 0.0)
            if reverse
            else jnp.where(place >= 1, shifted(total, -1), 0.0)
        )
    while step < span:
        if reverse:
            total = total + jnp.where(place < span - step, shifted(total, step), 0.0)
        else:
            total = total + jnp.where(place >= step, shifted(total, -step), 0.0)
        step *= 2
    return total


def log_sigmoid(logit):
    return jnp.minimum(logit, 0.0) - jnp.log(1.0 + jnp.exp(-jnp.abs(logit)))


def conv_rows(rows, taps, masks, adjoint):
    _, _, up_ok, down_ok = masks
    left, middle, right = neighbours(rows, masks)
    parts = []
    for row in range(3):
        if adjoint:
            weights = [taps[:, 3 * (2 - row) + 2 - col : 3 * (2 - row) + 3 - col] for col in range(3)]
        else:
            weights = [taps[:, 3 * row + col : 3 * row + col + 1] for col in range(3)]
        parts.append(left * weights[0] + middle * weights[1] + right * weights[2])
    above = jnp.where(up_ok, shifted(parts[0], -GRID), 0.0)
    below = jnp.where(down_ok, shifted(parts[2], GRID), 0.0)
    return above + parts[1] + below


def decay_block(row, column):
    span = row.shape[1]
    key_at = lax.broadcasted_iota(jnp.int32, (span, span), 0)
    query_at = lax.broadcasted_iota(jnp.int32, (span, span), 1)
    return jnp.where(query_at >= key_at, jnp.exp(jnp.minimum(row - column, 0.0)), 0.0)


def mixer_kernel(heads, proj_ref, logit_ref, taps_ref, mixed_ref, rec_ref, states_ref, wide, cum_ref, col_ref):
    part, length = rec_ref.shape
    spans = length // SPAN
    log_forget = log_sigmoid(logit_ref[...])
    cum = running_sum(log_forget, SPAN)
    cum_ref[...] = cum
    col_ref[...] = jnp.transpose(cum)
    wide[...] = proj_ref[...].astype(jnp.float32)
    scale = HD ** (-0.5)

    def one_span(at, states):
        lanes = pl.ds(pl.multiple_of(at * SPAN, SPAN), SPAN)
        after = []
        for head in range(heads):
            at_rows = [pl.ds(kind * part + head * HD, HD) for kind in range(3)]
            query, key, value = (wide[rows, lanes] for rows in at_rows)
            row = cum_ref[head : head + 1, lanes]
            column = col_ref[lanes, head : head + 1]
            last = row[:, SPAN - 1 : SPAN]
            state = states[head]
            states_ref[at, head] = state
            weights = decay_block(row, column) * mm(low(key), low(query), TN)
            out = mm(low(value), low(weights), NN)
            out = out + mm(low(state), low(query * jnp.exp(row)), NN)
            rec_ref[pl.ds(head * HD, HD), lanes] = out * scale
            carried = low(key * jnp.exp(last - row))
            after.append(state * jnp.exp(last) + mm(low(value), carried, NT))
        return tuple(after)

    lax.fori_loop(0, spans, one_span, tuple(jnp.zeros((HD, HD), jnp.float32) for _ in range(heads)))
    masks = edge_masks(length)

    def one_group(at, carry):
        rows = pl.ds(pl.multiple_of(at * 16, 16), 16)
        mixed_ref[rows, :] = low(conv_rows(rec_ref[rows, :], taps_ref[rows, :], masks, False))
        return carry

    lax.fori_loop(0, part // 16, one_group, 0)


def mixer(proj, logit, taps, heads):
    part = proj.shape[0] // 3
    length = proj.shape[1]
    spans = length // SPAN
    return pl.pallas_call(
        functools.partial(mixer_kernel, heads),
        out_shape=(
            jax.ShapeDtypeStruct((part, length), jnp.bfloat16),
            jax.ShapeDtypeStruct((part, length), jnp.float32),
            jax.ShapeDtypeStruct((spans, heads, HD, HD), jnp.float32),
        ),
        in_specs=[pl.BlockSpec(memory_space=pltpu.VMEM)] * 3,
        out_specs=[pl.BlockSpec(memory_space=pltpu.VMEM)] * 3,
        scratch_shapes=[
            pltpu.VMEM((3 * part, length), jnp.float32),
            pltpu.VMEM((8, length), jnp.float32),
            pltpu.VMEM((length, 8), jnp.float32),
        ],
        compiler_params=pltpu.CompilerParams(vmem_limit_bytes=56 * 2**20),
        name="mixer",
    )(proj, logit, taps)


def back_kernel(
    heads, proj_ref, logit_ref, taps_ref, rec_ref, states_ref, grad_ref,
    gproj_ref, gtaps_ref, wide, gwide, cum_ref, col_ref, grec_ref, rows_ref,
):
    part, length = rec_ref.shape
    spans = length // SPAN
    logit = logit_ref[...]
    cum = running_sum(log_sigmoid(logit), SPAN)
    cum_ref[...] = cum
    col_ref[...] = jnp.transpose(cum)
    wide[...] = proj_ref[...].astype(jnp.float32)
    masks = edge_masks(length)
    scale = HD ** (-0.5)
    lane = lax.broadcasted_iota(jnp.int32, (16, 16), 1)

    def one_group(at, carry):
        rows = pl.ds(pl.multiple_of(at * 16, 16), 16)
        grad = grad_ref[rows, :].astype(jnp.float32)
        grec_ref[rows, :] = conv_rows(grad, taps_ref[rows, :], masks, True) * scale
        moved = neighbours(rec_ref[rows, :], masks)
        _, _, up_ok, down_ok = masks
        grads = (
            jnp.where(down_ok, shifted(grad, GRID), 0.0),
            grad,
            jnp.where(up_ok, shifted(grad, -GRID), 0.0),
        )
        result = jnp.zeros((16, 16), jnp.float32)
        for row in range(3):
            for col in range(3):
                one = jnp.sum(moved[col] * grads[row], axis=1, keepdims=True)
                result = jnp.where(lane == 3 * row + col, one, result)
        gtaps_ref[rows, :] = result
        return carry

    lax.fori_loop(0, part // 16, one_group, 0)
    rows_ref[...] = jnp.zeros_like(rows_ref)
    key_at = lax.broadcasted_iota(jnp.int32, (SPAN, SPAN), 0)
    query_at = lax.broadcasted_iota(jnp.int32, (SPAN, SPAN), 1)
    later = low(jnp.where(key_at >= query_at, 1.0, 0.0))

    def one_span(step, back_states):
        at = spans - 1 - step
        lanes = pl.ds(pl.multiple_of(at * SPAN, SPAN), SPAN)
        after = []
        for head in range(heads):
            at_rows = [pl.ds(kind * part + head * HD, HD) for kind in range(3)]
            query, key, value = (wide[rows, lanes] for rows in at_rows)
            grad = low(grec_ref[pl.ds(head * HD, HD), lanes])
            row = cum_ref[head : head + 1, lanes]
            column = col_ref[lanes, head : head + 1]
            last = row[:, SPAN - 1 : SPAN]
            state = states_ref[at, head]
            back = back_states[head]
            decay = decay_block(row, column)
            score = mm(low(key), low(query), TN)
            weights = decay * score
            grad_weights = mm(low(value), grad, TN)
            grad_score = grad_weights * decay
            product = low(grad_weights * weights)
            grad_score = low(grad_score)
            in_decay = jnp.exp(row)
            out_decay = jnp.exp(last - row)
            query_in = mm(low(state), grad, TN) * in_decay
            key_out = mm(low(back), low(value), TN) * out_decay
            gwide[at_rows[0], lanes] = mm(low(key), grad_score, NN) + query_in
            gwide[at_rows[1], lanes] = mm(low(query), grad_score, NT) + key_out
            carried = low(key * out_decay)
            gwide[at_rows[2], lanes] = mm(grad, low(weights), NT) + mm(low(back), carried, NN)
            inside = mm(product, later, NN)
            inside = jnp.sum(jnp.where(key_at < query_at, inside, 0.0), axis=0, keepdims=True)
            span_decay = jnp.exp(last)
            across = jnp.sum(back * state, keepdims=True) * span_decay
            rows_ref[0, head : head + 1, lanes] = jnp.sum(query * query_in, axis=0, keepdims=True)
            rows_ref[1, head : head + 1, lanes] = jnp.sum(key * key_out, axis=0, keepdims=True)
            rows_ref[2, head : head + 1, lanes] = inside + across
            after.append(back * span_decay + mm(grad, low(query * in_decay), NT))
        return tuple(after)

    lax.fori_loop(0, spans, one_span, tuple(jnp.zeros((HD, HD), jnp.float32) for _ in range(heads)))
    grad_log = (
        running_sum(rows_ref[0], SPAN, reverse=True)
        + running_sum(rows_ref[1], SPAN, exclusive=True)
        + rows_ref[2]
    )
    gwide[3 * part :, :] = jnp.zeros((gwide.shape[0] - 3 * part, length), jnp.float32)
    gwide[3 * part : 3 * part + heads, :] = (grad_log / (1.0 + jnp.exp(logit)))[:heads]
    gproj_ref[...] = low(gwide[...])


def mixer_back(proj, logit, taps, rec, states, grad, heads):
    part = proj.shape[0] // 3
    length = proj.shape[1]
    return pl.pallas_call(
        functools.partial(back_kernel, heads),
        out_shape=(
            jax.ShapeDtypeStruct((WIDE_ROWS, length), jnp.bfloat16),
            jax.ShapeDtypeStruct((part, 16), jnp.float32),
        ),
        in_specs=[pl.BlockSpec(memory_space=pltpu.VMEM)] * 6,
        out_specs=[pl.BlockSpec(memory_space=pltpu.VMEM)] * 2,
        scratch_shapes=[
            pltpu.VMEM((3 * part, length), jnp.float32),
            pltpu.VMEM((WIDE_ROWS, length), jnp.float32),
            pltpu.VMEM((8, length), jnp.float32),
            pltpu.VMEM((length, 8), jnp.float32),
            pltpu.VMEM((part, length), jnp.float32),
            pltpu.VMEM((3, 8, length), jnp.float32),
        ],
        compiler_params=pltpu.CompilerParams(vmem_limit_bytes=56 * 2**20),
        name="mixer_back",
    )(proj, logit, taps, rec, states, grad)


MESH = pl.DeviceIdType.MESH
CHUNK = 256
VMEM_LIMIT = 58 * 2**20
VMEM_SPEC = pl.BlockSpec(memory_space=pltpu.VMEM)
WIDE_ROWS = 896


def places():
    me = lax.axis_index("tensor")
    across = lax.rem(me + 2, 4)
    beside = me + 1 - 2 * lax.rem(me, 2)
    corner = lax.rem(beside + 2, 4)
    return me, across, beside, corner


def greet(peers):
    barrier = pltpu.get_barrier_semaphore()
    for peer in peers:
        pl.semaphore_signal(barrier, inc=1, device_id={"tensor": peer}, device_id_type=MESH)
    pl.semaphore_wait(barrier, len(peers))


def send(source, target, sems, at, peer):
    copy = pltpu.make_async_remote_copy(
        src_ref=source,
        dst_ref=target,
        send_sem=sems.at[0, at],
        recv_sem=sems.at[1, at],
        device_id={"tensor": peer},
        device_id_type=MESH,
    )
    copy.start()
    return copy


def shard(at, part):
    return pl.ds(pl.multiple_of(at * part, 32), part)


class Spread:
    def __init__(self, where, buffer, sems, part):
        self.me, self.across, self.beside, _ = where
        self.buffer, self.sems, self.part = buffer, sems, part
        self.far, self.near, self.on = {}, {}, {}

    def view(self, owner, lanes):
        return self.buffer.at[shard(owner, self.part), lanes]

    def start(self, k, lanes, source=None):
        block = self.view(self.me, lanes)
        source = block if source is None else source
        self.far[k] = send(source, block, self.sems, 3 * k, self.across)
        self.near[k] = send(source, block, self.sems, 3 * k + 1, self.beside)

    def relay(self, k, lanes):
        self.far[k].wait_recv()
        block = self.view(self.across, lanes)
        self.on[k] = send(block, block, self.sems, 3 * k + 2, self.beside)

    def end(self, k):
        self.near[k].wait_recv()
        self.on[k].wait_recv()

    def finish(self):
        for copies in (self.far, self.near, self.on):
            for copy in copies.values():
                copy.wait_send()


class Reduce:
    def __init__(self, where, part, bufs, sems):
        self.me, self.across, self.beside, self.corner = where
        self.part = part
        self.pair_out, self.pair_in, self.far_out, self.far_in, self.keep = bufs
        self.sems = sems
        self.pair, self.far = {}, {}

    def start(self, k, lanes, term):
        for index, owner in enumerate((self.corner, self.beside)):
            self.pair_out[index, :, lanes] = low(term(owner))
            self.pair[k, index] = send(
                self.pair_out.at[index, :, lanes],
                self.pair_in.at[index, :, lanes],
                self.sems,
                3 * k + index,
                self.beside,
            )
            self.keep[index, :, lanes] = term((self.across, self.me)[index])

    def relay(self, k, lanes, remote=True):
        self.pair[k, 0].wait_recv()
        block = low(self.keep[0, :, lanes] + self.pair_in[0, :, lanes].astype(jnp.float32))
        self.far_out[:, lanes] = block
        if remote:
            self.far[k] = send(
                self.far_out.at[:, lanes], self.far_in.at[:, lanes], self.sems, 3 * k + 2, self.across
            )

    def near_sum(self, k, lanes):
        self.pair[k, 1].wait_recv()
        return self.keep[1, :, lanes] + self.pair_in[1, :, lanes].astype(jnp.float32)

    def end(self, k, lanes):
        total = self.near_sum(k, lanes)
        self.far[k].wait_recv()
        return total + self.far_in[:, lanes].astype(jnp.float32)

    def finish(self):
        for copies in (self.pair, self.far):
            for copy in copies.values():
                copy.wait_send()


class Rows:
    def __init__(self, where, buffer, sems):
        self.me, self.peers = where[0], where[1:]
        self.buffer, self.sems = buffer, sems
        self.copies = {}

    def start(self, k, lanes, first, second):
        self.buffer[self.me, 0:1, lanes] = first
        self.buffer[self.me, 1:2, lanes] = second
        block = self.buffer.at[self.me, :, lanes]
        self.copies[k] = [
            send(block, block, self.sems, 3 * k + index, peer) for index, peer in enumerate(self.peers)
        ]

    def end(self, k, lanes):
        for copy in self.copies[k]:
            copy.wait_recv()
        total = sum(self.buffer[index, :, lanes] for index in range(4))
        return total[0:1], total[1:2]

    def finish(self):
        for copies in self.copies.values():
            for copy in copies:
                copy.wait_send()


def reduce_scratch(part, length):
    return [
        pltpu.VMEM((2, part, length), jnp.bfloat16),
        pltpu.VMEM((2, part, length), jnp.bfloat16),
        pltpu.VMEM((part, length), jnp.bfloat16),
        pltpu.VMEM((part, length), jnp.bfloat16),
        pltpu.VMEM((2, part, length), jnp.float32),
    ]


def copy_sems(count):
    return pltpu.SemaphoreType.DMA((2, count))


def column_sums(rows):
    return jnp.sum(rows, axis=1, keepdims=True)


def row_sums(rows):
    return jnp.sum(rows, axis=0, keepdims=True)


def open_kernel(
    x_ref, cot_ref, silu_ref, ada_ref, bias_ref, qkv_ref, gate_ref, gate_bias_ref,
    normed_ref, proj_ref, logit_ref, stats_ref, mods_ref, gmlp_ref, wback_ref,
    raw, rows, wide, raw_sems, row_sems,
):
    part, length = x_ref.shape
    width = 4 * part
    chunks = length // CHUNK
    lanes = [pl.ds(k * CHUNK, CHUNK) for k in range(chunks)]
    where = places()
    me, _, _, _ = where
    greet(where[1:])
    spread = Spread(where, raw, raw_sems, part)
    for k in range(chunks):
        spread.start(k, lanes[k], x_ref.at[:, lanes[k]])
    raw[shard(me, part), :] = x_ref[...]

    row_at = lax.broadcasted_iota(jnp.int32, (8, part), 0)
    mods = bias_ref[:, :part]
    silu = silu_ref[...]
    for index in range(6):
        product = mm(silu, ada_ref[index * part : (index + 1) * part, :], NT)
        mods = mods + jnp.where(row_at == index, product, 0.0)
    rows[me] = bias_ref[...]
    rows[me, :, :part] = mods
    row_copies = [
        send(rows.at[me], rows.at[me], row_sems, index, peer) for index, peer in enumerate(where[1:])
    ]
    own_mods = jnp.transpose(rows[me])[:part]
    mods_ref[...] = own_mods
    gmlp_ref[...] = low(cot_ref[...].astype(jnp.float32) * own_mods[:, 5:6])
    projected = qkv_ref.shape[0]
    wide[:projected, :] = qkv_ref[...]
    wide[projected:, :] = gate_ref[...]
    wback_ref[...] = jnp.transpose(wide[...])
    for copy in row_copies:
        copy.wait_recv()
    columns = [jnp.transpose(rows[index])[:part] for index in range(4)]

    def one_chunk(k):
        spread.end(k)
        blocks = [raw[index * part : (index + 1) * part, lanes[k]].astype(jnp.float32) for index in range(4)]
        mean = sum(row_sums(block) for block in blocks) / width
        square = sum(row_sums(block * block) for block in blocks) / width
        inv_std = lax.rsqrt(square - mean * mean + norm_eps)
        stats_ref[0:1, lanes[k]] = mean
        stats_ref[1:2, lanes[k]] = inv_std
        for index in range(4):
            unit = (blocks[index] - mean) * inv_std
            normed = unit * (1.0 + columns[index][:, 1:2]) + columns[index][:, 0:1]
            normed_ref[index * part : (index + 1) * part, lanes[k]] = low(normed)
        product = mm(wide[...], normed_ref[:, lanes[k]], NN)
        proj_ref[:, lanes[k]] = low(product[:projected])
        logit_ref[:, lanes[k]] = product[projected : projected + 8] + gate_bias_ref[...]

    stats_ref[2:, :] = jnp.zeros((6, length), jnp.float32)
    for k in range(chunks):
        spread.relay(k, lanes[k])
        if k > 0:
            one_chunk(k - 1)
    one_chunk(chunks - 1)
    spread.finish()
    for copy in row_copies:
        copy.wait_send()


def open_layer(x, cot, silu, ada, bias, qkv, gate, gate_bias):
    part, length = x.shape
    width = 4 * part
    chunks = length // CHUNK
    shape = jax.ShapeDtypeStruct
    return pl.pallas_call(
        open_kernel,
        out_shape=(
            shape((width, length), jnp.bfloat16),
            shape((3 * part, length), jnp.bfloat16),
            shape((8, length), jnp.float32),
            shape((8, length), jnp.float32),
            shape((part, 8), jnp.float32),
            shape((part, length), jnp.bfloat16),
            shape((width, WIDE_ROWS), jnp.bfloat16),
        ),
        in_specs=[VMEM_SPEC] * 8,
        out_specs=[VMEM_SPEC] * 7,
        scratch_shapes=[
            pltpu.VMEM((width, length), jnp.bfloat16),
            pltpu.VMEM((4, 8, bias.shape[1]), jnp.float32),
            pltpu.VMEM((WIDE_ROWS, width), jnp.bfloat16),
            copy_sems(3 * chunks),
            copy_sems(3),
        ],
        compiler_params=pltpu.CompilerParams(
            collective_id=1, has_side_effects=True, vmem_limit_bytes=VMEM_LIMIT
        ),
        name="open_layer",
    )(x, cot, silu, ada, bias, qkv, gate, gate_bias)


GELU_SLOPE = math.sqrt(2.0 / math.pi)
GELU_CUBE = 0.044715


def middle_kernel(
    mix_ref, x_ref, mods_ref, gmlp_ref, gmlp_far_ref, cot_ref, out_w_ref, up_ref, down_ref,
    attn_ref, after_ref, mlp_keep_ref, mlp_send_ref, gafter_ref, gattn_ref, gmix_ref, gup_ref, gdown_ref,
    gout_ref, sums_ref,
    out_t, turned, gmlp, gact, normed, act, gup_rows, unit,
    a_pair_out, a_pair_in, a_far_out, a_far_in, a_keep,
    g_pair_out, g_pair_in, g_far_out, g_far_in, g_keep,
    first_rows, second_rows,
    gm_sems, a_sems, n_sems, g_sems, t_sems, m_sems, first_sems, second_sems,
):
    part, length = x_ref.shape
    width = 4 * part
    hidden = up_ref.shape[1]
    chunks = length // CHUNK
    lanes = [pl.ds(k * CHUNK, CHUNK) for k in range(chunks)]
    where = places()
    me, across, beside, _ = where
    first_rows[...] = jnp.zeros_like(first_rows)
    second_rows[...] = jnp.zeros_like(second_rows)
    greet(where[1:])
    own, other = shard(me, part), shard(across, part)
    gm_copies = [
        send(gmlp_ref, gmlp.at[own, :], gm_sems, 0, beside),
        send(gmlp_far_ref, gmlp.at[other, :], gm_sems, 1, beside),
    ]
    gmlp[own, :] = gmlp_ref[...]
    gmlp[other, :] = gmlp_far_ref[...]
    gate_one, scale_two, shift_two = mods_ref[:, 2:3], mods_ref[:, 4:5], mods_ref[:, 3:4]

    attn_sum = Reduce(where, part, (a_pair_out, a_pair_in, a_far_out, a_far_in, a_keep), a_sems)
    grad_sum = Reduce(where, part, (g_pair_out, g_pair_in, g_far_out, g_far_in, g_keep), g_sems)
    norm_spread = Spread(where, normed, n_sems, part)
    grad_spread = Spread(where, gattn_ref, t_sems, part)
    moments = Rows(where, first_rows, first_sems)
    means = Rows(where, second_rows, second_sems)

    out_t[...] = jnp.transpose(out_w_ref[...])
    sums_ref[...] = jnp.zeros_like(sums_ref)

    def attn_start(k):
        mixed = mix_ref[:, lanes[k]]
        attn_sum.start(k, lanes[k], lambda owner: mm(out_t[shard(owner, part), :], mixed, NN))

    def attn_end(k):
        attn = attn_sum.end(k, lanes[k])
        attn_ref[:, lanes[k]] = attn
        after = x_ref[:, lanes[k]].astype(jnp.float32) + gate_one * attn
        after_ref[:, lanes[k]] = after
        moments.start(k, lanes[k], row_sums(after), row_sums(after * after))

    inverse = [None] * chunks

    def norm_chunk(k):
        total, squares = moments.end(k, lanes[k])
        mean = total / width
        inverse[k] = lax.rsqrt(squares / width - mean * mean + norm_eps)
        rows = (after_ref[:, lanes[k]] - mean) * inverse[k]
        unit[:, lanes[k]] = rows
        normed[own, lanes[k]] = low(rows * (1.0 + scale_two) + shift_two)
        norm_spread.start(k, lanes[k])

    def grad_act_chunk(k):
        gact[:, lanes[k]] = mm(down_ref[...], gmlp[:, lanes[k]], NN)

    def hidden_chunk(k):
        norm_spread.end(k)
        block = normed[:, lanes[k]]

        def one_block(at, carry):
            rows = pl.ds(pl.multiple_of(at * part, 32), part)
            up = mm(turned[rows, :], block, NN)
            square = up * up
            bend = jnp.tanh(GELU_SLOPE * up * (1.0 + GELU_CUBE * square))
            half = 0.5 * (1.0 + bend)
            act[rows, lanes[k]] = low(up * half)
            slope = half + 0.5 * up * (1.0 - bend * bend) * GELU_SLOPE * (1.0 + 3.0 * GELU_CUBE * square)
            gup_rows[rows, lanes[k]] = low(gact[rows, lanes[k]] * slope)
            return carry

        lax.fori_loop(0, hidden // part, one_block, 0)

    def grad_start(k):
        block = gup_rows[:, lanes[k]]
        grad_sum.start(k, lanes[k], lambda owner: mm(up_ref[shard(owner, part), :], block, NN))

    def grad_end(k):
        grad = grad_sum.end(k, lanes[k])
        rows = unit[:, lanes[k]]
        sums_ref[:, 3:4] += column_sums(grad)
        sums_ref[:, 4:5] += column_sums(grad * rows)
        scaled = grad * (1.0 + scale_two)
        gafter_ref[:, lanes[k]] = scaled
        means.start(k, lanes[k], row_sums(scaled), row_sums(scaled * rows))

    def after_chunk(k):
        total, along = means.end(k, lanes[k])
        scaled = gafter_ref[:, lanes[k]]
        back = inverse[k] * (scaled - total / width - unit[:, lanes[k]] * (along / width))
        grad = cot_ref[:, lanes[k]].astype(jnp.float32) + back
        gafter_ref[:, lanes[k]] = grad
        gattn_ref[own, lanes[k]] = low(grad * gate_one)
        grad_spread.start(k, lanes[k])
        sums_ref[:, 2:3] += column_sums(grad * attn_ref[:, lanes[k]])

    def mixed_chunk(k):
        grad_spread.end(k)
        gmix_ref[:, lanes[k]] = mm(out_w_ref[...], gattn_ref[:, lanes[k]], NN)

    def weight_grad(target, left, right, half):
        rows = target.shape[0] // 2
        target[half * rows : (half + 1) * rows, :] = low(mm(left[half * rows : (half + 1) * rows, :], right[...], NT))

    mlp_sum = Reduce(where, part, (a_pair_out, a_pair_in, mlp_send_ref, None, a_keep), m_sems)

    def mlp_start(k):
        block = act[:, lanes[k]]
        mlp_sum.start(k, lanes[k], lambda owner: mm(turned[shard(owner, part), :], block, NN))

    def mlp_end(k):
        mlp_sum.relay(k, lanes[k], remote=False)
        mlp_keep_ref[:, lanes[k]] = mlp_sum.near_sum(k, lanes[k])

    attn_start(0)
    attn_start(1)
    attn_sum.relay(0, lanes[0])
    attn_start(2)
    attn_sum.relay(1, lanes[1])
    attn_start(3)
    attn_sum.relay(2, lanes[2])
    turned[...] = jnp.transpose(up_ref[...])
    attn_sum.relay(3, lanes[3])
    attn_end(0)
    for copy in gm_copies:
        copy.wait_recv()
    grad_act_chunk(0)
    attn_end(1)
    norm_chunk(0)
    grad_act_chunk(1)
    attn_end(2)
    norm_chunk(1)
    grad_act_chunk(2)
    attn_end(3)
    norm_chunk(2)
    norm_spread.relay(0, lanes[0])
    grad_act_chunk(3)
    norm_chunk(3)
    norm_spread.relay(1, lanes[1])
    hidden_chunk(0)
    grad_start(0)
    norm_spread.relay(2, lanes[2])
    hidden_chunk(1)
    grad_sum.relay(0, lanes[0])
    grad_start(1)
    norm_spread.relay(3, lanes[3])
    hidden_chunk(2)
    grad_sum.relay(1, lanes[1])
    grad_start(2)
    grad_end(0)
    hidden_chunk(3)
    grad_sum.relay(2, lanes[2])
    after_chunk(0)
    grad_start(3)
    grad_end(1)
    grad_sum.relay(3, lanes[3])
    after_chunk(1)
    grad_end(2)
    weight_grad(gdown_ref, gmlp, act, 0)
    grad_spread.relay(0, lanes[0])
    after_chunk(2)
    grad_end(3)
    weight_grad(gdown_ref, gmlp, act, 1)
    after_chunk(3)
    grad_spread.relay(1, lanes[1])
    mixed_chunk(0)
    attn_sum.finish()
    turned[...] = jnp.transpose(down_ref[...])
    weight_grad(gup_ref, normed, gup_rows, 0)
    grad_spread.relay(2, lanes[2])
    mixed_chunk(1)
    weight_grad(gup_ref, normed, gup_rows, 1)
    grad_spread.relay(3, lanes[3])
    mixed_chunk(2)
    mlp_start(0)
    mlp_start(1)
    mlp_end(0)
    mixed_chunk(3)
    mlp_start(2)
    mlp_end(1)
    mlp_start(3)
    mlp_end(2)
    gout_ref[...] = low(mm(gattn_ref[...], mix_ref[...], NT))
    mlp_end(3)
    for copy in gm_copies:
        copy.wait_send()
    for group in (norm_spread, grad_spread, grad_sum, mlp_sum, moments, means):
        group.finish()


def middle_layer(mix, x, mods, gmlp, gmlp_far, cot, out_w, up, down):
    part, length = x.shape
    width = 4 * part
    hidden = up.shape[1]
    chunks = length // CHUNK
    shape = jax.ShapeDtypeStruct
    return pl.pallas_call(
        middle_kernel,
        out_shape=(
            shape((part, length), jnp.float32),
            shape((part, length), jnp.float32),
            shape((part, length), jnp.float32),
            shape((part, length), jnp.bfloat16),
            shape((part, length), jnp.float32),
            shape((width, length), jnp.bfloat16),
            shape((part, length), jnp.float32),
            shape((width, hidden), jnp.bfloat16),
            shape((width, hidden), jnp.bfloat16),
            shape((width, part), jnp.bfloat16),
            shape((part, 8), jnp.float32),
        ),
        in_specs=[VMEM_SPEC] * 9,
        out_specs=[VMEM_SPEC] * 11,
        scratch_shapes=[
            pltpu.VMEM((width, part), jnp.bfloat16),
            pltpu.VMEM((hidden, width), jnp.bfloat16),
            pltpu.VMEM((width, length), jnp.bfloat16),
            pltpu.VMEM((hidden, length), jnp.float32),
            pltpu.VMEM((width, length), jnp.bfloat16),
            pltpu.VMEM((hidden, length), jnp.bfloat16),
            pltpu.VMEM((hidden, length), jnp.bfloat16),
            pltpu.VMEM((part, length), jnp.float32),
            *reduce_scratch(part, length),
            *reduce_scratch(part, length),
            pltpu.VMEM((4, 8, length), jnp.float32),
            pltpu.VMEM((4, 8, length), jnp.float32),
            copy_sems(2),
            *[copy_sems(3 * chunks)] * 7,
        ],
        compiler_params=pltpu.CompilerParams(
            collective_id=2, has_side_effects=True, vmem_limit_bytes=VMEM_LIMIT
        ),
        name="middle_layer",
    )(mix, x, mods, gmlp, gmlp_far, cot, out_w, up, down)


def close_kernel(
    gproj_ref, wback_ref, normed_ref, x_ref, stats_ref, mods_ref, gafter_ref, after_ref, cot_ref,
    mlp_keep_ref, mlp_far_ref, sums_ref,
    gtokens_ref, out_ref, gqkv_ref, gmods_ref,
    pair_out, pair_in, far_out, far_in, keep, mean_rows, sum_sems, mean_sems,
):
    part, length = x_ref.shape
    width = 4 * part
    chunks = length // CHUNK
    lanes = [pl.ds(k * CHUNK, CHUNK) for k in range(chunks)]
    where = places()
    mean_rows[...] = jnp.zeros_like(mean_rows)
    greet(where[1:])
    total_sum = Reduce(where, part, (pair_out, pair_in, far_out, far_in, keep), sum_sems)
    means = Rows(where, mean_rows, mean_sems)
    scale_one, gate_two = mods_ref[:, 1:2], mods_ref[:, 5:6]
    gmods_ref[...] = sums_ref[...]

    def start(k):
        block = gproj_ref[:, lanes[k]]
        total_sum.start(k, lanes[k], lambda owner: mm(wback_ref[shard(owner, part), :], block, NN))

    def unit_of(k):
        return (x_ref[:, lanes[k]].astype(jnp.float32) - stats_ref[0:1, lanes[k]]) * stats_ref[1:2, lanes[k]]

    def end(k):
        grad = total_sum.end(k, lanes[k])
        unit = unit_of(k)
        gmods_ref[:, 0:1] += column_sums(grad)
        gmods_ref[:, 1:2] += column_sums(grad * unit)
        scaled = grad * (1.0 + scale_one)
        gtokens_ref[:, lanes[k]] = scaled
        means.start(k, lanes[k], row_sums(scaled), row_sums(scaled * unit))

    def tokens(k):
        total, along = means.end(k, lanes[k])
        back = gtokens_ref[:, lanes[k]] - total / width - unit_of(k) * (along / width)
        gtokens_ref[:, lanes[k]] = gafter_ref[:, lanes[k]] + stats_ref[1:2, lanes[k]] * back

    def outputs(k):
        mlp = mlp_keep_ref[:, lanes[k]] + mlp_far_ref[:, lanes[k]].astype(jnp.float32)
        out_ref[:, lanes[k]] = low(after_ref[:, lanes[k]] + gate_two * mlp)
        gmods_ref[:, 5:6] += column_sums(cot_ref[:, lanes[k]].astype(jnp.float32) * mlp)

    def weight_grad(quarter):
        rows = pl.ds(quarter * part, part)
        gqkv_ref[rows, :] = low(mm(normed_ref[rows, :], gproj_ref[...], NT))

    start(0)
    start(1)
    total_sum.relay(0, lanes[0])
    start(2)
    total_sum.relay(1, lanes[1])
    start(3)
    total_sum.relay(2, lanes[2])
    outputs(0)
    total_sum.relay(3, lanes[3])
    for k in range(chunks):
        if k > 0:
            outputs(k)
        weight_grad(k)
        end(k)
        if k > 0:
            tokens(k - 1)
    tokens(chunks - 1)
    total_sum.finish()
    means.finish()


def close_layer(gproj, wback, normed, x, stats, mods, gafter, after, cot, mlp_keep, mlp_far, sums):
    part, length = x.shape
    width = 4 * part
    chunks = length // CHUNK
    shape = jax.ShapeDtypeStruct
    return pl.pallas_call(
        close_kernel,
        out_shape=(
            shape((part, length), jnp.float32),
            shape((part, length), jnp.bfloat16),
            shape((width, WIDE_ROWS), jnp.bfloat16),
            shape((part, 8), jnp.float32),
        ),
        in_specs=[VMEM_SPEC] * 12,
        out_specs=[VMEM_SPEC] * 4,
        scratch_shapes=[
            *reduce_scratch(part, length),
            pltpu.VMEM((4, 8, length), jnp.float32),
            copy_sems(3 * chunks),
            copy_sems(3 * chunks),
        ],
        compiler_params=pltpu.CompilerParams(
            collective_id=3, has_side_effects=True, vmem_limit_bytes=VMEM_LIMIT
        ),
        name="close_layer",
    )(gproj, wback, normed, x, stats, mods, gafter, after, cot, mlp_keep, mlp_far, sums)


def dp_total(partial, shard_count):
    rows, columns = partial.shape
    own = rows // shard_count
    spots = shard_count // 2
    at = lax.axis_index("dp")
    spot, side = at // 2, lax.rem(at, 2)
    blocks = partial.reshape(spots, 2, own, columns)
    outgoing = lax.dynamic_index_in_dim(blocks, 1 - side, axis=1, keepdims=False)
    kept = lax.dynamic_index_in_dim(blocks, side, axis=1, keepdims=False)
    arrived = lax.ppermute(outgoing, "dp", [(index, index ^ 1) for index in range(shard_count)])
    half = low(kept.astype(jnp.float32) + arrived.astype(jnp.float32))
    if spots > 4:
        groups = [[2 * index + bit for index in range(spots)] for bit in range(2)]
        total = lax.psum_scatter(
            half.reshape(spots * own, columns), "dp", scatter_dimension=0, axis_index_groups=groups, tiled=True
        )
        return total.astype(jnp.float32)
    total = lax.dynamic_index_in_dim(half, spot, axis=0, keepdims=False).astype(jnp.float32)
    for step in range(1, spots):
        block = lax.dynamic_index_in_dim(half, lax.rem(spot + step, spots), axis=0, keepdims=False)
        moved = lax.ppermute(
            block, "dp", [(index, (index + 2 * step) % shard_count) for index in range(shard_count)]
        )
        total = total + moved.astype(jnp.float32)
    return total


def shards(
    latent_tokens,
    timesteps,
    labels,
    class_table,
    ada_weight,
    ada_bias,
    query_key_value_weight,
    gate_weight,
    gate_bias,
    conv_weight,
    out_weight,
    up_weight,
    down_weight,
    cotangent,
):
    _, length, part = latent_tokens.shape
    heads = gate_weight.shape[1]
    hidden = up_weight.shape[1]
    shard_count = lax.psum(1, "dp")
    shard_at = lax.axis_index("dp")
    own_width = MODEL_DIM // shard_count
    x = latent_tokens[0].T
    cot = cotangent[0].T
    qkv = jnp.transpose(query_key_value_weight, (1, 2, 0)).reshape(3 * part, MODEL_DIM)
    ada = jnp.transpose(ada_weight, (1, 2, 0)).reshape(6 * part, MODEL_DIM)
    gate = jnp.pad(gate_weight.T, ((0, WIDE_ROWS - 3 * part - heads), (0, 0)))
    gate_column = jnp.pad(gate_bias.astype(jnp.float32), (0, 8 - heads))[:, None]
    bias_rows = jnp.pad(ada_bias.astype(jnp.float32), ((0, 2), (0, -part % 128)))
    taps = jnp.pad(conv_weight.astype(jnp.float32).reshape(9, part).T, ((0, 0), (0, 7)))

    cond = lax.dynamic_slice_in_dim(class_table, labels[0], 1, axis=0).astype(jnp.float32) + embed_time(
        timesteps, MODEL_DIM
    )
    silu_cond = low(jax.nn.silu(cond))
    normed_one, projected, forget_logit, stats, mods, grad_mlp, wide_back = open_layer(
        x, cot, jnp.broadcast_to(silu_cond, (8, MODEL_DIM)), ada, bias_rows, qkv, gate, gate_column
    )
    swap_chips = [(0, 2), (1, 3), (2, 0), (3, 1)]
    grad_mlp_far = lax.ppermute(grad_mlp, "tensor", swap_chips)
    mixed_low, recurrent, states = mixer(projected, forget_logit, taps, heads)
    (
        _,
        after_attn,
        mlp_keep,
        mlp_send,
        grad_after,
        _,
        grad_mixed,
        grad_up,
        grad_down,
        grad_out_w,
        sums_two,
    ) = middle_layer(mixed_low, x, mods, grad_mlp, grad_mlp_far, cot, out_weight, up_weight, down_weight)
    mlp_far = lax.ppermute(mlp_send, "tensor", swap_chips)
    grad_down = dp_total(grad_down, shard_count)
    grad_up = dp_total(grad_up, shard_count)
    grad_out_w = dp_total(grad_out_w, shard_count)
    grad_projected, grad_taps = mixer_back(projected, forget_logit, taps, recurrent, states, grad_mixed, heads)
    grad_tokens, layer_out, grad_wide, grad_mod_columns = close_layer(
        grad_projected, wide_back, normed_one, x, stats, mods, grad_after, after_attn, cot, mlp_keep, mlp_far, sums_two
    )
    grad_wide = dp_total(grad_wide, shard_count)

    grad_mods = low(grad_mod_columns.T[:6])
    mods_flat = grad_mods.reshape(1, 6 * part)
    grad_silu = mm(mods_flat, ada, NN)
    grad_gate_b = jnp.sum(grad_projected[3 * part : 3 * part + heads].astype(jnp.float32), axis=1)
    small = jnp.concatenate(
        [
            mods_flat.astype(jnp.float32).reshape(6 * part),
            lax.psum(grad_silu, "tensor").reshape(MODEL_DIM),
            cond.reshape(MODEL_DIM),
            grad_gate_b,
            grad_taps[:, :9].T.reshape(9 * part),
        ]
    )
    every = lax.all_gather(small, "dp", axis=0, tiled=False)
    every_labels = lax.all_gather(labels, "dp", axis=0, tiled=True)
    sizes = [6 * part, MODEL_DIM, MODEL_DIM, heads, 9 * part]
    starts = [sum(sizes[:index]) for index in range(len(sizes) + 1)]
    every_mods, every_silu, every_cond, every_gate_b, every_conv = (
        every[:, begin:end] for begin, end in zip(starts[:-1], starts[1:])
    )
    grad_ada_b = jnp.sum(every_mods, axis=0).reshape(6, part)
    grad_gate_b = jnp.sum(every_gate_b, axis=0)
    grad_conv = jnp.sum(every_conv, axis=0).reshape(3, 3, part)

    def own_columns(rows):
        return lax.dynamic_slice_in_dim(rows, shard_at * own_width, own_width, axis=1)

    own_silu, own_pull = jax.vjp(jax.nn.silu, own_columns(every_cond))
    own_cond = own_pull(own_columns(every_silu))[0]
    grad_ada_w = mm(low(own_silu), low(every_mods), TN).reshape(own_width, 6, part)
    every_onehot = every_labels[:, None] == jnp.arange(NCLASS, dtype=jnp.int32)[None, :]
    grad_class = jnp.dot(every_onehot.astype(jnp.float32).T, own_cond, precision=TOP_PRECISION)
    return (
        layer_out.T[None],
        grad_tokens.T[None],
        grad_class,
        grad_ada_w,
        grad_ada_b,
        grad_wide[:, : 3 * part].reshape(own_width, 3, part),
        grad_wide[:, 3 * part : 3 * part + heads],
        grad_gate_b,
        grad_conv,
        grad_out_w.T,
        grad_up,
        grad_down.T,
    )


def solution(mesh):
    in_specs = (
        P("dp", None, "tensor"),
        P("dp"),
        P("dp"),
        P(),
        P(None, None, "tensor"),
        P(None, "tensor"),
        P(None, None, "tensor"),
        P(None, "tensor"),
        P("tensor"),
        P(None, None, "tensor"),
        P("tensor", None),
        P(None, "tensor"),
        P("tensor", None),
        P("dp", None, "tensor"),
    )
    out_specs = (
        P("dp", None, "tensor"),
        P("dp", None, "tensor"),
        P(None, "dp"),
        P("dp", None, "tensor"),
        P(None, "tensor"),
        P("dp", None, "tensor"),
        P("dp", "tensor"),
        P("tensor"),
        P(None, None, "tensor"),
        P("tensor", "dp"),
        P("dp", "tensor"),
        P("tensor", "dp"),
    )
    return jax.shard_map(shards, mesh=mesh, in_specs=in_specs, out_specs=out_specs, check_vma=False)
```

```python
import functools
import math

import jax
import jax.numpy as jnp
from jax import lax
from jax.experimental import pallas as pl
from jax.experimental.pallas import tpu as pltpu
from jax.sharding import PartitionSpec as P

MODEL_DIM = 1152
HD = 72
NCLASS = 1000
GRID = 32


TOP_PRECISION = lax.Precision.HIGHEST
norm_eps = 1e-06


def embed_time(time_steps, model_width):
    half_width = model_width // 2
    frequency = jnp.exp(-math.log(10000.0) * jnp.arange(half_width, dtype=jnp.float32) / half_width)
    angles = time_steps.astype(jnp.float32)[:, None] * frequency[None, :]
    return jnp.concatenate([jnp.cos(angles), jnp.sin(angles)], axis=1)


SPAN = 256

TN = (((0,), (0,)), ((), ()))
NT = (((1,), (1,)), ((), ()))
NN = (((1,), (0,)), ((), ()))


def mm(left, right, form):
    return lax.dot_general(left, right, form, preferred_element_type=jnp.float32)


def low(values):
    return values.astype(jnp.bfloat16)


def shifted(rows, offset):
    length = rows.shape[1]
    return pltpu.roll(rows, (-offset) % length, 1)


def edge_masks(length):
    token = lax.broadcasted_iota(jnp.int32, (1, length), 1)
    column = lax.rem(token, GRID)
    return column > 0, column < GRID - 1, token >= GRID, token < length - GRID


def neighbours(rows, masks):
    left_ok, right_ok, _, _ = masks
    return (
        jnp.where(left_ok, shifted(rows, -1), 0.0),
        rows,
        jnp.where(right_ok, shifted(rows, 1), 0.0),
    )


def running_sum(rows, span, reverse=False, exclusive=False):
    length = rows.shape[1]
    place = lax.rem(lax.broadcasted_iota(jnp.int32, (1, length), 1), span)
    total = rows
    step = 1
    if exclusive:
        total = (
            jnp.where(place < span - 1, shifted(total, 1), 0.0)
            if reverse
            else jnp.where(place >= 1, shifted(total, -1), 0.0)
        )
    while step < span:
        if reverse:
            total = total + jnp.where(place < span - step, shifted(total, step), 0.0)
        else:
            total = total + jnp.where(place >= step, shifted(total, -step), 0.0)
        step *= 2
    return total


def log_sigmoid(logit):
    return jnp.minimum(logit, 0.0) - jnp.log(1.0 + jnp.exp(-jnp.abs(logit)))


def conv_rows(rows, taps, masks, adjoint):
    _, _, up_ok, down_ok = masks
    left, middle, right = neighbours(rows, masks)
    parts = []
    for row in range(3):
        if adjoint:
            weights = [taps[:, 3 * (2 - row) + 2 - col : 3 * (2 - row) + 3 - col] for col in range(3)]
        else:
            weights = [taps[:, 3 * row + col : 3 * row + col + 1] for col in range(3)]
        parts.append(left * weights[0] + middle * weights[1] + right * weights[2])
    above = jnp.where(up_ok, shifted(parts[0], -GRID), 0.0)
    below = jnp.where(down_ok, shifted(parts[2], GRID), 0.0)
    return above + parts[1] + below


def decay_block(row, column):
    span = row.shape[1]
    key_at = lax.broadcasted_iota(jnp.int32, (span, span), 0)
    query_at = lax.broadcasted_iota(jnp.int32, (span, span), 1)
    return jnp.where(query_at >= key_at, jnp.exp(jnp.minimum(row - column, 0.0)), 0.0)


def mixer_kernel(heads, proj_ref, logit_ref, taps_ref, mixed_ref, rec_ref, states_ref, wide, cum_ref, col_ref):
    part, length = rec_ref.shape
    spans = length // SPAN
    log_forget = log_sigmoid(logit_ref[...])
    cum = running_sum(log_forget, SPAN)
    cum_ref[...] = cum
    col_ref[...] = jnp.transpose(cum)
    wide[...] = proj_ref[...].astype(jnp.float32)
    scale = HD ** (-0.5)

    def one_span(at, states):
        lanes = pl.ds(pl.multiple_of(at * SPAN, SPAN), SPAN)
        after = []
        for head in range(heads):
            at_rows = [pl.ds(kind * part + head * HD, HD) for kind in range(3)]
            query, key, value = (wide[rows, lanes] for rows in at_rows)
            row = cum_ref[head : head + 1, lanes]
            column = col_ref[lanes, head : head + 1]
            last = row[:, SPAN - 1 : SPAN]
            state = states[head]
            states_ref[at, head] = state
            weights = decay_block(row, column) * mm(low(key), low(query), TN)
            out = mm(low(value), low(weights), NN)
            out = out + mm(low(state), low(query * jnp.exp(row)), NN)
            rec_ref[pl.ds(head * HD, HD), lanes] = out * scale
            carried = low(key * jnp.exp(last - row))
            after.append(state * jnp.exp(last) + mm(low(value), carried, NT))
        return tuple(after)

    lax.fori_loop(0, spans, one_span, tuple(jnp.zeros((HD, HD), jnp.float32) for _ in range(heads)))
    masks = edge_masks(length)

    def one_group(at, carry):
        rows = pl.ds(pl.multiple_of(at * 16, 16), 16)
        mixed_ref[rows, :] = low(conv_rows(rec_ref[rows, :], taps_ref[rows, :], masks, False))
        return carry

    lax.fori_loop(0, part // 16, one_group, 0)


def mixer(proj, logit, taps, heads):
    part = proj.shape[0] // 3
    length = proj.shape[1]
    spans = length // SPAN
    return pl.pallas_call(
        functools.partial(mixer_kernel, heads),
        out_shape=(
            jax.ShapeDtypeStruct((part, length), jnp.bfloat16),
            jax.ShapeDtypeStruct((part, length), jnp.float32),
            jax.ShapeDtypeStruct((spans, heads, HD, HD), jnp.float32),
        ),
        in_specs=[pl.BlockSpec(memory_space=pltpu.VMEM)] * 3,
        out_specs=[pl.BlockSpec(memory_space=pltpu.VMEM)] * 3,
        scratch_shapes=[
            pltpu.VMEM((3 * part, length), jnp.float32),
            pltpu.VMEM((8, length), jnp.float32),
            pltpu.VMEM((length, 8), jnp.float32),
        ],
        compiler_params=pltpu.CompilerParams(vmem_limit_bytes=56 * 2**20),
        cost_estimate=work_for(11),
        name="mixer",
    )(proj, logit, taps)


def back_kernel(
    heads, proj_ref, logit_ref, taps_ref, rec_ref, states_ref, grad_ref,
    gproj_ref, gtaps_ref, wide, gwide, cum_ref, col_ref, grec_ref, rows_ref,
):
    part, length = rec_ref.shape
    spans = length // SPAN
    logit = logit_ref[...]
    cum = running_sum(log_sigmoid(logit), SPAN)
    cum_ref[...] = cum
    col_ref[...] = jnp.transpose(cum)
    wide[...] = proj_ref[...].astype(jnp.float32)
    masks = edge_masks(length)
    scale = HD ** (-0.5)
    lane = lax.broadcasted_iota(jnp.int32, (16, 16), 1)

    def one_group(at, carry):
        rows = pl.ds(pl.multiple_of(at * 16, 16), 16)
        grad = grad_ref[rows, :].astype(jnp.float32)
        grec_ref[rows, :] = conv_rows(grad, taps_ref[rows, :], masks, True) * scale
        moved = neighbours(rec_ref[rows, :], masks)
        _, _, up_ok, down_ok = masks
        grads = (
            jnp.where(down_ok, shifted(grad, GRID), 0.0),
            grad,
            jnp.where(up_ok, shifted(grad, -GRID), 0.0),
        )
        result = jnp.zeros((16, 16), jnp.float32)
        for row in range(3):
            for col in range(3):
                one = jnp.sum(moved[col] * grads[row], axis=1, keepdims=True)
                result = jnp.where(lane == 3 * row + col, one, result)
        gtaps_ref[rows, :] = result
        return carry

    lax.fori_loop(0, part // 16, one_group, 0)
    rows_ref[...] = jnp.zeros_like(rows_ref)
    key_at = lax.broadcasted_iota(jnp.int32, (SPAN, SPAN), 0)
    query_at = lax.broadcasted_iota(jnp.int32, (SPAN, SPAN), 1)
    later = low(jnp.where(key_at >= query_at, 1.0, 0.0))

    def one_span(step, back_states):
        at = spans - 1 - step
        lanes = pl.ds(pl.multiple_of(at * SPAN, SPAN), SPAN)
        after = []
        for head in range(heads):
            at_rows = [pl.ds(kind * part + head * HD, HD) for kind in range(3)]
            query, key, value = (wide[rows, lanes] for rows in at_rows)
            grad = low(grec_ref[pl.ds(head * HD, HD), lanes])
            row = cum_ref[head : head + 1, lanes]
            column = col_ref[lanes, head : head + 1]
            last = row[:, SPAN - 1 : SPAN]
            state = states_ref[at, head]
            back = back_states[head]
            decay = decay_block(row, column)
            score = mm(low(key), low(query), TN)
            weights = decay * score
            grad_weights = mm(low(value), grad, TN)
            grad_score = grad_weights * decay
            product = low(grad_weights * weights)
            grad_score = low(grad_score)
            in_decay = jnp.exp(row)
            out_decay = jnp.exp(last - row)
            query_in = mm(low(state), grad, TN) * in_decay
            key_out = mm(low(back), low(value), TN) * out_decay
            gwide[at_rows[0], lanes] = mm(low(key), grad_score, NN) + query_in
            gwide[at_rows[1], lanes] = mm(low(query), grad_score, NT) + key_out
            carried = low(key * out_decay)
            gwide[at_rows[2], lanes] = mm(grad, low(weights), NT) + mm(low(back), carried, NN)
            inside = mm(product, later, NN)
            inside = jnp.sum(jnp.where(key_at < query_at, inside, 0.0), axis=0, keepdims=True)
            span_decay = jnp.exp(last)
            across = jnp.sum(back * state, keepdims=True) * span_decay
            rows_ref[0, head : head + 1, lanes] = jnp.sum(query * query_in, axis=0, keepdims=True)
            rows_ref[1, head : head + 1, lanes] = jnp.sum(key * key_out, axis=0, keepdims=True)
            rows_ref[2, head : head + 1, lanes] = inside + across
            after.append(back * span_decay + mm(grad, low(query * in_decay), NT))
        return tuple(after)

    lax.fori_loop(0, spans, one_span, tuple(jnp.zeros((HD, HD), jnp.float32) for _ in range(heads)))
    grad_log = (
        running_sum(rows_ref[0], SPAN, reverse=True)
        + running_sum(rows_ref[1], SPAN, exclusive=True)
        + rows_ref[2]
    )
    gwide[3 * part :, :] = jnp.zeros((gwide.shape[0] - 3 * part, length), jnp.float32)
    gwide[3 * part : 3 * part + heads, :] = (grad_log / (1.0 + jnp.exp(logit)))[:heads]
    gproj_ref[...] = low(gwide[...])


def mixer_back(proj, logit, taps, rec, states, grad, heads):
    part = proj.shape[0] // 3
    length = proj.shape[1]
    return pl.pallas_call(
        functools.partial(back_kernel, heads),
        out_shape=(
            jax.ShapeDtypeStruct((WIDE_ROWS, length), jnp.bfloat16),
            jax.ShapeDtypeStruct((part, 16), jnp.float32),
        ),
        in_specs=[pl.BlockSpec(memory_space=pltpu.VMEM)] * 6,
        out_specs=[pl.BlockSpec(memory_space=pltpu.VMEM)] * 2,
        scratch_shapes=[
            pltpu.VMEM((3 * part, length), jnp.float32),
            pltpu.VMEM((WIDE_ROWS, length), jnp.float32),
            pltpu.VMEM((8, length), jnp.float32),
            pltpu.VMEM((length, 8), jnp.float32),
            pltpu.VMEM((part, length), jnp.float32),
            pltpu.VMEM((3, 8, length), jnp.float32),
        ],
        compiler_params=pltpu.CompilerParams(vmem_limit_bytes=56 * 2**20),
        cost_estimate=work_for(18),
        name="mixer_back",
    )(proj, logit, taps, rec, states, grad)


MESH = pl.DeviceIdType.MESH
CHUNK = 256
VMEM_LIMIT = 58 * 2**20
VMEM_SPEC = pl.BlockSpec(memory_space=pltpu.VMEM)
WIDE_ROWS = 896


def work_for(microseconds):
    return pl.CostEstimate(flops=int(microseconds * 1e9), bytes_accessed=0, transcendentals=0)


def places():
    me = lax.axis_index("tensor")
    across = lax.rem(me + 2, 4)
    beside = me + 1 - 2 * lax.rem(me, 2)
    corner = lax.rem(beside + 2, 4)
    return me, across, beside, corner


def greet(peers):
    barrier = pltpu.get_barrier_semaphore()
    for peer in peers:
        pl.semaphore_signal(barrier, inc=1, device_id={"tensor": peer}, device_id_type=MESH)
    pl.semaphore_wait(barrier, len(peers))


def send(source, target, sems, at, peer):
    copy = pltpu.make_async_remote_copy(
        src_ref=source,
        dst_ref=target,
        send_sem=sems.at[0, at],
        recv_sem=sems.at[1, at],
        device_id={"tensor": peer},
        device_id_type=MESH,
    )
    copy.start()
    return copy


def shard(at, part):
    return pl.ds(pl.multiple_of(at * part, 32), part)


class Spread:
    def __init__(self, where, buffer, sems, part):
        self.me, self.across, self.beside, _ = where
        self.buffer, self.sems, self.part = buffer, sems, part
        self.far, self.near, self.on = {}, {}, {}

    def view(self, owner, lanes):
        return self.buffer.at[shard(owner, self.part), lanes]

    def start(self, k, lanes, source=None):
        block = self.view(self.me, lanes)
        source = block if source is None else source
        self.far[k] = send(source, block, self.sems, 3 * k, self.across)
        self.near[k] = send(source, block, self.sems, 3 * k + 1, self.beside)

    def relay(self, k, lanes):
        self.far[k].wait_recv()
        block = self.view(self.across, lanes)
        self.on[k] = send(block, block, self.sems, 3 * k + 2, self.beside)

    def end(self, k):
        self.near[k].wait_recv()
        self.on[k].wait_recv()

    def finish(self):
        for copies in (self.far, self.near, self.on):
            for copy in copies.values():
                copy.wait_send()


class Reduce:
    def __init__(self, where, part, bufs, sems):
        self.me, self.across, self.beside, self.corner = where
        self.part = part
        self.pair_out, self.pair_in, self.far_out, self.far_in, self.keep = bufs
        self.sems = sems
        self.pair, self.far = {}, {}

    def start(self, k, lanes, term):
        for index, owner in enumerate((self.corner, self.beside)):
            self.pair_out[index, :, lanes] = low(term(owner))
            self.pair[k, index] = send(
                self.pair_out.at[index, :, lanes],
                self.pair_in.at[index, :, lanes],
                self.sems,
                3 * k + index,
                self.beside,
            )
            self.keep[index, :, lanes] = term((self.across, self.me)[index])

    def relay(self, k, lanes, remote=True):
        self.pair[k, 0].wait_recv()
        block = low(self.keep[0, :, lanes] + self.pair_in[0, :, lanes].astype(jnp.float32))
        self.far_out[:, lanes] = block
        if remote:
            self.far[k] = send(
                self.far_out.at[:, lanes], self.far_in.at[:, lanes], self.sems, 3 * k + 2, self.across
            )

    def near_sum(self, k, lanes):
        self.pair[k, 1].wait_recv()
        return self.keep[1, :, lanes] + self.pair_in[1, :, lanes].astype(jnp.float32)

    def end(self, k, lanes):
        total = self.near_sum(k, lanes)
        self.far[k].wait_recv()
        return total + self.far_in[:, lanes].astype(jnp.float32)

    def finish(self):
        for copies in (self.pair, self.far):
            for copy in copies.values():
                copy.wait_send()


class Rows:
    def __init__(self, where, buffer, sems):
        self.me, self.peers = where[0], where[1:]
        self.buffer, self.sems = buffer, sems
        self.copies = {}

    def start(self, k, lanes, first, second):
        self.buffer[self.me, 0:1, lanes] = first
        self.buffer[self.me, 1:2, lanes] = second
        block = self.buffer.at[self.me, :, lanes]
        self.copies[k] = [
            send(block, block, self.sems, 3 * k + index, peer) for index, peer in enumerate(self.peers)
        ]

    def end(self, k, lanes):
        for copy in self.copies[k]:
            copy.wait_recv()
        total = sum(self.buffer[index, :, lanes] for index in range(4))
        return total[0:1], total[1:2]

    def finish(self):
        for copies in self.copies.values():
            for copy in copies:
                copy.wait_send()


def reduce_scratch(part, length):
    return [
        pltpu.VMEM((2, part, length), jnp.bfloat16),
        pltpu.VMEM((2, part, length), jnp.bfloat16),
        pltpu.VMEM((part, length), jnp.bfloat16),
        pltpu.VMEM((part, length), jnp.bfloat16),
        pltpu.VMEM((2, part, length), jnp.float32),
    ]


def copy_sems(count):
    return pltpu.SemaphoreType.DMA((2, count))


def column_sums(rows):
    return jnp.sum(rows, axis=1, keepdims=True)


def row_sums(rows):
    return jnp.sum(rows, axis=0, keepdims=True)


def open_kernel(
    x_ref, cot_ref, silu_ref, ada_ref, bias_ref, qkv_ref, gate_ref, gate_bias_ref,
    normed_ref, proj_ref, logit_ref, stats_ref, mods_ref, gmlp_ref, wback_ref,
    raw, rows, wide, raw_sems, row_sems,
):
    part, length = x_ref.shape
    width = 4 * part
    chunks = length // CHUNK
    lanes = [pl.ds(k * CHUNK, CHUNK) for k in range(chunks)]
    where = places()
    me, _, _, _ = where
    greet(where[1:])
    spread = Spread(where, raw, raw_sems, part)
    for k in range(chunks):
        spread.start(k, lanes[k], x_ref.at[:, lanes[k]])
    raw[shard(me, part), :] = x_ref[...]

    row_at = lax.broadcasted_iota(jnp.int32, (8, part), 0)
    mods = bias_ref[:, :part]
    silu = silu_ref[...]
    for index in range(6):
        product = mm(silu, ada_ref[index * part : (index + 1) * part, :], NT)
        mods = mods + jnp.where(row_at == index, product, 0.0)
    rows[me] = bias_ref[...]
    rows[me, :, :part] = mods
    row_copies = [
        send(rows.at[me], rows.at[me], row_sems, index, peer) for index, peer in enumerate(where[1:])
    ]
    own_mods = jnp.transpose(rows[me])[:part]
    mods_ref[...] = own_mods
    gmlp_ref[...] = low(cot_ref[...].astype(jnp.float32) * own_mods[:, 5:6])
    projected = qkv_ref.shape[0]
    wide[:projected, :] = qkv_ref[...]
    wide[projected:, :] = gate_ref[...]
    wback_ref[...] = jnp.transpose(wide[...])
    for copy in row_copies:
        copy.wait_recv()
    columns = [jnp.transpose(rows[index])[:part] for index in range(4)]

    def one_chunk(k):
        spread.end(k)
        blocks = [raw[index * part : (index + 1) * part, lanes[k]].astype(jnp.float32) for index in range(4)]
        mean = sum(row_sums(block) for block in blocks) / width
        square = sum(row_sums(block * block) for block in blocks) / width
        inv_std = lax.rsqrt(square - mean * mean + norm_eps)
        stats_ref[0:1, lanes[k]] = mean
        stats_ref[1:2, lanes[k]] = inv_std
        for index in range(4):
            unit = (blocks[index] - mean) * inv_std
            normed = unit * (1.0 + columns[index][:, 1:2]) + columns[index][:, 0:1]
            normed_ref[index * part : (index + 1) * part, lanes[k]] = low(normed)
        product = mm(wide[...], normed_ref[:, lanes[k]], NN)
        proj_ref[:, lanes[k]] = low(product[:projected])
        logit_ref[:, lanes[k]] = product[projected : projected + 8] + gate_bias_ref[...]

    stats_ref[2:, :] = jnp.zeros((6, length), jnp.float32)
    for k in range(chunks):
        spread.relay(k, lanes[k])
        if k > 0:
            one_chunk(k - 1)
    one_chunk(chunks - 1)
    spread.finish()
    for copy in row_copies:
        copy.wait_send()


def open_layer(x, cot, silu, ada, bias, qkv, gate, gate_bias):
    part, length = x.shape
    width = 4 * part
    chunks = length // CHUNK
    shape = jax.ShapeDtypeStruct
    return pl.pallas_call(
        open_kernel,
        out_shape=(
            shape((width, length), jnp.bfloat16),
            shape((3 * part, length), jnp.bfloat16),
            shape((8, length), jnp.float32),
            shape((8, length), jnp.float32),
            shape((part, 8), jnp.float32),
            shape((part, length), jnp.bfloat16),
            shape((width, WIDE_ROWS), jnp.bfloat16),
        ),
        in_specs=[VMEM_SPEC] * 8,
        out_specs=[VMEM_SPEC] * 7,
        scratch_shapes=[
            pltpu.VMEM((width, length), jnp.bfloat16),
            pltpu.VMEM((4, 8, bias.shape[1]), jnp.float32),
            pltpu.VMEM((WIDE_ROWS, width), jnp.bfloat16),
            copy_sems(3 * chunks),
            copy_sems(3),
        ],
        compiler_params=pltpu.CompilerParams(
            collective_id=1, has_side_effects=True, vmem_limit_bytes=VMEM_LIMIT
        ),
        cost_estimate=work_for(25),
        name="open_layer",
    )(x, cot, silu, ada, bias, qkv, gate, gate_bias)


GELU_SLOPE = math.sqrt(2.0 / math.pi)
GELU_CUBE = 0.044715


def middle_kernel(
    mix_ref, x_ref, mods_ref, gmlp_ref, gmlp_far_ref, cot_ref, out_w_ref, up_ref, down_ref,
    attn_ref, after_ref, mlp_keep_ref, mlp_send_ref, gafter_ref, gattn_ref, gmix_ref, gup_ref, gdown_ref,
    gout_ref, sums_ref,
    out_t, turned, gmlp, gact, normed, act, gup_rows, unit,
    a_pair_out, a_pair_in, a_far_out, a_far_in, a_keep,
    g_pair_out, g_pair_in, g_far_out, g_far_in, g_keep,
    first_rows, second_rows,
    gm_sems, a_sems, n_sems, g_sems, t_sems, m_sems, first_sems, second_sems,
):
    part, length = x_ref.shape
    width = 4 * part
    hidden = up_ref.shape[1]
    chunks = length // CHUNK
    lanes = [pl.ds(k * CHUNK, CHUNK) for k in range(chunks)]
    where = places()
    me, across, beside, _ = where
    first_rows[...] = jnp.zeros_like(first_rows)
    second_rows[...] = jnp.zeros_like(second_rows)
    greet(where[1:])
    own, other = shard(me, part), shard(across, part)
    gm_copies = [
        send(gmlp_ref, gmlp.at[own, :], gm_sems, 0, beside),
        send(gmlp_far_ref, gmlp.at[other, :], gm_sems, 1, beside),
    ]
    gmlp[own, :] = gmlp_ref[...]
    gmlp[other, :] = gmlp_far_ref[...]
    gate_one, scale_two, shift_two = mods_ref[:, 2:3], mods_ref[:, 4:5], mods_ref[:, 3:4]

    attn_sum = Reduce(where, part, (a_pair_out, a_pair_in, a_far_out, a_far_in, a_keep), a_sems)
    grad_sum = Reduce(where, part, (g_pair_out, g_pair_in, g_far_out, g_far_in, g_keep), g_sems)
    norm_spread = Spread(where, normed, n_sems, part)
    grad_spread = Spread(where, gattn_ref, t_sems, part)
    moments = Rows(where, first_rows, first_sems)
    means = Rows(where, second_rows, second_sems)

    out_t[...] = jnp.transpose(out_w_ref[...])
    sums_ref[...] = jnp.zeros_like(sums_ref)

    def attn_start(k):
        mixed = mix_ref[:, lanes[k]]
        attn_sum.start(k, lanes[k], lambda owner: mm(out_t[shard(owner, part), :], mixed, NN))

    def attn_end(k):
        attn = attn_sum.end(k, lanes[k])
        attn_ref[:, lanes[k]] = attn
        after = x_ref[:, lanes[k]].astype(jnp.float32) + gate_one * attn
        after_ref[:, lanes[k]] = after
        moments.start(k, lanes[k], row_sums(after), row_sums(after * after))

    inverse = [None] * chunks

    def norm_chunk(k):
        total, squares = moments.end(k, lanes[k])
        mean = total / width
        inverse[k] = lax.rsqrt(squares / width - mean * mean + norm_eps)
        rows = (after_ref[:, lanes[k]] - mean) * inverse[k]
        unit[:, lanes[k]] = rows
        normed[own, lanes[k]] = low(rows * (1.0 + scale_two) + shift_two)
        norm_spread.start(k, lanes[k])

    def grad_act_chunk(k):
        gact[:, lanes[k]] = mm(down_ref[...], gmlp[:, lanes[k]], NN)

    def hidden_chunk(k):
        norm_spread.end(k)
        block = normed[:, lanes[k]]

        def one_block(at, carry):
            rows = pl.ds(pl.multiple_of(at * part, 32), part)
            up = mm(turned[rows, :], block, NN)
            square = up * up
            bend = jnp.tanh(GELU_SLOPE * up * (1.0 + GELU_CUBE * square))
            half = 0.5 * (1.0 + bend)
            act[rows, lanes[k]] = low(up * half)
            slope = half + 0.5 * up * (1.0 - bend * bend) * GELU_SLOPE * (1.0 + 3.0 * GELU_CUBE * square)
            gup_rows[rows, lanes[k]] = low(gact[rows, lanes[k]] * slope)
            return carry

        lax.fori_loop(0, hidden // part, one_block, 0)

    def grad_start(k):
        block = gup_rows[:, lanes[k]]
        grad_sum.start(k, lanes[k], lambda owner: mm(up_ref[shard(owner, part), :], block, NN))

    def grad_end(k):
        grad = grad_sum.end(k, lanes[k])
        rows = unit[:, lanes[k]]
        sums_ref[:, 3:4] += column_sums(grad)
        sums_ref[:, 4:5] += column_sums(grad * rows)
        scaled = grad * (1.0 + scale_two)
        gafter_ref[:, lanes[k]] = scaled
        means.start(k, lanes[k], row_sums(scaled), row_sums(scaled * rows))

    def after_chunk(k):
        total, along = means.end(k, lanes[k])
        scaled = gafter_ref[:, lanes[k]]
        back = inverse[k] * (scaled - total / width - unit[:, lanes[k]] * (along / width))
        grad = cot_ref[:, lanes[k]].astype(jnp.float32) + back
        gafter_ref[:, lanes[k]] = grad
        gattn_ref[own, lanes[k]] = low(grad * gate_one)
        grad_spread.start(k, lanes[k])
        sums_ref[:, 2:3] += column_sums(grad * attn_ref[:, lanes[k]])

    def mixed_chunk(k):
        grad_spread.end(k)
        gmix_ref[:, lanes[k]] = mm(out_w_ref[...], gattn_ref[:, lanes[k]], NN)

    def weight_grad(target, left, right, half):
        rows = target.shape[0] // 2
        target[half * rows : (half + 1) * rows, :] = low(mm(left[half * rows : (half + 1) * rows, :], right[...], NT))

    mlp_sum = Reduce(where, part, (a_pair_out, a_pair_in, mlp_send_ref, None, a_keep), m_sems)

    def mlp_start(k):
        block = act[:, lanes[k]]
        mlp_sum.start(k, lanes[k], lambda owner: mm(turned[shard(owner, part), :], block, NN))

    def mlp_end(k):
        mlp_sum.relay(k, lanes[k], remote=False)
        mlp_keep_ref[:, lanes[k]] = mlp_sum.near_sum(k, lanes[k])

    attn_start(0)
    attn_start(1)
    attn_sum.relay(0, lanes[0])
    attn_start(2)
    attn_sum.relay(1, lanes[1])
    attn_start(3)
    attn_sum.relay(2, lanes[2])
    turned[...] = jnp.transpose(up_ref[...])
    attn_sum.relay(3, lanes[3])
    attn_end(0)
    for copy in gm_copies:
        copy.wait_recv()
    grad_act_chunk(0)
    attn_end(1)
    norm_chunk(0)
    grad_act_chunk(1)
    attn_end(2)
    norm_chunk(1)
    grad_act_chunk(2)
    attn_end(3)
    norm_chunk(2)
    norm_spread.relay(0, lanes[0])
    grad_act_chunk(3)
    norm_chunk(3)
    norm_spread.relay(1, lanes[1])
    hidden_chunk(0)
    grad_start(0)
    norm_spread.relay(2, lanes[2])
    hidden_chunk(1)
    grad_sum.relay(0, lanes[0])
    grad_start(1)
    norm_spread.relay(3, lanes[3])
    hidden_chunk(2)
    grad_sum.relay(1, lanes[1])
    grad_start(2)
    grad_end(0)
    hidden_chunk(3)
    grad_sum.relay(2, lanes[2])
    after_chunk(0)
    grad_start(3)
    grad_end(1)
    grad_sum.relay(3, lanes[3])
    after_chunk(1)
    grad_end(2)
    weight_grad(gdown_ref, gmlp, act, 0)
    grad_spread.relay(0, lanes[0])
    after_chunk(2)
    grad_end(3)
    weight_grad(gdown_ref, gmlp, act, 1)
    after_chunk(3)
    grad_spread.relay(1, lanes[1])
    mixed_chunk(0)
    attn_sum.finish()
    turned[...] = jnp.transpose(down_ref[...])
    weight_grad(gup_ref, normed, gup_rows, 0)
    grad_spread.relay(2, lanes[2])
    mixed_chunk(1)
    weight_grad(gup_ref, normed, gup_rows, 1)
    grad_spread.relay(3, lanes[3])
    mixed_chunk(2)
    mlp_start(0)
    mlp_start(1)
    mlp_end(0)
    mixed_chunk(3)
    mlp_start(2)
    mlp_end(1)
    mlp_start(3)
    mlp_end(2)
    gout_ref[...] = low(mm(gattn_ref[...], mix_ref[...], NT))
    mlp_end(3)
    for copy in gm_copies:
        copy.wait_send()
    for group in (norm_spread, grad_spread, grad_sum, mlp_sum, moments, means):
        group.finish()


def middle_layer(mix, x, mods, gmlp, gmlp_far, cot, out_w, up, down):
    part, length = x.shape
    width = 4 * part
    hidden = up.shape[1]
    chunks = length // CHUNK
    shape = jax.ShapeDtypeStruct
    return pl.pallas_call(
        middle_kernel,
        out_shape=(
            shape((part, length), jnp.float32),
            shape((part, length), jnp.float32),
            shape((part, length), jnp.float32),
            shape((part, length), jnp.bfloat16),
            shape((part, length), jnp.float32),
            shape((width, length), jnp.bfloat16),
            shape((part, length), jnp.float32),
            shape((width, hidden), jnp.bfloat16),
            shape((width, hidden), jnp.bfloat16),
            shape((width, part), jnp.bfloat16),
            shape((part, 8), jnp.float32),
        ),
        in_specs=[VMEM_SPEC] * 9,
        out_specs=[VMEM_SPEC] * 11,
        scratch_shapes=[
            pltpu.VMEM((width, part), jnp.bfloat16),
            pltpu.VMEM((hidden, width), jnp.bfloat16),
            pltpu.VMEM((width, length), jnp.bfloat16),
            pltpu.VMEM((hidden, length), jnp.float32),
            pltpu.VMEM((width, length), jnp.bfloat16),
            pltpu.VMEM((hidden, length), jnp.bfloat16),
            pltpu.VMEM((hidden, length), jnp.bfloat16),
            pltpu.VMEM((part, length), jnp.float32),
            *reduce_scratch(part, length),
            *reduce_scratch(part, length),
            pltpu.VMEM((4, 8, length), jnp.float32),
            pltpu.VMEM((4, 8, length), jnp.float32),
            copy_sems(2),
            *[copy_sems(3 * chunks)] * 7,
        ],
        compiler_params=pltpu.CompilerParams(
            collective_id=2, has_side_effects=True, vmem_limit_bytes=VMEM_LIMIT
        ),
        cost_estimate=work_for(80),
        name="middle_layer",
    )(mix, x, mods, gmlp, gmlp_far, cot, out_w, up, down)


def send_dp(source, target, sems, at, peer):
    copy = pltpu.make_async_remote_copy(
        src_ref=source,
        dst_ref=target,
        send_sem=sems.at[0, at],
        recv_sem=sems.at[1, at],
        device_id={"dp": peer},
        device_id_type=MESH,
    )
    copy.start()
    return copy


def close_kernel(
    shard_count,
    gproj_ref, wback_ref, normed_ref, x_ref, stats_ref, mods_ref, gafter_ref, after_ref, cot_ref,
    mlp_keep_ref, mlp_far_ref, sums_ref, gtaps_ref, cond_ref, label_ref, ada_ref,
    gtokens_ref, out_ref, gqkv_ref, gclass_ref, gada_ref, gsmall_ref,
    pair_out, pair_in, far_out, far_in, keep, mean_rows, silu_rows, gmods, ada, parcels, latent_in, mods_out, mods_in,
    gcond, silu_own, mods_own, label_own,
    sum_sems, mean_sems, silu_sems, dp_sems, ada_sem,
):
    part, length = x_ref.shape
    width = 4 * part
    own = width // shard_count
    chunks = length // CHUNK
    lanes = [pl.ds(k * CHUNK, CHUNK) for k in range(chunks)]
    where = places()
    spot = lax.axis_index("dp")
    mean_rows[...] = jnp.zeros_like(mean_rows)
    silu_rows[...] = jnp.zeros_like(silu_rows)
    parcels[...] = jnp.zeros_like(parcels)
    mods_out[...] = jnp.zeros_like(mods_out)
    barrier = pltpu.get_barrier_semaphore()
    for peer in where[1:]:
        pl.semaphore_signal(barrier, inc=1, device_id={"tensor": peer}, device_id_type=MESH)
    for step in range(1, shard_count):
        pl.semaphore_signal(
            barrier, inc=1, device_id={"dp": lax.rem(spot + step, shard_count)}, device_id_type=MESH
        )
    pl.semaphore_wait(barrier, shard_count + 2)
    ada_copy = pltpu.make_async_copy(ada_ref, ada, ada_sem)
    ada_copy.start()
    total_sum = Reduce(where, part, (pair_out, pair_in, far_out, far_in, keep), sum_sems)
    means = Rows(where, mean_rows, mean_sems)
    scale_one, gate_two = mods_ref[:, 1:2], mods_ref[:, 5:6]
    gmods[...] = sums_ref[...]

    def start(k):
        block = gproj_ref[:, lanes[k]]
        total_sum.start(k, lanes[k], lambda owner: mm(wback_ref[shard(owner, part), :], block, NN))

    def unit_of(k):
        return (x_ref[:, lanes[k]].astype(jnp.float32) - stats_ref[0:1, lanes[k]]) * stats_ref[1:2, lanes[k]]

    def end(k):
        grad = total_sum.end(k, lanes[k])
        unit = unit_of(k)
        gmods[:, 0:1] += column_sums(grad)
        gmods[:, 1:2] += column_sums(grad * unit)
        scaled = grad * (1.0 + scale_one)
        gtokens_ref[:, lanes[k]] = scaled
        means.start(k, lanes[k], row_sums(scaled), row_sums(scaled * unit))

    def tokens(k):
        total, along = means.end(k, lanes[k])
        back = gtokens_ref[:, lanes[k]] - total / width - unit_of(k) * (along / width)
        gtokens_ref[:, lanes[k]] = gafter_ref[:, lanes[k]] + stats_ref[1:2, lanes[k]] * back

    def outputs(k):
        mlp = mlp_keep_ref[:, lanes[k]] + mlp_far_ref[:, lanes[k]].astype(jnp.float32)
        out_ref[:, lanes[k]] = low(after_ref[:, lanes[k]] + gate_two * mlp)
        gmods[:, 5:6] += column_sums(cot_ref[:, lanes[k]].astype(jnp.float32) * mlp)

    def weight_grad(quarter):
        rows = pl.ds(quarter * part, part)
        gqkv_ref[rows, :] = low(mm(normed_ref[rows, :], gproj_ref[...], NT))

    start(0)
    start(1)
    total_sum.relay(0, lanes[0])
    start(2)
    total_sum.relay(1, lanes[1])
    start(3)
    total_sum.relay(2, lanes[2])
    outputs(0)
    total_sum.relay(3, lanes[3])
    for k in range(chunks):
        if k > 0:
            outputs(k)
        weight_grad(k)
        end(k)
        if k > 0:
            tokens(k - 1)

    rows = jnp.transpose(gmods[...])
    low_rows = low(rows)
    row_at = lax.broadcasted_iota(jnp.int32, (8, width), 0)
    ada_copy.wait()
    product = jnp.zeros((8, width), jnp.float32)
    for index in range(6):
        product = product + jnp.where(row_at == index, mm(low_rows, ada[index * part : (index + 1) * part, :], NN), 0.0)
    me = where[0]
    silu_rows[me, 0:1, :] = row_sums(product)
    silu_copies = [
        send(silu_rows.at[me], silu_rows.at[me], silu_sems, index, peer) for index, peer in enumerate(where[1:])
    ]
    taps = jnp.transpose(gtaps_ref[...])
    forget = gproj_ref[3 * part : 3 * part + 8, :].astype(jnp.float32)
    forget = jnp.transpose(jnp.broadcast_to(column_sums(forget), (8, 128)))[0:1]
    small = jnp.concatenate([rows[:6], taps[:9], jnp.zeros((1, part), jnp.float32)], axis=0)
    mods_out[:, :part] = low(small)
    mods_out[:, part : part + 8] = low(jnp.broadcast_to(forget, (16, 8)))
    mods_in[spot] = mods_out[...]
    dp_copies = []
    for step in range(1, shard_count):
        peer = lax.rem(spot + step, shard_count)
        dp_copies.append(send_dp(mods_out, mods_in.at[spot], dp_sems, step, peer))
    tokens(chunks - 1)
    for copy in silu_copies:
        copy.wait_recv()
    grad_silu = sum(silu_rows[index, 0:1, :] for index in range(4))
    cond = cond_ref[0:1, :]
    sigmoid = 1.0 / (1.0 + jnp.exp(-cond))
    grad_cond = grad_silu * (sigmoid * (1.0 + cond * (1.0 - sigmoid)))
    silu = low(cond * sigmoid).astype(jnp.float32)
    for index in range(shard_count):
        columns = slice(index * own, (index + 1) * own)
        parcels[index, 0:1, :own] = grad_cond[:, columns]
        parcels[index, 1:2, :own] = silu[:, columns]
        parcels[index, 2:3, :] = jnp.broadcast_to(label_ref[...], (1, parcels.shape[2]))
    latent_in[spot] = parcels[spot]
    for step in range(1, shard_count):
        peer = lax.rem(spot + step, shard_count)
        dp_copies.append(send_dp(parcels.at[peer], latent_in.at[spot], dp_sems, shard_count + step, peer))
    for copy in dp_copies:
        copy.wait_recv()
    totals = jnp.zeros(mods_out.shape, jnp.float32)
    for index in range(shard_count):
        arrived = mods_in[index].astype(jnp.float32)
        totals = totals + arrived
        for row in range(6):
            mods_own[row, index : index + 1, :] = arrived[row : row + 1, :part]
        gcond[index : index + 1, :] = latent_in[index, 0:1, :own]
        silu_own[index : index + 1, :] = latent_in[index, 1:2, :own]
        label_own[index : index + 1, :] = latent_in[index, 2:3, :128]
    gsmall_ref[...] = totals
    class_at = lax.broadcasted_iota(jnp.int32, (shard_count, NCLASS), 1).astype(jnp.float32)
    onehot = jnp.where(label_own[:, 0:1] == class_at, 1.0, 0.0)
    gclass_ref[...] = lax.dot_general(
        gcond[...], onehot, TN, precision=TOP_PRECISION, preferred_element_type=jnp.float32
    )
    for row in range(6):
        gada_ref[row] = mm(low(silu_own[...]), low(mods_own[row]), TN)
    for copy in dp_copies + silu_copies:
        copy.wait_send()
    total_sum.finish()
    means.finish()


def close_layer(
    gproj, wback, normed, x, stats, mods, gafter, after, cot, mlp_keep, mlp_far, sums, gtaps, cond, label, ada,
    shard_count,
):
    part, length = x.shape
    width = 4 * part
    own = width // shard_count
    chunks = length // CHUNK
    padded = part + -part % 128
    own_padded = own + -own % 128
    shape = jax.ShapeDtypeStruct
    return pl.pallas_call(
        functools.partial(close_kernel, shard_count),
        out_shape=(
            shape((part, length), jnp.float32),
            shape((part, length), jnp.bfloat16),
            shape((width, WIDE_ROWS), jnp.bfloat16),
            shape((own, NCLASS), jnp.float32),
            shape((6, own, part), jnp.float32),
            shape((16, padded), jnp.float32),
        ),
        in_specs=[VMEM_SPEC] * 15 + [pl.BlockSpec(memory_space=pl.ANY)],
        out_specs=[VMEM_SPEC] * 6,
        scratch_shapes=[
            *reduce_scratch(part, length),
            pltpu.VMEM((4, 8, length), jnp.float32),
            pltpu.VMEM((4, 8, width), jnp.float32),
            pltpu.VMEM((part, 8), jnp.float32),
            pltpu.VMEM(ada.shape, jnp.bfloat16),
            pltpu.VMEM((shard_count, 8, own_padded), jnp.float32),
            pltpu.VMEM((shard_count, 8, own_padded), jnp.float32),
            pltpu.VMEM((16, padded), jnp.bfloat16),
            pltpu.VMEM((shard_count, 16, padded), jnp.bfloat16),
            pltpu.VMEM((shard_count, own), jnp.float32),
            pltpu.VMEM((shard_count, own), jnp.float32),
            pltpu.VMEM((6, shard_count, part), jnp.float32),
            pltpu.VMEM((shard_count, 128), jnp.float32),
            copy_sems(3 * chunks),
            copy_sems(3 * chunks),
            copy_sems(3),
            copy_sems(2 * shard_count),
            pltpu.SemaphoreType.DMA,
        ],
        compiler_params=pltpu.CompilerParams(
            collective_id=3, has_side_effects=True, vmem_limit_bytes=VMEM_LIMIT
        ),
        cost_estimate=work_for(30),
        name="close_layer",
    )(gproj, wback, normed, x, stats, mods, gafter, after, cot, mlp_keep, mlp_far, sums, gtaps, cond, label, ada)


def dp_total(partial, shard_count):
    rows, columns = partial.shape
    own = rows // shard_count
    spots = shard_count // 2
    at = lax.axis_index("dp")
    spot, side = at // 2, lax.rem(at, 2)
    blocks = partial.reshape(spots, 2, own, columns)
    outgoing = lax.dynamic_index_in_dim(blocks, 1 - side, axis=1, keepdims=False)
    kept = lax.dynamic_index_in_dim(blocks, side, axis=1, keepdims=False)
    arrived = lax.ppermute(outgoing, "dp", [(index, index ^ 1) for index in range(shard_count)])
    half = low(kept.astype(jnp.float32) + arrived.astype(jnp.float32))
    if spots > 4:
        groups = [[2 * index + bit for index in range(spots)] for bit in range(2)]
        total = lax.psum_scatter(
            half.reshape(spots * own, columns), "dp", scatter_dimension=0, axis_index_groups=groups, tiled=True
        )
        return total.astype(jnp.float32)
    total = lax.dynamic_index_in_dim(half, spot, axis=0, keepdims=False).astype(jnp.float32)
    for step in range(1, spots):
        block = lax.dynamic_index_in_dim(half, lax.rem(spot + step, spots), axis=0, keepdims=False)
        moved = lax.ppermute(
            block, "dp", [(index, (index + 2 * step) % shard_count) for index in range(shard_count)]
        )
        total = total + moved.astype(jnp.float32)
    return total


def shards(
    latent_tokens,
    timesteps,
    labels,
    class_table,
    ada_weight,
    ada_bias,
    query_key_value_weight,
    gate_weight,
    gate_bias,
    conv_weight,
    out_weight,
    up_weight,
    down_weight,
    cotangent,
):
    _, length, part = latent_tokens.shape
    heads = gate_weight.shape[1]
    shard_count = lax.psum(1, "dp")
    own_width = MODEL_DIM // shard_count
    x = latent_tokens[0].T
    cot = cotangent[0].T
    qkv = jnp.transpose(query_key_value_weight, (1, 2, 0)).reshape(3 * part, MODEL_DIM)
    ada = jnp.transpose(ada_weight, (1, 2, 0)).reshape(6 * part, MODEL_DIM)
    gate = jnp.pad(gate_weight.T, ((0, WIDE_ROWS - 3 * part - heads), (0, 0)))
    gate_column = jnp.pad(gate_bias.astype(jnp.float32), (0, 8 - heads))[:, None]
    bias_rows = jnp.pad(ada_bias.astype(jnp.float32), ((0, 2), (0, -part % 128)))
    taps = jnp.pad(conv_weight.astype(jnp.float32).reshape(9, part).T, ((0, 0), (0, 7)))

    cond = lax.dynamic_slice_in_dim(class_table, labels[0], 1, axis=0).astype(jnp.float32) + embed_time(
        timesteps, MODEL_DIM
    )
    silu_cond = low(jax.nn.silu(cond))
    normed_one, projected, forget_logit, stats, mods, grad_mlp, wide_back = open_layer(
        x, cot, jnp.broadcast_to(silu_cond, (8, MODEL_DIM)), ada, bias_rows, qkv, gate, gate_column
    )
    swap_chips = [(0, 2), (1, 3), (2, 0), (3, 1)]
    grad_mlp_far = lax.ppermute(grad_mlp, "tensor", swap_chips)
    mixed_low, recurrent, states = mixer(projected, forget_logit, taps, heads)
    (
        _,
        after_attn,
        mlp_keep,
        mlp_send,
        grad_after,
        _,
        grad_mixed,
        grad_up,
        grad_down,
        grad_out_w,
        sums_two,
    ) = middle_layer(mixed_low, x, mods, grad_mlp, grad_mlp_far, cot, out_weight, up_weight, down_weight)
    mlp_far = lax.ppermute(mlp_send, "tensor", swap_chips)
    grad_down = dp_total(grad_down, shard_count)
    grad_up = dp_total(grad_up, shard_count)
    grad_out_w = dp_total(grad_out_w, shard_count)
    grad_projected, grad_taps = mixer_back(projected, forget_logit, taps, recurrent, states, grad_mixed, heads)
    grad_tokens, layer_out, grad_wide, grad_class, grad_ada_w, small = close_layer(
        grad_projected, wide_back, normed_one, x, stats, mods, grad_after, after_attn, cot, mlp_keep, mlp_far,
        sums_two, grad_taps, cond, labels.astype(jnp.float32)[None], ada, shard_count,
    )
    grad_wide = dp_total(grad_wide, shard_count)
    return (
        layer_out.T[None],
        grad_tokens.T[None],
        grad_class.T,
        jnp.transpose(grad_ada_w, (1, 0, 2)),
        small[:6, :part],
        grad_wide[:, : 3 * part].reshape(own_width, 3, part),
        grad_wide[:, 3 * part : 3 * part + heads],
        small[15, part : part + heads],
        small[6:15, :part].reshape(3, 3, part),
        grad_out_w.T,
        grad_up,
        grad_down.T,
    )


def solution(mesh):
    in_specs = (
        P("dp", None, "tensor"),
        P("dp"),
        P("dp"),
        P(),
        P(None, None, "tensor"),
        P(None, "tensor"),
        P(None, None, "tensor"),
        P(None, "tensor"),
        P("tensor"),
        P(None, None, "tensor"),
        P("tensor", None),
        P(None, "tensor"),
        P("tensor", None),
        P("dp", None, "tensor"),
    )
    out_specs = (
        P("dp", None, "tensor"),
        P("dp", None, "tensor"),
        P(None, "dp"),
        P("dp", None, "tensor"),
        P(None, "tensor"),
        P("dp", None, "tensor"),
        P("dp", "tensor"),
        P("tensor"),
        P(None, None, "tensor"),
        P("tensor", "dp"),
        P("dp", "tensor"),
        P("tensor", "dp"),
    )
    return jax.shard_map(shards, mesh=mesh, in_specs=in_specs, out_specs=out_specs, check_vma=False)
```

```python
import functools
import math

import jax
import jax.numpy as jnp
from jax import lax
from jax.experimental import pallas as pl
from jax.experimental.pallas import tpu as pltpu
from jax.sharding import PartitionSpec as P

MODEL_DIM = 1152
HD = 72
HEAD_ROWS = 80
NCLASS = 1000
GRID = 32


TOP_PRECISION = lax.Precision.HIGHEST
norm_eps = 1e-06


def embed_time(time_steps, model_width):
    half_width = model_width // 2
    frequency = jnp.exp(-math.log(10000.0) * jnp.arange(half_width, dtype=jnp.float32) / half_width)
    angles = time_steps.astype(jnp.float32)[:, None] * frequency[None, :]
    return jnp.concatenate([jnp.cos(angles), jnp.sin(angles)], axis=1)


SPAN = 256

TN = (((0,), (0,)), ((), ()))
NT = (((1,), (1,)), ((), ()))
NN = (((1,), (0,)), ((), ()))


def mm(left, right, form):
    return lax.dot_general(left, right, form, preferred_element_type=jnp.float32)


def low(values):
    return values.astype(jnp.bfloat16)


def shifted(rows, offset):
    length = rows.shape[1]
    return pltpu.roll(rows, (-offset) % length, 1)


def edge_masks(length):
    token = lax.broadcasted_iota(jnp.int32, (1, length), 1)
    column = lax.rem(token, GRID)
    return column > 0, column < GRID - 1, token >= GRID, token < length - GRID


def neighbours(rows, masks):
    left_ok, right_ok, _, _ = masks
    return (
        jnp.where(left_ok, shifted(rows, -1), 0.0),
        rows,
        jnp.where(right_ok, shifted(rows, 1), 0.0),
    )


def running_sum(rows, span, reverse=False, exclusive=False):
    length = rows.shape[1]
    place = lax.rem(lax.broadcasted_iota(jnp.int32, (1, length), 1), span)
    total = rows
    step = 1
    if exclusive:
        total = (
            jnp.where(place < span - 1, shifted(total, 1), 0.0)
            if reverse
            else jnp.where(place >= 1, shifted(total, -1), 0.0)
        )
    while step < span:
        if reverse:
            total = total + jnp.where(place < span - step, shifted(total, step), 0.0)
        else:
            total = total + jnp.where(place >= step, shifted(total, -step), 0.0)
        step *= 2
    return total


def log_sigmoid(logit):
    return jnp.minimum(logit, 0.0) - jnp.log(1.0 + jnp.exp(-jnp.abs(logit)))


def conv_rows(rows, taps, masks, adjoint):
    _, _, up_ok, down_ok = masks
    left, middle, right = neighbours(rows, masks)
    parts = []
    for row in range(3):
        if adjoint:
            weights = [taps[:, 3 * (2 - row) + 2 - col : 3 * (2 - row) + 3 - col] for col in range(3)]
        else:
            weights = [taps[:, 3 * row + col : 3 * row + col + 1] for col in range(3)]
        parts.append(left * weights[0] + middle * weights[1] + right * weights[2])
    above = jnp.where(up_ok, shifted(parts[0], -GRID), 0.0)
    below = jnp.where(down_ok, shifted(parts[2], GRID), 0.0)
    return above + parts[1] + below


def decay_block(row, column):
    span = row.shape[1]
    key_at = lax.broadcasted_iota(jnp.int32, (span, span), 0)
    query_at = lax.broadcasted_iota(jnp.int32, (span, span), 1)
    return jnp.where(query_at >= key_at, jnp.exp(jnp.minimum(row - column, 0.0)), 0.0)


MESH = pl.DeviceIdType.MESH
CHUNK = 256
VMEM_LIMIT = 63 * 2**20
VMEM_SPEC = pl.BlockSpec(memory_space=pltpu.VMEM)
ANY_SPEC = pl.BlockSpec(memory_space=pl.ANY)
WIDE_ROWS = 896


def work_for(microseconds):
    return pl.CostEstimate(flops=int(microseconds * 1e9), bytes_accessed=0, transcendentals=0)


def places():
    me = lax.axis_index("tensor")
    across = lax.rem(me + 2, 4)
    beside = me + 1 - 2 * lax.rem(me, 2)
    corner = lax.rem(beside + 2, 4)
    return me, across, beside, corner


def greet(peers):
    barrier = pltpu.get_barrier_semaphore()
    for peer in peers:
        pl.semaphore_signal(barrier, inc=1, device_id={"tensor": peer}, device_id_type=MESH)
    pl.semaphore_wait(barrier, len(peers))


def send(source, target, sems, at, peer):
    copy = pltpu.make_async_remote_copy(
        src_ref=source,
        dst_ref=target,
        send_sem=sems.at[0, at],
        recv_sem=sems.at[1, at],
        device_id={"tensor": peer},
        device_id_type=MESH,
    )
    copy.start()
    return copy


def send_dp(source, target, sems, at, peer):
    copy = pltpu.make_async_remote_copy(
        src_ref=source,
        dst_ref=target,
        send_sem=sems.at[0, at],
        recv_sem=sems.at[1, at],
        device_id={"dp": peer},
        device_id_type=MESH,
    )
    copy.start()
    return copy


class Moves:
    def __init__(self, sems):
        self.sems, self.copies = sems, {}

    def start(self, name, source, target):
        copy = pltpu.make_async_copy(source, target, self.sems.at[len(self.copies)])
        copy.start()
        self.copies[name] = copy

    def wait(self, name):
        self.copies[name].wait()


def shard(at, part):
    return pl.ds(pl.multiple_of(at * part, 32), part)


class Spread:
    def __init__(self, where, buffer, sems, part):
        self.me, self.across, self.beside, _ = where
        self.buffer, self.sems, self.part = buffer, sems, part
        self.far, self.near, self.on = {}, {}, {}

    def view(self, owner, lanes):
        return self.buffer.at[shard(owner, self.part), lanes]

    def start(self, k, lanes, source=None):
        block = self.view(self.me, lanes)
        source = block if source is None else source
        self.far[k] = send(source, block, self.sems, 3 * k, self.across)
        self.near[k] = send(source, block, self.sems, 3 * k + 1, self.beside)

    def relay(self, k, lanes):
        self.far[k].wait_recv()
        block = self.view(self.across, lanes)
        self.on[k] = send(block, block, self.sems, 3 * k + 2, self.beside)

    def end(self, k):
        self.near[k].wait_recv()
        self.on[k].wait_recv()

    def finish(self):
        for copies in (self.far, self.near, self.on):
            for copy in copies.values():
                copy.wait_send()


class Reduce:
    def __init__(self, where, part, bufs, sems):
        self.me, self.across, self.beside, self.corner = where
        self.part = part
        self.pair_out, self.pair_in, self.far_out, self.far_in, self.keep = bufs
        self.sems = sems
        self.pair, self.far = {}, {}

    def start(self, k, lanes, term):
        for index, owner in enumerate((self.corner, self.beside)):
            self.pair_out[index, :, lanes] = low(term(owner))
            self.pair[k, index] = send(
                self.pair_out.at[index, :, lanes],
                self.pair_in.at[index, :, lanes],
                self.sems,
                3 * k + index,
                self.beside,
            )
            self.keep[index, :, lanes] = term((self.across, self.me)[index])

    def relay(self, k, lanes, remote=True):
        self.pair[k, 0].wait_recv()
        block = low(self.keep[0, :, lanes] + self.pair_in[0, :, lanes].astype(jnp.float32))
        self.far_out[:, lanes] = block
        if remote:
            self.far[k] = send(
                self.far_out.at[:, lanes], self.far_in.at[:, lanes], self.sems, 3 * k + 2, self.across
            )

    def near_sum(self, k, lanes):
        self.pair[k, 1].wait_recv()
        return self.keep[1, :, lanes] + self.pair_in[1, :, lanes].astype(jnp.float32)

    def end(self, k, lanes):
        total = self.near_sum(k, lanes)
        self.far[k].wait_recv()
        return total + self.far_in[:, lanes].astype(jnp.float32)

    def finish(self):
        for copies in (self.pair, self.far):
            for copy in copies.values():
                copy.wait_send()


class Rows:
    def __init__(self, where, buffer, sems):
        self.me, self.peers = where[0], where[1:]
        self.buffer, self.sems = buffer, sems
        self.copies = {}

    def start(self, k, lanes, first, second):
        self.buffer[self.me, 0:1, lanes] = first
        self.buffer[self.me, 1:2, lanes] = second
        block = self.buffer.at[self.me, :, lanes]
        self.copies[k] = [
            send(block, block, self.sems, 3 * k + index, peer) for index, peer in enumerate(self.peers)
        ]

    def end(self, k, lanes):
        for copy in self.copies[k]:
            copy.wait_recv()
        total = sum(self.buffer[index, :, lanes] for index in range(4))
        return total[0:1], total[1:2]

    def finish(self):
        for copies in self.copies.values():
            for copy in copies:
                copy.wait_send()


class Halving:
    def __init__(self, count, buffer, lanes, arrivals, sems, order):
        self.count, self.buffer, self.lanes = count, buffer, lanes
        self.arrivals, self.sems, self.order = arrivals, sems, order
        self.own = buffer.shape[0] // count
        self.me = lax.axis_index("dp")
        self.bit = {bit: lax.rem(self.me // 2**bit, 2) for bit in order}
        self.phase, self.slot, self.copies, self.sent = 0, 0, [], []

    def rows(self, block):
        return pl.ds(pl.multiple_of(block * self.own, 16), self.own)

    def blocks(self, side):
        bit = self.order[self.phase]
        found = [self.bit[bit] * (1 - 2 * side) * 2**bit + side * 2**bit]
        for done in self.order[: self.phase]:
            found = [block + self.bit[done] * 2**done for block in found]
        for free in self.order[self.phase + 1 :]:
            found = [block + value * 2**free for block in found for value in range(2)]
        return found

    def start(self):
        bit = self.order[self.phase]
        partner = self.me + 2**bit - 2 * 2**bit * self.bit[bit]
        self.copies = []
        for offset, block in enumerate(self.blocks(1)):
            at = self.slot + offset
            self.copies.append(
                send_dp(self.buffer.at[self.rows(block), self.lanes], self.arrivals.at[at], self.sems, at, partner)
            )
        self.sent += self.copies

    def step(self, result=None):
        for offset, block in enumerate(self.blocks(0)):
            self.copies[offset].wait_recv()
            total = self.buffer[self.rows(block), self.lanes].astype(jnp.float32) + self.arrivals[
                self.slot + offset
            ].astype(jnp.float32)
            if result is None:
                self.buffer[self.rows(block), self.lanes] = low(total)
            else:
                result[...] = total
        self.slot += len(self.copies)
        self.phase += 1
        if self.phase < len(self.order):
            self.start()

    def finish(self):
        for copy in self.sent:
            copy.wait_send()


def halving_scratch(count, rows, columns):
    return pltpu.VMEM((count - 1, rows // count, columns), jnp.bfloat16)


def reduce_scratch(part, length):
    return [
        pltpu.VMEM((2, part, length), jnp.bfloat16),
        pltpu.VMEM((2, part, length), jnp.bfloat16),
        pltpu.VMEM((part, length), jnp.bfloat16),
        pltpu.VMEM((part, length), jnp.bfloat16),
        pltpu.VMEM((2, part, length), jnp.float32),
    ]


def copy_sems(count):
    return pltpu.SemaphoreType.DMA((2, count))


def column_sums(rows):
    return jnp.sum(rows, axis=1, keepdims=True)


def row_sums(rows):
    return jnp.sum(rows, axis=0, keepdims=True)


def spans_forward(heads, proj, cum_ref, col_ref, rec, states_ref):
    spans = rec.shape[1] // SPAN
    scale = HD ** (-0.5)

    def one_span(at, states):
        lanes = pl.ds(pl.multiple_of(at * SPAN, SPAN), SPAN)
        after = []
        for head in range(heads):
            query, key, value = (
                proj[(kind * heads + head) * HEAD_ROWS : (kind * heads + head + 1) * HEAD_ROWS, lanes]
                for kind in range(3)
            )
            row = cum_ref[head : head + 1, lanes]
            column = col_ref[lanes, head : head + 1]
            last = row[:, SPAN - 1 : SPAN]
            state = states[head]
            states_ref[at, head] = state
            weights = decay_block(row, column) * mm(key, query, TN)
            out = mm(value, low(weights), NN)
            out = out + mm(low(state), low(query.astype(jnp.float32) * jnp.exp(row)), NN)
            rec[head * HD : (head + 1) * HD, lanes] = out[:HD] * scale
            carried = low(key.astype(jnp.float32) * jnp.exp(last - row))
            after.append(state * jnp.exp(last) + mm(value, carried, NT))
        return tuple(after)

    lax.fori_loop(
        0, spans, one_span, tuple(jnp.zeros((HEAD_ROWS, HEAD_ROWS), jnp.float32) for _ in range(heads))
    )


def conv_forward(rec, taps, mixed_ref):
    masks = edge_masks(rec.shape[1])

    def one_group(at, carry):
        rows = pl.ds(pl.multiple_of(at * 16, 16), 16)
        mixed_ref[rows, :] = low(conv_rows(rec[rows, :], taps[rows, :], masks, False))
        return carry

    lax.fori_loop(0, rec.shape[0] // 16, one_group, 0)


def conv_backward(grad_ref, rec, taps, grec, gtaps):
    masks = edge_masks(rec.shape[1])
    lane = lax.broadcasted_iota(jnp.int32, (16, 16), 1)
    scale = HD ** (-0.5)

    def one_group(at, carry):
        rows = pl.ds(pl.multiple_of(at * 16, 16), 16)
        grad = grad_ref[rows, :]
        grec[rows, :] = conv_rows(grad, taps[rows, :], masks, True) * scale
        moved = neighbours(rec[rows, :], masks)
        _, _, up_ok, down_ok = masks
        grads = (
            jnp.where(down_ok, shifted(grad, GRID), 0.0),
            grad,
            jnp.where(up_ok, shifted(grad, -GRID), 0.0),
        )
        result = jnp.zeros((16, 16), jnp.float32)
        for row in range(3):
            for col in range(3):
                one = jnp.sum(moved[col] * grads[row], axis=1, keepdims=True)
                result = jnp.where(lane == 3 * row + col, one, result)
        gtaps[rows, :] = result
        return carry

    lax.fori_loop(0, rec.shape[0] // 16, one_group, 0)


def spans_backward(heads, proj, logit_ref, cum_ref, col_ref, states, grec, staged, rows_ref, gproj):
    part, length = grec.shape
    spans = length // SPAN
    wide_rows = staged.shape[0]
    rows_ref[...] = jnp.zeros_like(rows_ref)
    staged[3 * part :, :] = jnp.zeros((wide_rows - 3 * part, SPAN), jnp.float32)
    key_at = lax.broadcasted_iota(jnp.int32, (SPAN, SPAN), 0)
    query_at = lax.broadcasted_iota(jnp.int32, (SPAN, SPAN), 1)
    later = low(jnp.where(key_at >= query_at, 1.0, 0.0))
    filler = jnp.zeros((HEAD_ROWS - HD, SPAN), jnp.float32)

    def one_span(step, back_states):
        at = spans - 1 - step
        lanes = pl.ds(pl.multiple_of(at * SPAN, SPAN), SPAN)
        after = []
        for head in range(heads):
            query, key, value = (
                proj[(kind * heads + head) * HEAD_ROWS : (kind * heads + head + 1) * HEAD_ROWS, lanes]
                for kind in range(3)
            )
            grad = low(jnp.concatenate([grec[head * HD : (head + 1) * HD, lanes], filler], axis=0))
            row = cum_ref[head : head + 1, lanes]
            column = col_ref[lanes, head : head + 1]
            last = row[:, SPAN - 1 : SPAN]
            state = states[at, head]
            back = back_states[head]
            decay = decay_block(row, column)
            weights = decay * mm(key, query, TN)
            grad_weights = mm(value, grad, TN)
            product = low(grad_weights * weights)
            grad_score = low(grad_weights * decay)
            in_decay = jnp.exp(row)
            out_decay = jnp.exp(last - row)
            query_in = mm(low(state), grad, TN) * in_decay
            key_out = mm(low(back), value, TN) * out_decay
            query_wide = query.astype(jnp.float32)
            key_wide = key.astype(jnp.float32)
            grad_query = mm(key, grad_score, NN) + query_in
            grad_key = mm(query, grad_score, NT) + key_out
            grad_value = mm(grad, low(weights), NT) + mm(low(back), low(key_wide * out_decay), NN)
            for kind, piece in enumerate((grad_query, grad_key, grad_value)):
                staged[kind * part + head * HD : kind * part + (head + 1) * HD, :] = piece[:HD]
            inside = mm(product, later, NN)
            inside = jnp.sum(jnp.where(key_at < query_at, inside, 0.0), axis=0, keepdims=True)
            span_decay = jnp.exp(last)
            across = jnp.sum(back * state, keepdims=True) * span_decay
            rows_ref[0, head : head + 1, :] = jnp.sum(query_wide * query_in, axis=0, keepdims=True)
            rows_ref[1, head : head + 1, :] = jnp.sum(key_wide * key_out, axis=0, keepdims=True)
            rows_ref[2, head : head + 1, :] = inside + across
            after.append(back * span_decay + mm(grad, low(query_wide * in_decay), NT))
        grad_log = (
            running_sum(rows_ref[0], SPAN, reverse=True)
            + running_sum(rows_ref[1], SPAN, exclusive=True)
            + rows_ref[2]
        )
        grad_forget = grad_log / (1.0 + jnp.exp(logit_ref[:, lanes]))
        staged[3 * part : 3 * part + heads, :] = grad_forget[:heads]
        gproj[:wide_rows, lanes] = low(staged[...])
        return tuple(after)

    lax.fori_loop(
        0, spans, one_span, tuple(jnp.zeros((HEAD_ROWS, HEAD_ROWS), jnp.float32) for _ in range(heads))
    )


def first_kernel(
    heads,
    x_ref, cot_ref, silu_ref, ada_ref, bias_ref, qkv_ref, gate_ref, gate_bias_ref, conv_ref,
    normed_out, proj_out, logit_ref, stats_ref, mods_ref, gmlp_ref, gmlp_far_ref, wback_out, mix_ref, rec_out,
    states_out,
    raw, normed, proj, cot, ada, wide, wback, rows, cum_ref, col_ref, rec, states, taps,
    raw_sems, row_sems, gm_sems, move_sems,
):
    part, length = x_ref.shape
    width = 4 * part
    chunks = length // CHUNK
    lanes = [pl.ds(k * CHUNK, CHUNK) for k in range(chunks)]
    where = places()
    me, across, _, _ = where
    projected = qkv_ref.shape[0]
    moves = Moves(move_sems)
    moves.start("ada", ada_ref, ada)
    moves.start("x", x_ref, raw.at[shard(me, part), :])
    moves.start("qkv", qkv_ref, wide.at[:projected, :])
    moves.start("cot", cot_ref, cot)
    greet(where[1:])
    spread = Spread(where, raw, raw_sems, part)
    for k in range(chunks // 2):
        spread.start(k, lanes[k], x_ref.at[:, lanes[k]])

    row_at = lax.broadcasted_iota(jnp.int32, (8, part), 0)
    bias = bias_ref[...].astype(jnp.float32)
    mods = jnp.concatenate([bias, jnp.zeros((8 - bias.shape[0], part), jnp.float32)], axis=0)
    silu = silu_ref[...]
    moves.wait("ada")
    for index in range(6):
        product = mm(silu, ada[index * part : (index + 1) * part, :], NT)
        mods = mods + jnp.where(row_at == index, product, 0.0)
    rows[me] = jnp.zeros(rows.shape[1:], jnp.float32)
    rows[me, :, :part] = mods
    row_copies = [
        send(rows.at[me], rows.at[me], row_sems, index, peer) for index, peer in enumerate(where[1:])
    ]
    for k in range(chunks // 2, chunks):
        spread.start(k, lanes[k], x_ref.at[:, lanes[k]])
    own_mods = jnp.transpose(rows[me])[:part]
    mods_ref[...] = own_mods
    moves.wait("cot")
    gmlp_ref[...] = low(cot[...].astype(jnp.float32) * own_mods[:, 5:6])
    gm_copy = send(gmlp_ref, gmlp_far_ref, gm_sems, 0, across)
    moves.wait("qkv")
    gate = gate_ref[...].astype(jnp.float32)
    wide[projected:, :] = low(
        jnp.concatenate([gate, jnp.zeros((WIDE_ROWS - projected - heads, width), jnp.float32)], axis=0)
    )
    wback[...] = jnp.transpose(wide[...])
    moves.start("wback", wback, wback_out)
    gate_at = lax.broadcasted_iota(jnp.int32, (8, 1), 0)
    gate_bias = jnp.zeros((8, 1), jnp.float32)
    for head in range(heads):
        gate_bias = gate_bias + jnp.where(gate_at == head, gate_bias_ref[0:1, head : head + 1].astype(jnp.float32), 0.0)
    conv = [conv_ref[index].astype(jnp.float32) for index in range(3)]
    taps[...] = jnp.transpose(jnp.concatenate(conv + [jnp.zeros((7, part), jnp.float32)], axis=0))
    moves.wait("x")
    for copy in row_copies:
        copy.wait_recv()
    columns = [jnp.transpose(rows[index])[:part] for index in range(4)]
    filler = jnp.zeros((HEAD_ROWS - HD, CHUNK), jnp.float32)

    def one_chunk(k):
        spread.end(k)
        blocks = [raw[index * part : (index + 1) * part, lanes[k]].astype(jnp.float32) for index in range(4)]
        mean = sum(row_sums(block) for block in blocks) / width
        square = sum(row_sums(block * block) for block in blocks) / width
        inv_std = lax.rsqrt(square - mean * mean + norm_eps)
        stats_ref[0:1, lanes[k]] = mean
        stats_ref[1:2, lanes[k]] = inv_std
        for index in range(4):
            unit = (blocks[index] - mean) * inv_std
            value = unit * (1.0 + columns[index][:, 1:2]) + columns[index][:, 0:1]
            normed[index * part : (index + 1) * part, lanes[k]] = low(value)
        product = mm(wide[...], normed[:, lanes[k]], NN)
        for index in range(3 * heads):
            piece = jnp.concatenate([product[index * HD : (index + 1) * HD], filler], axis=0)
            proj[index * HEAD_ROWS : (index + 1) * HEAD_ROWS, lanes[k]] = low(piece)
        logit_ref[:, lanes[k]] = product[projected : projected + 8] + gate_bias

    stats_ref[2:, :] = jnp.zeros((6, length), jnp.float32)
    for k in range(chunks):
        spread.relay(k, lanes[k])
        if k > 0:
            one_chunk(k - 1)
    one_chunk(chunks - 1)
    moves.start("normed", normed, normed_out)
    moves.start("proj", proj, proj_out)

    cum = running_sum(log_sigmoid(logit_ref[...]), SPAN)
    cum_ref[...] = cum
    col_ref[...] = jnp.transpose(cum)
    spans_forward(heads, proj, cum_ref, col_ref, rec, states)
    moves.start("rec", rec, rec_out)
    moves.start("states", states, states_out)
    conv_forward(rec, taps, mix_ref)
    gm_copy.wait_recv()
    gm_copy.wait_send()
    spread.finish()
    for copy in row_copies:
        copy.wait_send()
    for name in ("wback", "normed", "proj", "rec", "states"):
        moves.wait(name)


def first_layer(x, cot, silu, ada, bias, qkv, gate, gate_bias, conv, heads):
    part, length = x.shape
    width = 4 * part
    chunks = length // CHUNK
    spans = length // SPAN
    padded = part + -part % 128
    proj_rows = 3 * heads * HEAD_ROWS
    shape = jax.ShapeDtypeStruct
    vmem = pltpu.VMEM
    bf16, f32 = jnp.bfloat16, jnp.float32
    return pl.pallas_call(
        functools.partial(first_kernel, heads),
        out_shape=(
            shape((width, length), bf16),
            shape((proj_rows, length), bf16),
            shape((8, length), f32),
            shape((8, length), f32),
            shape((part, 8), f32),
            shape((part, length), bf16),
            shape((part, length), bf16),
            shape((width, WIDE_ROWS), bf16),
            shape((part, length), bf16),
            shape((part, length), f32),
            shape((spans, heads, HEAD_ROWS, HEAD_ROWS), f32),
        ),
        in_specs=[ANY_SPEC, ANY_SPEC, VMEM_SPEC, ANY_SPEC, VMEM_SPEC, ANY_SPEC, VMEM_SPEC, VMEM_SPEC, VMEM_SPEC],
        out_specs=[
            ANY_SPEC, ANY_SPEC, VMEM_SPEC, VMEM_SPEC, VMEM_SPEC, VMEM_SPEC, VMEM_SPEC, ANY_SPEC, VMEM_SPEC, ANY_SPEC,
            ANY_SPEC,
        ],
        scratch_shapes=[
            vmem((width, length), bf16),
            vmem((width, length), bf16),
            vmem((proj_rows, length), bf16),
            vmem((part, length), bf16),
            vmem(ada.shape, bf16),
            vmem((WIDE_ROWS, width), bf16),
            vmem((width, WIDE_ROWS), bf16),
            vmem((4, 8, padded), f32),
            vmem((8, length), f32),
            vmem((length, 8), f32),
            vmem((part, length), f32),
            vmem((spans, heads, HEAD_ROWS, HEAD_ROWS), f32),
            vmem((part, 16), f32),
            copy_sems(3 * chunks),
            copy_sems(3),
            copy_sems(1),
            pltpu.SemaphoreType.DMA((9,)),
        ],
        compiler_params=pltpu.CompilerParams(
            collective_id=1, has_side_effects=True, vmem_limit_bytes=VMEM_LIMIT
        ),
        cost_estimate=work_for(35),
        name="first_layer",
    )(x, cot, silu, ada, bias, qkv, gate, gate_bias, conv)


GELU_SLOPE = math.sqrt(2.0 / math.pi)
GELU_CUBE = 0.044715
X_FIRST, Z_FIRST = (0, 1, 2), (1, 0, 2)


def rest_kernel(
    shard_count, heads, direct,
    mix_ref, x_hbm, mods_ref, gmlp_hbm, gmlp_far_hbm, cot_hbm, out_w_ref, up_hbm, down_hbm,
    proj_hbm, logit_ref, rec_hbm, states_hbm, normed_hbm, wback_hbm, stats_ref, conv_ref, cond_ref, label_ref, ada_hbm,
    gtokens_ref, out_ref, gdown_out, gup_out, gqkv_out, gout_out, gclass_ref, gada_ref, gsmall_ref,
    x_ref, cot_ref, up, down, turned, gmlp, gact, normed, act, gup_rows, gattn,
    attn, after, gafter,
    a_pair_out, a_pair_in, a_far_out, a_far_in, a_keep,
    g_pair_out, g_pair_in, g_far_out, g_far_in, g_keep,
    first_rows, second_rows, third_rows, silu_rows,
    proj, rec, states, cum_ref, col_ref, span_rows, taps, gtaps, gmods, ada_rest,
    parcels, latent_in, mods_out, mods_in, gcond, silu_own, mods_own, label_own,
    down_in, up_in, qkv_in, out_in,
    gm_sems, a_sems, n_sems, g_sems, t_sems, m_sems, s_sems, first_sems, second_sems, third_sems, silu_sems,
    dp_sems, down_sems, up_sems, qkv_sems, out_sems, move_sems,
):
    part, length = mix_ref.shape
    width = 4 * part
    own_width = width // shard_count
    hidden = up.shape[1]
    chunks = length // CHUNK
    lanes = [pl.ds(k * CHUNK, CHUNK) for k in range(chunks)]
    where = places()
    me, across, beside, _ = where
    spot = lax.axis_index("dp")
    own, other = shard(me, part), shard(across, part)
    moves = Moves(move_sems)
    moves.start("x", x_hbm, x_ref)
    moves.start("up", up_hbm, up)
    moves.start("gm", gmlp_hbm, gmlp.at[own, :])
    moves.start("gm_far", gmlp_far_hbm, gmlp.at[other, :])
    moves.start("down", down_hbm, down)
    moves.start("cot", cot_hbm, cot_ref)
    for rows in (first_rows, second_rows, third_rows, silu_rows, parcels, mods_out):
        rows[...] = jnp.zeros(rows.shape, rows.dtype)
    barrier = pltpu.get_barrier_semaphore()
    for peer in where[1:]:
        pl.semaphore_signal(barrier, inc=1, device_id={"tensor": peer}, device_id_type=MESH)
    for step in range(1, shard_count):
        pl.semaphore_signal(
            barrier, inc=1, device_id={"dp": lax.rem(spot + step, shard_count)}, device_id_type=MESH
        )
    pl.semaphore_wait(barrier, shard_count + 2)
    gm_copies = [
        send(gmlp_hbm, gmlp.at[own, :], gm_sems, 0, beside),
        send(gmlp_far_hbm, gmlp.at[other, :], gm_sems, 1, beside),
    ]
    gate_one, scale_two, shift_two = mods_ref[:, 2:3], mods_ref[:, 4:5], mods_ref[:, 3:4]

    attn_sum = Reduce(where, part, (a_pair_out, a_pair_in, a_far_out, a_far_in, a_keep), a_sems)
    mlp_sum = Reduce(where, part, (a_pair_out, a_pair_in, a_far_out, a_far_in, a_keep), m_sems)
    grad_sum = Reduce(where, part, (g_pair_out, g_pair_in, g_far_out, g_far_in, g_keep), g_sems)
    last_sum = Reduce(where, part, (g_pair_out, g_pair_in, g_far_out, g_far_in, g_keep), s_sems)
    norm_spread = Spread(where, normed, n_sems, part)
    grad_spread = Spread(where, gattn, t_sems, part)
    moments = Rows(where, first_rows, first_sems)
    means = Rows(where, second_rows, second_sems)
    last_means = Rows(where, third_rows, third_sems)
    if direct:
        whole_lanes = pl.ds(0, hidden)
        down_total = Halving(shard_count, up, whole_lanes, down_in, down_sems, X_FIRST)
        up_total = Halving(shard_count, down, whole_lanes, up_in, up_sems, X_FIRST)
        qkv_total = Halving(shard_count, act, pl.ds(0, WIDE_ROWS), qkv_in, qkv_sems, Z_FIRST)
        out_total = Halving(shard_count, gup_rows, pl.ds(0, out_in.shape[2]), out_in, out_sems, X_FIRST)

    out_t = turned.at[:, :part]
    out_t[...] = jnp.transpose(out_w_ref[...])
    gmods[...] = jnp.zeros_like(gmods)
    gmix = gtokens_ref

    def attn_start(k):
        mixed = mix_ref[:, lanes[k]]
        attn_sum.start(k, lanes[k], lambda owner: mm(turned[shard(owner, part), :part], mixed, NN))

    def attn_end(k):
        value = attn_sum.end(k, lanes[k])
        attn[:, lanes[k]] = value
        total = x_ref[:, lanes[k]].astype(jnp.float32) + gate_one * value
        after[:, lanes[k]] = total
        moments.start(k, lanes[k], row_sums(total), row_sums(total * total))

    inverse, average = [None] * chunks, [None] * chunks

    def unit_two(k):
        return (after[:, lanes[k]] - average[k]) * inverse[k]

    def norm_chunk(k):
        total, squares = moments.end(k, lanes[k])
        average[k] = total / width
        inverse[k] = lax.rsqrt(squares / width - average[k] * average[k] + norm_eps)
        normed[own, lanes[k]] = low(unit_two(k) * (1.0 + scale_two) + shift_two)
        norm_spread.start(k, lanes[k])

    def grad_act_chunk(k):
        gact[...] = mm(down[...], gmlp[:, lanes[k]], NN)

    def hidden_chunk(k):
        norm_spread.end(k)
        block = normed[:, lanes[k]]

        def one_block(at, carry):
            rows = pl.ds(pl.multiple_of(at * part, 32), part)
            value = mm(turned[rows, :], block, NN)
            square = value * value
            bend = jnp.tanh(GELU_SLOPE * value * (1.0 + GELU_CUBE * square))
            half = 0.5 * (1.0 + bend)
            act[rows, lanes[k]] = low(value * half)
            slope = half + 0.5 * value * (1.0 - bend * bend) * GELU_SLOPE * (1.0 + 3.0 * GELU_CUBE * square)
            gup_rows[rows, lanes[k]] = low(gact[rows, :] * slope)
            return carry

        lax.fori_loop(0, hidden // part, one_block, 0)

    def grad_start(k):
        block = gup_rows[:, lanes[k]]
        grad_sum.start(k, lanes[k], lambda owner: mm(up[shard(owner, part), :], block, NN))

    def grad_end(k):
        grad = grad_sum.end(k, lanes[k])
        rows = unit_two(k)
        gmods[:, 3:4] += column_sums(grad)
        gmods[:, 4:5] += column_sums(grad * rows)
        scaled = grad * (1.0 + scale_two)
        gafter[:, lanes[k]] = scaled
        means.start(k, lanes[k], row_sums(scaled), row_sums(scaled * rows))

    def after_chunk(k):
        total, along = means.end(k, lanes[k])
        scaled = gafter[:, lanes[k]]
        back = inverse[k] * (scaled - total / width - unit_two(k) * (along / width))
        grad = cot_ref[:, lanes[k]].astype(jnp.float32) + back
        gafter[:, lanes[k]] = grad
        gattn[own, lanes[k]] = low(grad * gate_one)
        grad_spread.start(k, lanes[k])
        gmods[:, 2:3] += column_sums(grad * attn[:, lanes[k]])

    def mixed_chunk(k):
        grad_spread.end(k)
        gmix[:, lanes[k]] = mm(out_w_ref[...], gattn[:, lanes[k]], NN)

    def weight_grad(target, columns, left, right, at, pieces):
        rows = target.shape[0] // pieces
        rows = slice(at * rows, (at + 1) * rows)
        target[rows, columns] = low(mm(left[rows, :], right[...], NT))

    def mlp_start(k):
        block = act[:, lanes[k]]
        mlp_sum.start(k, lanes[k], lambda owner: mm(turned[shard(owner, part), :], block, NN))

    def outputs(k):
        mlp = mlp_sum.end(k, lanes[k])
        out_ref[:, lanes[k]] = low(after[:, lanes[k]] + mods_ref[:, 5:6] * mlp)
        gmods[:, 5:6] += column_sums(cot_ref[:, lanes[k]].astype(jnp.float32) * mlp)

    every_column = slice(None)
    attn_start(0)
    attn_start(1)
    attn_sum.relay(0, lanes[0])
    attn_start(2)
    attn_sum.relay(1, lanes[1])
    attn_start(3)
    moves.wait("up")
    turned[...] = jnp.transpose(up[...])
    moves.wait("x")
    attn_end(0)
    attn_sum.relay(2, lanes[2])
    moves.wait("gm")
    moves.wait("gm_far")
    moves.wait("down")
    for copy in gm_copies:
        copy.wait_recv()
    grad_act_chunk(0)
    attn_end(1)
    norm_chunk(0)
    attn_sum.relay(3, lanes[3])
    attn_end(2)
    norm_chunk(1)
    norm_spread.relay(0, lanes[0])
    hidden_chunk(0)
    attn_end(3)
    norm_chunk(2)
    grad_start(0)
    norm_spread.relay(1, lanes[1])
    norm_chunk(3)
    grad_sum.relay(0, lanes[0])
    grad_act_chunk(1)
    hidden_chunk(1)
    grad_start(1)
    norm_spread.relay(2, lanes[2])
    grad_sum.relay(1, lanes[1])
    grad_act_chunk(2)
    hidden_chunk(2)
    grad_start(2)
    norm_spread.relay(3, lanes[3])
    moves.wait("cot")
    grad_end(0)
    grad_sum.relay(2, lanes[2])
    grad_act_chunk(3)
    hidden_chunk(3)
    grad_start(3)
    grad_sum.relay(3, lanes[3])
    after_chunk(0)
    grad_end(1)
    turned[...] = jnp.transpose(down[...])
    weight_grad(up, every_column, gmlp, act, 0, 2)
    grad_spread.relay(0, lanes[0])
    after_chunk(1)
    grad_end(2)
    weight_grad(up, every_column, gmlp, act, 1, 2)
    if direct:
        down_total.start()
    else:
        moves.start("gdown", up, gdown_out)
    after_chunk(2)
    grad_spread.relay(1, lanes[1])
    mixed_chunk(0)
    grad_end(3)
    weight_grad(down, every_column, normed, gup_rows, 0, 2)
    after_chunk(3)
    attn_sum.finish()
    grad_spread.relay(2, lanes[2])
    mixed_chunk(1)
    weight_grad(down, every_column, normed, gup_rows, 1, 2)
    if direct:
        up_total.start()
    else:
        moves.start("gup", down, gup_out)
    moves.start("proj", proj_hbm, proj)
    moves.start("rec", rec_hbm, rec)
    moves.start("states", states_hbm, states)
    grad_spread.relay(3, lanes[3])
    mixed_chunk(2)
    mlp_start(0)
    mlp_start(1)
    mlp_sum.relay(0, lanes[0])
    mixed_chunk(3)
    mlp_start(2)
    mlp_sum.relay(1, lanes[1])
    mlp_start(3)
    mlp_sum.relay(2, lanes[2])
    norm_spread.finish()
    moves.start("normed", normed_hbm, normed)
    weight_grad(gup_rows, slice(0, part), gattn, mix_ref, 0, 1)
    mlp_sum.relay(3, lanes[3])
    moves.start("wback", wback_hbm, turned.at[:, :WIDE_ROWS])
    if not direct:
        moves.start("gout", gup_rows.at[:, : out_in.shape[2]], gout_out)

    conv = [conv_ref[index].astype(jnp.float32) for index in range(3)]
    taps[...] = jnp.transpose(jnp.concatenate(conv + [jnp.zeros((7, part), jnp.float32)], axis=0))
    cum = running_sum(log_sigmoid(logit_ref[...]), SPAN)
    cum_ref[...] = cum
    col_ref[...] = jnp.transpose(cum)
    moves.wait("rec")
    conv_backward(gmix, rec, taps, attn, gtaps)
    grad_spread.finish()
    grad_sum.finish()
    moves.wait("proj")
    moves.wait("states")
    if direct:
        down_total.step()
    staged = gact.at[:WIDE_ROWS, :]
    spans_backward(heads, proj, logit_ref, cum_ref, col_ref, states, attn, staged, span_rows, gattn)
    gproj = gattn.at[:WIDE_ROWS, :]

    def last_start(k):
        block = gproj[:, lanes[k]]
        last_sum.start(k, lanes[k], lambda owner: mm(turned[shard(owner, part), :WIDE_ROWS], block, NN))

    def unit_one(k):
        return (x_ref[:, lanes[k]].astype(jnp.float32) - stats_ref[0:1, lanes[k]]) * stats_ref[1:2, lanes[k]]

    def last_end(k):
        grad = last_sum.end(k, lanes[k])
        unit = unit_one(k)
        gmods[:, 0:1] += column_sums(grad)
        gmods[:, 1:2] += column_sums(grad * unit)
        scaled = grad * (1.0 + mods_ref[:, 1:2])
        gtokens_ref[:, lanes[k]] = scaled
        last_means.start(k, lanes[k], row_sums(scaled), row_sums(scaled * unit))

    def tokens(k):
        total, along = last_means.end(k, lanes[k])
        back = gtokens_ref[:, lanes[k]] - total / width - unit_one(k) * (along / width)
        gtokens_ref[:, lanes[k]] = gafter[:, lanes[k]] + stats_ref[1:2, lanes[k]] * back

    moves.wait("wback")
    last_start(0)
    last_start(1)
    last_sum.relay(0, lanes[0])
    last_start(2)
    last_sum.relay(1, lanes[1])
    last_start(3)
    last_sum.relay(2, lanes[2])
    moves.wait("normed")
    for piece in range(2):
        weight_grad(act, slice(0, WIDE_ROWS), normed, gproj, piece, 2)
    last_sum.relay(3, lanes[3])
    moves.start("ada", ada_hbm.at[:width, :], turned)
    moves.start("ada_rest", ada_hbm.at[width:, :], ada_rest)
    if direct:
        qkv_total.start()
        out_total.start()
        down_total.step()
    else:
        moves.start("gqkv", act.at[:, :WIDE_ROWS], gqkv_out)
    for k in range(chunks):
        outputs(k)
    for k in range(chunks):
        last_end(k)
        if k > 0:
            tokens(k - 1)

    mod_rows = jnp.transpose(gmods[...])
    low_rows = low(mod_rows)
    row_at = lax.broadcasted_iota(jnp.int32, (8, width), 0)
    moves.wait("ada")
    moves.wait("ada_rest")
    product = jnp.zeros((8, width), jnp.float32)
    for index in range(6):
        if index < 4:
            piece = turned[index * part : (index + 1) * part, :]
        else:
            piece = ada_rest[(index - 4) * part : (index - 3) * part, :]
        product = product + jnp.where(row_at == index, mm(low_rows, piece, NN), 0.0)
    silu_rows[me, 0:1, :] = row_sums(product)
    silu_copies = [
        send(silu_rows.at[me], silu_rows.at[me], silu_sems, index, peer) for index, peer in enumerate(where[1:])
    ]
    tap_rows = jnp.transpose(gtaps[...])
    forget = gattn[3 * part : WIDE_ROWS, :].astype(jnp.float32)[:8]
    forget = jnp.transpose(jnp.broadcast_to(column_sums(forget), (8, 128)))[0:1]
    small = jnp.concatenate([mod_rows[:6], tap_rows[:9], jnp.zeros((1, part), jnp.float32)], axis=0)
    mods_out[:, :part] = low(small)
    mods_out[:, part : part + 8] = low(jnp.broadcast_to(forget, (16, 8)))
    mods_in[spot] = mods_out[...]
    dp_copies = []
    for step in range(1, shard_count):
        peer = lax.rem(spot + step, shard_count)
        dp_copies.append(send_dp(mods_out, mods_in.at[spot], dp_sems, step, peer))
    tokens(chunks - 1)
    for copy in silu_copies:
        copy.wait_recv()
    grad_silu = sum(silu_rows[index, 0:1, :] for index in range(4))
    cond = cond_ref[0:1, :]
    sigmoid = 1.0 / (1.0 + jnp.exp(-cond))
    grad_cond = grad_silu * (sigmoid * (1.0 + cond * (1.0 - sigmoid)))
    silu = low(cond * sigmoid).astype(jnp.float32)
    for index in range(shard_count):
        columns = slice(index * own_width, (index + 1) * own_width)
        parcels[index, 0:1, :own_width] = grad_cond[:, columns]
        parcels[index, 1:2, :own_width] = silu[:, columns]
        parcels[index, 2:3, :] = jnp.broadcast_to(label_ref[...], (1, parcels.shape[2]))
    latent_in[spot] = parcels[spot]
    for step in range(1, shard_count):
        peer = lax.rem(spot + step, shard_count)
        dp_copies.append(send_dp(parcels.at[peer], latent_in.at[spot], dp_sems, shard_count + step, peer))
    if direct:
        up_total.step()
        down_total.step(gdown_out)
        qkv_total.step()
        out_total.step()
    for copy in dp_copies:
        copy.wait_recv()
    totals = jnp.zeros(mods_out.shape, jnp.float32)
    for index in range(shard_count):
        arrived = mods_in[index].astype(jnp.float32)
        totals = totals + arrived
        for row in range(6):
            mods_own[row, index : index + 1, :] = arrived[row : row + 1, :part]
        gcond[index : index + 1, :] = latent_in[index, 0:1, :own_width]
        silu_own[index : index + 1, :] = latent_in[index, 1:2, :own_width]
        label_own[index : index + 1, :] = latent_in[index, 2:3, :128]
    gsmall_ref[...] = totals
    class_at = lax.broadcasted_iota(jnp.int32, (shard_count, NCLASS), 1).astype(jnp.float32)
    onehot = jnp.where(label_own[:, 0:1] == class_at, 1.0, 0.0)
    gclass_ref[...] = lax.dot_general(
        gcond[...], onehot, TN, precision=TOP_PRECISION, preferred_element_type=jnp.float32
    )
    for row in range(6):
        gada_ref[row] = mm(low(silu_own[...]), low(mods_own[row]), TN)
    if direct:
        up_total.step()
        qkv_total.step()
        out_total.step()
        up_total.step(gup_out)
        out_total.step(gout_out)
        qkv_total.step(gqkv_out)
        for total in (down_total, up_total, qkv_total, out_total):
            total.finish()
    else:
        for name in ("gdown", "gup", "gqkv", "gout"):
            moves.wait(name)
    for copy in gm_copies + dp_copies + silu_copies:
        copy.wait_send()
    for group in (mlp_sum, last_sum, moments, means, last_means):
        group.finish()


def rest_layer(
    mix, x, mods, gmlp, gmlp_far, cot, out_w, up, down, proj, logit, rec, states, normed, wback, stats, conv, cond,
    label, ada, shard_count, heads, direct,
):
    part, length = x.shape
    width = 4 * part
    hidden = up.shape[1]
    own = width // shard_count
    chunks = length // CHUNK
    padded = part + -part % 128
    own_padded = own + -own % 128
    shape = jax.ShapeDtypeStruct
    vmem = pltpu.VMEM
    bf16, f32 = jnp.bfloat16, jnp.float32
    grad_rows, grad_type, grad_spec = (own, f32, VMEM_SPEC) if direct else (width, bf16, ANY_SPEC)
    arrivals = shard_count if direct else 2
    arrival_rows = width if direct else 32
    return pl.pallas_call(
        functools.partial(rest_kernel, shard_count, heads, direct),
        out_shape=(
            shape((part, length), f32),
            shape((part, length), bf16),
            shape((grad_rows, hidden), grad_type),
            shape((grad_rows, hidden), grad_type),
            shape((grad_rows, WIDE_ROWS), grad_type),
            shape((grad_rows, padded), grad_type),
            shape((own, NCLASS), f32),
            shape((6, own, part), f32),
            shape((16, padded), f32),
        ),
        in_specs=[
            VMEM_SPEC, ANY_SPEC, VMEM_SPEC, ANY_SPEC, ANY_SPEC, ANY_SPEC, VMEM_SPEC, ANY_SPEC, ANY_SPEC, ANY_SPEC,
            VMEM_SPEC, ANY_SPEC, ANY_SPEC, ANY_SPEC, ANY_SPEC, VMEM_SPEC, VMEM_SPEC, VMEM_SPEC, VMEM_SPEC, ANY_SPEC,
        ],
        out_specs=[VMEM_SPEC, VMEM_SPEC] + [grad_spec] * 4 + [VMEM_SPEC] * 3,
        scratch_shapes=[
            vmem((part, length), bf16),
            vmem((part, length), bf16),
            vmem((width, hidden), bf16),
            vmem((hidden, width), bf16),
            vmem((hidden, width), bf16),
            vmem((width, length), bf16),
            vmem((hidden, CHUNK), f32),
            vmem((width, length), bf16),
            vmem((hidden, length), bf16),
            vmem((hidden, length), bf16),
            vmem((width, length), bf16),
            *[vmem((part, length), f32)] * 3,
            *reduce_scratch(part, length),
            *reduce_scratch(part, length),
            *[vmem((4, 8, length), f32)] * 3,
            vmem((4, 8, width), f32),
            vmem(proj.shape, bf16),
            vmem((part, length), f32),
            vmem(states.shape, f32),
            vmem((8, length), f32),
            vmem((length, 8), f32),
            vmem((3, 8, SPAN), f32),
            vmem((part, 16), f32),
            vmem((part, 16), f32),
            vmem((part, 8), f32),
            vmem((ada.shape[0] - width, width), bf16),
            vmem((shard_count, 8, own_padded), f32),
            vmem((shard_count, 8, own_padded), f32),
            vmem((16, padded), bf16),
            vmem((shard_count, 16, padded), bf16),
            vmem((shard_count, own), f32),
            vmem((shard_count, own), f32),
            vmem((6, shard_count, part), f32),
            vmem((shard_count, 128), f32),
            halving_scratch(arrivals, arrival_rows, hidden),
            halving_scratch(arrivals, arrival_rows, hidden),
            halving_scratch(arrivals, arrival_rows, WIDE_ROWS),
            halving_scratch(arrivals, arrival_rows, padded),
            copy_sems(2),
            *[copy_sems(3 * chunks)] * 6,
            *[copy_sems(3 * chunks)] * 3,
            copy_sems(3),
            copy_sems(2 * shard_count),
            *[copy_sems(shard_count)] * 4,
            pltpu.SemaphoreType.DMA((20,)),
        ],
        compiler_params=pltpu.CompilerParams(
            collective_id=2, has_side_effects=True, vmem_limit_bytes=VMEM_LIMIT
        ),
        cost_estimate=work_for(150),
        name="rest_layer",
    )(
        mix, x, mods, gmlp, gmlp_far, cot, out_w, up, down, proj, logit, rec, states, normed, wback, stats, conv,
        cond, label, ada,
    )


def shards(
    latent_tokens,
    timesteps,
    labels,
    class_table,
    ada_weight,
    ada_bias,
    query_key_value_weight,
    gate_weight,
    gate_bias,
    conv_weight,
    out_weight,
    up_weight,
    down_weight,
    cotangent,
):
    part = latent_tokens.shape[2]
    heads = gate_weight.shape[1]
    shard_count = lax.psum(1, "dp")
    own_width = MODEL_DIM // shard_count
    x = latent_tokens[0].T
    cot = cotangent[0].T
    qkv = jnp.transpose(query_key_value_weight, (1, 2, 0)).reshape(3 * part, MODEL_DIM)
    ada = jnp.transpose(ada_weight, (1, 2, 0)).reshape(6 * part, MODEL_DIM)
    cond = lax.dynamic_slice_in_dim(class_table, labels[0], 1, axis=0).astype(jnp.float32) + embed_time(
        timesteps, MODEL_DIM
    )
    silu = jnp.broadcast_to(low(jax.nn.silu(cond)), (8, MODEL_DIM))
    normed, proj, logit, stats, mods, grad_mlp, grad_mlp_far, wide_back, mixed, recurrent, states = first_layer(
        x, cot, silu, ada, ada_bias, qkv, gate_weight.T, gate_bias[None], conv_weight, heads
    )
    direct = shard_count == 8 and own_width % 16 == 0
    grad_tokens, layer_out, grad_down, grad_up, grad_wide, grad_out_w, grad_class, grad_ada_w, small = rest_layer(
        mixed, x, mods, grad_mlp, grad_mlp_far, cot, out_weight, up_weight, down_weight, proj, logit, recurrent,
        states, normed, wide_back, stats, conv_weight, cond, labels.astype(jnp.float32)[None], ada, shard_count, heads,
        direct,
    )
    if not direct:
        grad_down, grad_up, grad_wide, grad_out_w = (
            lax.psum_scatter(partial, "dp", scatter_dimension=0, tiled=True).astype(jnp.float32)
            for partial in (grad_down, grad_up, grad_wide, grad_out_w)
        )
    return (
        layer_out.T[None],
        grad_tokens.T[None],
        grad_class.T,
        jnp.transpose(grad_ada_w, (1, 0, 2)),
        small[:6, :part],
        grad_wide[:, : 3 * part].reshape(own_width, 3, part),
        grad_wide[:, 3 * part : 3 * part + heads],
        small[15, part : part + heads],
        small[6:15, :part].reshape(3, 3, part),
        grad_out_w[:, :part].T,
        grad_up,
        grad_down.T,
    )


def solution(mesh):
    in_specs = (
        P("dp", None, "tensor"),
        P("dp"),
        P("dp"),
        P(),
        P(None, None, "tensor"),
        P(None, "tensor"),
        P(None, None, "tensor"),
        P(None, "tensor"),
        P("tensor"),
        P(None, None, "tensor"),
        P("tensor", None),
        P(None, "tensor"),
        P("tensor", None),
        P("dp", None, "tensor"),
    )
    out_specs = (
        P("dp", None, "tensor"),
        P("dp", None, "tensor"),
        P(None, "dp"),
        P("dp", None, "tensor"),
        P(None, "tensor"),
        P("dp", None, "tensor"),
        P("dp", "tensor"),
        P("tensor"),
        P(None, None, "tensor"),
        P("tensor", "dp"),
        P("dp", "tensor"),
        P("tensor", "dp"),
    )
    return jax.shard_map(shards, mesh=mesh, in_specs=in_specs, out_specs=out_specs, check_vma=False)
```

```python
import functools
import math

import jax
import jax.numpy as jnp
from jax import lax
from jax.experimental import pallas as pl
from jax.experimental.pallas import tpu as pltpu
from jax.sharding import PartitionSpec as P

MODEL_DIM = 1152
HD = 72
HEAD_ROWS = 80
NCLASS = 1000
GRID = 32


TOP_PRECISION = lax.Precision.HIGHEST
norm_eps = 1e-06


def embed_time(time_steps, model_width):
    half_width = model_width // 2
    frequency = jnp.exp(-math.log(10000.0) * jnp.arange(half_width, dtype=jnp.float32) / half_width)
    angles = time_steps.astype(jnp.float32)[:, None] * frequency[None, :]
    return jnp.concatenate([jnp.cos(angles), jnp.sin(angles)], axis=1)


SPAN = 256

TN = (((0,), (0,)), ((), ()))
NT = (((1,), (1,)), ((), ()))
NN = (((1,), (0,)), ((), ()))


def mm(left, right, form):
    return lax.dot_general(left, right, form, preferred_element_type=jnp.float32)


def low(values):
    return values.astype(jnp.bfloat16)


def shifted(rows, offset):
    length = rows.shape[1]
    return pltpu.roll(rows, (-offset) % length, 1)


def edge_masks(length):
    token = lax.broadcasted_iota(jnp.int32, (1, length), 1)
    column = lax.rem(token, GRID)
    return column > 0, column < GRID - 1, token >= GRID, token < length - GRID


def neighbours(rows, masks):
    left_ok, right_ok, _, _ = masks
    return (
        jnp.where(left_ok, shifted(rows, -1), 0.0),
        rows,
        jnp.where(right_ok, shifted(rows, 1), 0.0),
    )


def running_sum(rows, span, reverse=False, exclusive=False):
    length = rows.shape[1]
    place = lax.rem(lax.broadcasted_iota(jnp.int32, (1, length), 1), span)
    total = rows
    step = 1
    if exclusive:
        total = (
            jnp.where(place < span - 1, shifted(total, 1), 0.0)
            if reverse
            else jnp.where(place >= 1, shifted(total, -1), 0.0)
        )
    while step < span:
        if reverse:
            total = total + jnp.where(place < span - step, shifted(total, step), 0.0)
        else:
            total = total + jnp.where(place >= step, shifted(total, -step), 0.0)
        step *= 2
    return total


def log_sigmoid(logit):
    return jnp.minimum(logit, 0.0) - jnp.log(1.0 + jnp.exp(-jnp.abs(logit)))


def conv_rows(rows, taps, masks, adjoint):
    _, _, up_ok, down_ok = masks
    left, middle, right = neighbours(rows, masks)
    parts = []
    for row in range(3):
        if adjoint:
            weights = [taps[:, 3 * (2 - row) + 2 - col : 3 * (2 - row) + 3 - col] for col in range(3)]
        else:
            weights = [taps[:, 3 * row + col : 3 * row + col + 1] for col in range(3)]
        parts.append(left * weights[0] + middle * weights[1] + right * weights[2])
    above = jnp.where(up_ok, shifted(parts[0], -GRID), 0.0)
    below = jnp.where(down_ok, shifted(parts[2], GRID), 0.0)
    return above + parts[1] + below


def decay_block(row, column):
    span = row.shape[1]
    key_at = lax.broadcasted_iota(jnp.int32, (span, span), 0)
    query_at = lax.broadcasted_iota(jnp.int32, (span, span), 1)
    return jnp.where(query_at >= key_at, jnp.exp(jnp.minimum(row - column, 0.0)), 0.0)


MESH = pl.DeviceIdType.MESH
CHUNK = 256
VMEM_LIMIT = 63 * 2**20
VMEM_SPEC = pl.BlockSpec(memory_space=pltpu.VMEM)
ANY_SPEC = pl.BlockSpec(memory_space=pl.ANY)
WIDE_ROWS = 896


def work_for(microseconds):
    return pl.CostEstimate(flops=int(microseconds * 1e9), bytes_accessed=0, transcendentals=0)


def places():
    me = lax.axis_index("tensor")
    across = lax.rem(me + 2, 4)
    beside = me + 1 - 2 * lax.rem(me, 2)
    corner = lax.rem(beside + 2, 4)
    return me, across, beside, corner


def greet(peers):
    barrier = pltpu.get_barrier_semaphore()
    for peer in peers:
        pl.semaphore_signal(barrier, inc=1, device_id={"tensor": peer}, device_id_type=MESH)
    pl.semaphore_wait(barrier, len(peers))


def send(source, target, sems, at, peer):
    copy = pltpu.make_async_remote_copy(
        src_ref=source,
        dst_ref=target,
        send_sem=sems.at[0, at],
        recv_sem=sems.at[1, at],
        device_id={"tensor": peer},
        device_id_type=MESH,
    )
    copy.start()
    return copy


def send_dp(source, target, sems, at, peer):
    copy = pltpu.make_async_remote_copy(
        src_ref=source,
        dst_ref=target,
        send_sem=sems.at[0, at],
        recv_sem=sems.at[1, at],
        device_id={"dp": peer},
        device_id_type=MESH,
    )
    copy.start()
    return copy


class Moves:
    def __init__(self, sems):
        self.sems, self.copies = sems, {}

    def start(self, name, source, target):
        copy = pltpu.make_async_copy(source, target, self.sems.at[len(self.copies)])
        copy.start()
        self.copies[name] = copy

    def wait(self, name):
        self.copies[name].wait()


def shard(at, part):
    return pl.ds(pl.multiple_of(at * part, 32), part)


class Spread:
    def __init__(self, where, buffer, sems, part):
        self.me, self.across, self.beside, _ = where
        self.buffer, self.sems, self.part = buffer, sems, part
        self.far, self.near, self.on = {}, {}, {}

    def view(self, owner, lanes):
        return self.buffer.at[shard(owner, self.part), lanes]

    def start(self, k, lanes, source=None):
        block = self.view(self.me, lanes)
        source = block if source is None else source
        self.far[k] = send(source, block, self.sems, 3 * k, self.across)
        self.near[k] = send(source, block, self.sems, 3 * k + 1, self.beside)

    def relay(self, k, lanes):
        self.far[k].wait_recv()
        block = self.view(self.across, lanes)
        self.on[k] = send(block, block, self.sems, 3 * k + 2, self.beside)

    def end(self, k):
        self.near[k].wait_recv()
        self.on[k].wait_recv()

    def finish(self):
        for copies in (self.far, self.near, self.on):
            for copy in copies.values():
                copy.wait_send()


class Reduce:
    def __init__(self, where, part, bufs, sems):
        self.me, self.across, self.beside, self.corner = where
        self.part = part
        self.pair_out, self.pair_in, self.far_out, self.far_in, self.keep = bufs
        self.sems = sems
        self.pair, self.far = {}, {}

    def start(self, k, lanes, term):
        for index, owner in enumerate((self.corner, self.beside)):
            self.pair_out[index, :, lanes] = low(term(owner))
            self.pair[k, index] = send(
                self.pair_out.at[index, :, lanes],
                self.pair_in.at[index, :, lanes],
                self.sems,
                3 * k + index,
                self.beside,
            )
            self.keep[index, :, lanes] = term((self.across, self.me)[index])

    def relay(self, k, lanes, remote=True):
        self.pair[k, 0].wait_recv()
        block = low(self.keep[0, :, lanes] + self.pair_in[0, :, lanes].astype(jnp.float32))
        self.far_out[:, lanes] = block
        if remote:
            self.far[k] = send(
                self.far_out.at[:, lanes], self.far_in.at[:, lanes], self.sems, 3 * k + 2, self.across
            )

    def near_sum(self, k, lanes):
        self.pair[k, 1].wait_recv()
        return self.keep[1, :, lanes] + self.pair_in[1, :, lanes].astype(jnp.float32)

    def end(self, k, lanes):
        total = self.near_sum(k, lanes)
        self.far[k].wait_recv()
        return total + self.far_in[:, lanes].astype(jnp.float32)

    def finish(self):
        for copies in (self.pair, self.far):
            for copy in copies.values():
                copy.wait_send()


class Rows:
    def __init__(self, where, buffer, sems):
        self.me, self.peers = where[0], where[1:]
        self.buffer, self.sems = buffer, sems
        self.copies = {}

    def start(self, k, lanes, first, second):
        self.buffer[self.me, 0:1, lanes] = first
        self.buffer[self.me, 1:2, lanes] = second
        block = self.buffer.at[self.me, :, lanes]
        self.copies[k] = [
            send(block, block, self.sems, 3 * k + index, peer) for index, peer in enumerate(self.peers)
        ]

    def end(self, k, lanes):
        for copy in self.copies[k]:
            copy.wait_recv()
        total = sum(self.buffer[index, :, lanes] for index in range(4))
        return total[0:1], total[1:2]

    def finish(self):
        for copies in self.copies.values():
            for copy in copies:
                copy.wait_send()


class Halving:
    def __init__(self, count, buffer, lanes, arrivals, sems, order, result):
        self.result = result
        self.count, self.buffer, self.lanes = count, buffer, lanes
        self.arrivals, self.sems, self.order = arrivals, sems, order
        self.own = buffer.shape[0] // count
        self.me = lax.axis_index("dp")
        self.bit = {bit: lax.rem(self.me // 2**bit, 2) for bit in order}
        self.phase, self.slot, self.copies, self.sent = 0, 0, [], []

    def rows(self, block):
        return pl.ds(pl.multiple_of(block * self.own, 16), self.own)

    def blocks(self, side):
        bit = self.order[self.phase]
        found = [self.bit[bit] * (1 - 2 * side) * 2**bit + side * 2**bit]
        for done in self.order[: self.phase]:
            found = [block + self.bit[done] * 2**done for block in found]
        for free in self.order[self.phase + 1 :]:
            found = [block + value * 2**free for block in found for value in range(2)]
        return found

    def start(self):
        bit = self.order[self.phase]
        partner = self.me + 2**bit - 2 * 2**bit * self.bit[bit]
        self.copies = []
        for offset, block in enumerate(self.blocks(1)):
            at = self.slot + offset
            self.copies.append(
                send_dp(self.buffer.at[self.rows(block), self.lanes], self.arrivals.at[at], self.sems, at, partner)
            )
        self.sent += self.copies

    def step(self):
        for offset, block in enumerate(self.blocks(0)):
            self.copies[offset].wait_recv()
            total = self.buffer[self.rows(block), self.lanes].astype(jnp.float32) + self.arrivals[
                self.slot + offset
            ].astype(jnp.float32)
            if self.phase + 1 < len(self.order):
                self.buffer[self.rows(block), self.lanes] = low(total)
            else:
                self.result[:, self.lanes] = total
        self.slot += len(self.copies)
        self.phase += 1
        if self.phase < len(self.order):
            self.start()

    def finish(self):
        for copy in self.sent:
            copy.wait_send()


def halving_scratch(count, rows, columns):
    return pltpu.VMEM((count - 1, rows // count, columns), jnp.bfloat16)


def reduce_scratch(part, length):
    return [
        pltpu.VMEM((2, part, length), jnp.bfloat16),
        pltpu.VMEM((2, part, length), jnp.bfloat16),
        pltpu.VMEM((part, length), jnp.bfloat16),
        pltpu.VMEM((part, length), jnp.bfloat16),
        pltpu.VMEM((2, part, length), jnp.float32),
    ]


def copy_sems(count):
    return pltpu.SemaphoreType.DMA((2, count))


def column_sums(rows):
    return jnp.sum(rows, axis=1, keepdims=True)


def row_sums(rows):
    return jnp.sum(rows, axis=0, keepdims=True)


def span_forward(heads, at, lanes, states, proj, cum_ref, col_ref, rec, states_ref):
    scale = HD ** (-0.5)
    after = []
    for head in range(heads):
        query, key, value = (
            proj[(kind * heads + head) * HEAD_ROWS : (kind * heads + head + 1) * HEAD_ROWS, lanes]
            for kind in range(3)
        )
        row = cum_ref[head : head + 1, lanes]
        column = col_ref[lanes, head : head + 1]
        last = row[:, SPAN - 1 : SPAN]
        state = states[head]
        states_ref[at, head] = state
        weights = decay_block(row, column) * mm(key, query, TN)
        out = mm(value, low(weights), NN)
        out = out + mm(low(state), low(query.astype(jnp.float32) * jnp.exp(row)), NN)
        rec[head * HD : (head + 1) * HD, lanes] = out[:HD] * scale
        carried = low(key.astype(jnp.float32) * jnp.exp(last - row))
        after.append(state * jnp.exp(last) + mm(value, carried, NT))
    return after


def conv_forward(rec, taps, mixed_ref):
    masks = edge_masks(rec.shape[1])

    def one_group(at, carry):
        rows = pl.ds(pl.multiple_of(at * 16, 16), 16)
        mixed_ref[rows, :] = low(conv_rows(rec[rows, :], taps[rows, :], masks, False))
        return carry

    lax.fori_loop(0, rec.shape[0] // 16, one_group, 0)


def conv_backward(grad_ref, rec, taps, grec, gtaps):
    masks = edge_masks(rec.shape[1])
    lane = lax.broadcasted_iota(jnp.int32, (16, 16), 1)
    scale = HD ** (-0.5)

    def one_group(at, carry):
        rows = pl.ds(pl.multiple_of(at * 16, 16), 16)
        grad = grad_ref[rows, :]
        grec[rows, :] = conv_rows(grad, taps[rows, :], masks, True) * scale
        moved = neighbours(rec[rows, :], masks)
        _, _, up_ok, down_ok = masks
        grads = (
            jnp.where(down_ok, shifted(grad, GRID), 0.0),
            grad,
            jnp.where(up_ok, shifted(grad, -GRID), 0.0),
        )
        result = jnp.zeros((16, 16), jnp.float32)
        for row in range(3):
            for col in range(3):
                one = jnp.sum(moved[col] * grads[row], axis=1, keepdims=True)
                result = jnp.where(lane == 3 * row + col, one, result)
        gtaps[rows, :] = result
        return carry

    lax.fori_loop(0, rec.shape[0] // 16, one_group, 0)


def spans_backward(heads, proj, logit_ref, cum_ref, col_ref, states, grec, staged, rows_ref, gproj):
    part, length = grec.shape
    spans = length // SPAN
    wide_rows = staged.shape[0]
    rows_ref[...] = jnp.zeros_like(rows_ref)
    staged[3 * part :, :] = jnp.zeros((wide_rows - 3 * part, SPAN), jnp.float32)
    key_at = lax.broadcasted_iota(jnp.int32, (SPAN, SPAN), 0)
    query_at = lax.broadcasted_iota(jnp.int32, (SPAN, SPAN), 1)
    later = low(jnp.where(key_at >= query_at, 1.0, 0.0))
    filler = jnp.zeros((HEAD_ROWS - HD, SPAN), jnp.float32)

    def one_span(step, back_states):
        at = spans - 1 - step
        lanes = pl.ds(pl.multiple_of(at * SPAN, SPAN), SPAN)
        after = []
        for head in range(heads):
            query, key, value = (
                proj[(kind * heads + head) * HEAD_ROWS : (kind * heads + head + 1) * HEAD_ROWS, lanes]
                for kind in range(3)
            )
            grad = low(jnp.concatenate([grec[head * HD : (head + 1) * HD, lanes], filler], axis=0))
            row = cum_ref[head : head + 1, lanes]
            column = col_ref[lanes, head : head + 1]
            last = row[:, SPAN - 1 : SPAN]
            state = states[at, head]
            back = back_states[head]
            decay = decay_block(row, column)
            weights = decay * mm(key, query, TN)
            grad_weights = mm(value, grad, TN)
            product = low(grad_weights * weights)
            grad_score = low(grad_weights * decay)
            in_decay = jnp.exp(row)
            out_decay = jnp.exp(last - row)
            query_in = mm(low(state), grad, TN) * in_decay
            key_out = mm(low(back), value, TN) * out_decay
            query_wide = query.astype(jnp.float32)
            key_wide = key.astype(jnp.float32)
            grad_query = mm(key, grad_score, NN) + query_in
            grad_key = mm(query, grad_score, NT) + key_out
            grad_value = mm(grad, low(weights), NT) + mm(low(back), low(key_wide * out_decay), NN)
            for kind, piece in enumerate((grad_query, grad_key, grad_value)):
                staged[kind * part + head * HD : kind * part + (head + 1) * HD, :] = piece[:HD]
            inside = mm(product, later, NN)
            inside = jnp.sum(jnp.where(key_at < query_at, inside, 0.0), axis=0, keepdims=True)
            span_decay = jnp.exp(last)
            across = jnp.sum(back * state, keepdims=True) * span_decay
            rows_ref[0, head : head + 1, :] = jnp.sum(query_wide * query_in, axis=0, keepdims=True)
            rows_ref[1, head : head + 1, :] = jnp.sum(key_wide * key_out, axis=0, keepdims=True)
            rows_ref[2, head : head + 1, :] = inside + across
            after.append(back * span_decay + mm(grad, low(query_wide * in_decay), NT))
        grad_log = (
            running_sum(rows_ref[0], SPAN, reverse=True)
            + running_sum(rows_ref[1], SPAN, exclusive=True)
            + rows_ref[2]
        )
        grad_forget = grad_log / (1.0 + jnp.exp(logit_ref[:, lanes]))
        staged[3 * part : 3 * part + heads, :] = grad_forget[:heads]
        gproj[:wide_rows, lanes] = low(staged[...])
        return tuple(after)

    lax.fori_loop(
        0, spans, one_span, tuple(jnp.zeros((HEAD_ROWS, HEAD_ROWS), jnp.float32) for _ in range(heads))
    )


GELU_SLOPE = math.sqrt(2.0 / math.pi)
GELU_CUBE = 0.044715
X_FIRST, Z_FIRST = (0, 1, 2), (1, 0, 2)


def layer_kernel(
    shard_count, heads, direct,
    x_hbm, cot_hbm, silu_ref, ada_hbm, bias_ref, qkv_hbm, gate_ref, gate_bias_ref, conv_ref, out_w_ref, up_hbm,
    down_hbm, cond_ref, label_ref,
    gtokens_ref, out_ref, gdown_out, gup_out, gqkv_out, gout_out, gclass_ref, gada_ref, gsmall_ref, normed_hbm,
    wback_hbm,
    x_ref, cot_ref, up, down, turned, gmlp, gact, normed, act, gup_rows, gattn,
    attn, after, gafter, mix_ref,
    a_pair_out, a_pair_in, a_far_out, a_far_in, a_keep,
    g_pair_out, g_pair_in, g_far_out, g_far_in, g_keep,
    mod_parts, first_rows, second_rows, third_rows, silu_rows,
    proj, rec, states, logit_ref, stats_ref, cum_ref, col_ref, span_rows, taps, gtaps, mods_ref, gmods, ada_rest,
    parcels, latent_in, mods_out, mods_in, gcond, silu_own, mods_own, label_own,
    down_a, down_b, up_a, up_b, qkv_a, qkv_b, out_a,
    raw_sems, part_sems, gm_sems, a_sems, n_sems, g_sems, t_sems, m_sems, s_sems, first_sems, second_sems,
    third_sems, silu_sems, dp_sems, down_a_sems, down_b_sems, up_a_sems, up_b_sems, qkv_a_sems, qkv_b_sems,
    out_a_sems, move_sems,
):
    part, length = x_ref.shape
    width = 4 * part
    own_width = width // shard_count
    hidden = up.shape[1]
    chunks = length // CHUNK
    lanes = [pl.ds(k * CHUNK, CHUNK) for k in range(chunks)]
    where = places()
    me, across, beside, _ = where
    spot = lax.axis_index("dp")
    own, other = shard(me, part), shard(across, part)
    projected = qkv_hbm.shape[0]
    raw, wide = act, down.at[:WIDE_ROWS, :]
    moves = Moves(move_sems)
    moves.start("ada", ada_hbm.at[:width, :], up)
    moves.start("ada_rest", ada_hbm.at[width:, :], ada_rest)
    moves.start("raw", x_hbm, raw.at[own, :])
    moves.start("qkv", qkv_hbm, wide.at[:projected, :])
    moves.start("cot", cot_hbm, cot_ref)
    moves.start("x", x_hbm, x_ref)
    for rows in (mod_parts, first_rows, second_rows, third_rows, silu_rows, parcels, mods_out):
        rows[...] = jnp.zeros(rows.shape, rows.dtype)
    barrier = pltpu.get_barrier_semaphore()
    for peer in where[1:]:
        pl.semaphore_signal(barrier, inc=1, device_id={"tensor": peer}, device_id_type=MESH)
    for step in range(1, shard_count):
        pl.semaphore_signal(
            barrier, inc=1, device_id={"dp": lax.rem(spot + step, shard_count)}, device_id_type=MESH
        )
    pl.semaphore_wait(barrier, shard_count + 2)

    spread = Spread(where, raw, raw_sems, part)
    gm_spread = Spread(where, gmlp, gm_sems, part)
    spread.start(0, lanes[0], x_hbm.at[:, lanes[0]])
    spread.start(1, lanes[1], x_hbm.at[:, lanes[1]])
    part_at = lax.broadcasted_iota(jnp.int32, (8, part), 0)
    bias = bias_ref[...].astype(jnp.float32)
    mod_sum = jnp.concatenate([bias, jnp.zeros((8 - bias.shape[0], part), jnp.float32)], axis=0)
    silu_rows_low = silu_ref[...]

    def ada_piece(index):
        if index < 4:
            return up[index * part : (index + 1) * part, :]
        return ada_rest[(index - 4) * part : (index - 3) * part, :]

    moves.wait("ada")
    moves.wait("ada_rest")
    for index in range(6):
        mod_sum = mod_sum + jnp.where(part_at == index, mm(silu_rows_low, ada_piece(index), NT), 0.0)
    mod_parts[me, :, :part] = mod_sum
    part_copies = [
        send(mod_parts.at[me], mod_parts.at[me], part_sems, index, peer) for index, peer in enumerate(where[1:])
    ]
    spread.start(2, lanes[2], x_hbm.at[:, lanes[2]])
    spread.start(3, lanes[3], x_hbm.at[:, lanes[3]])
    moves.start("up", up_hbm, up)
    mods_ref[...] = jnp.transpose(mod_parts[me])[:part]
    moves.wait("cot")
    gmlp[own, :] = low(cot_ref[...].astype(jnp.float32) * mods_ref[:, 5:6])
    for k in range(3):
        gm_spread.start(k, lanes[k])
    moves.wait("qkv")
    gate = gate_ref[...].astype(jnp.float32)
    wide[projected:, :] = low(
        jnp.concatenate([gate, jnp.zeros((WIDE_ROWS - projected - heads, width), jnp.float32)], axis=0)
    )
    turned[:, :WIDE_ROWS] = jnp.transpose(wide[...])
    moves.start("wback_out", turned.at[:, :WIDE_ROWS], wback_hbm)
    gate_at = lax.broadcasted_iota(jnp.int32, (8, 1), 0)
    gate_bias = jnp.zeros((8, 1), jnp.float32)
    for head in range(heads):
        gate_bias = gate_bias + jnp.where(gate_at == head, gate_bias_ref[0:1, head : head + 1].astype(jnp.float32), 0.0)
    conv = [conv_ref[index].astype(jnp.float32) for index in range(3)]
    taps[...] = jnp.transpose(jnp.concatenate(conv + [jnp.zeros((7, part), jnp.float32)], axis=0))
    stats_ref[2:, :] = jnp.zeros((6, length), jnp.float32)
    moves.wait("raw")
    for copy in part_copies:
        copy.wait_recv()
    columns = [jnp.transpose(mod_parts[index])[:part] for index in range(4)]
    filler = jnp.zeros((HEAD_ROWS - HD, CHUNK), jnp.float32)
    carried = [jnp.zeros((HEAD_ROWS, HEAD_ROWS), jnp.float32) for _ in range(heads)]

    def project_chunk(k, carried):
        spread.end(k)
        blocks = [raw[index * part : (index + 1) * part, lanes[k]].astype(jnp.float32) for index in range(4)]
        mean = sum(row_sums(block) for block in blocks) / width
        square = sum(row_sums(block * block) for block in blocks) / width
        inv_std = lax.rsqrt(square - mean * mean + norm_eps)
        stats_ref[0:1, lanes[k]] = mean
        stats_ref[1:2, lanes[k]] = inv_std
        for index in range(4):
            unit = (blocks[index] - mean) * inv_std
            value = unit * (1.0 + columns[index][:, 1:2]) + columns[index][:, 0:1]
            gattn[index * part : (index + 1) * part, lanes[k]] = low(value)
        product = mm(wide[...], gattn[:, lanes[k]], NN)
        for index in range(3 * heads):
            piece = jnp.concatenate([product[index * HD : (index + 1) * HD], filler], axis=0)
            proj[index * HEAD_ROWS : (index + 1) * HEAD_ROWS, lanes[k]] = low(piece)
        logit = product[projected : projected + 8] + gate_bias
        logit_ref[:, lanes[k]] = logit
        cum = running_sum(log_sigmoid(logit), SPAN)
        cum_ref[:, lanes[k]] = cum
        col_ref[lanes[k], :] = jnp.transpose(cum)
        return span_forward(heads, k, lanes[k], carried, proj, cum_ref, col_ref, rec, states)

    for k in range(chunks):
        spread.relay(k, lanes[k])
        if k > 0:
            carried = project_chunk(k - 1, carried)
    project_chunk(chunks - 1, carried)
    spread.finish()
    moves.start("normed_out", gattn, normed_hbm)
    moves.start("down", down_hbm, down)
    gm_spread.relay(0, lanes[0])
    conv_forward(rec, taps, mix_ref)
    gm_spread.relay(1, lanes[1])
    gate_one, scale_two, shift_two = mods_ref[:, 2:3], mods_ref[:, 4:5], mods_ref[:, 3:4]

    attn_sum = Reduce(where, part, (a_pair_out, a_pair_in, a_far_out, a_far_in, a_keep), a_sems)
    mlp_sum = Reduce(where, part, (a_pair_out, a_pair_in, a_far_out, a_far_in, a_keep), m_sems)
    grad_sum = Reduce(where, part, (g_pair_out, g_pair_in, g_far_out, g_far_in, g_keep), g_sems)
    last_sum = Reduce(where, part, (g_pair_out, g_pair_in, g_far_out, g_far_in, g_keep), s_sems)
    norm_spread = Spread(where, normed, n_sems, part)
    grad_spread = Spread(where, gattn, t_sems, part)
    moments = Rows(where, first_rows, first_sems)
    means = Rows(where, second_rows, second_sems)
    last_means = Rows(where, third_rows, third_sems)
    if direct:
        totals = {}
        for name, buffer, result, (first, second), sems in (
            ("down", up, gdown_out, (down_a, down_b), (down_a_sems, down_b_sems)),
            ("up", down, gup_out, (up_a, up_b), (up_a_sems, up_b_sems)),
            ("qkv", act, gqkv_out, (qkv_a, qkv_b), (qkv_a_sems, qkv_b_sems)),
        ):
            cut = first.shape[2]
            totals[name + "_a"] = Halving(shard_count, buffer, pl.ds(0, cut), first, sems[0], X_FIRST, result)
            totals[name + "_b"] = Halving(
                shard_count, buffer, pl.ds(cut, second.shape[2]), second, sems[1], Z_FIRST, result
            )
        totals["out"] = Halving(
            shard_count, gup_rows, pl.ds(0, out_a.shape[2]), out_a, out_a_sems, X_FIRST, gout_out
        )

    def begin(*names):
        if direct:
            for name in names:
                totals[name].start()

    def advance(*names):
        if direct:
            for name in names:
                totals[name].step()

    moves.wait("wback_out")
    turned[:, :part] = jnp.transpose(out_w_ref[...])
    gmods[...] = jnp.zeros_like(gmods)
    gmix = gtokens_ref

    def attn_start(k):
        mixed = mix_ref[:, lanes[k]]
        attn_sum.start(k, lanes[k], lambda owner: mm(turned[shard(owner, part), :part], mixed, NN))

    def attn_end(k):
        value = attn_sum.end(k, lanes[k])
        attn[:, lanes[k]] = value
        total = x_ref[:, lanes[k]].astype(jnp.float32) + gate_one * value
        after[:, lanes[k]] = total
        moments.start(k, lanes[k], row_sums(total), row_sums(total * total))

    inverse, average = [None] * chunks, [None] * chunks

    def unit_two(k):
        return (after[:, lanes[k]] - average[k]) * inverse[k]

    def norm_chunk(k):
        total, squares = moments.end(k, lanes[k])
        average[k] = total / width
        inverse[k] = lax.rsqrt(squares / width - average[k] * average[k] + norm_eps)
        normed[own, lanes[k]] = low(unit_two(k) * (1.0 + scale_two) + shift_two)
        norm_spread.start(k, lanes[k])

    def grad_act_chunk(k):
        gact[...] = mm(down[...], gmlp[:, lanes[k]], NN)

    def hidden_chunk(k):
        norm_spread.end(k)
        block = normed[:, lanes[k]]

        def one_block(at, carry):
            rows = pl.ds(pl.multiple_of(at * part, 32), part)
            value = mm(turned[rows, :], block, NN)
            square = value * value
            bend = jnp.tanh(GELU_SLOPE * value * (1.0 + GELU_CUBE * square))
            half = 0.5 * (1.0 + bend)
            act[rows, lanes[k]] = low(value * half)
            slope = half + 0.5 * value * (1.0 - bend * bend) * GELU_SLOPE * (1.0 + 3.0 * GELU_CUBE * square)
            gup_rows[rows, lanes[k]] = low(gact[rows, :] * slope)
            return carry

        lax.fori_loop(0, hidden // part, one_block, 0)

    def grad_start(k):
        block = gup_rows[:, lanes[k]]
        grad_sum.start(k, lanes[k], lambda owner: mm(up[shard(owner, part), :], block, NN))

    def grad_end(k):
        grad = grad_sum.end(k, lanes[k])
        rows = unit_two(k)
        gmods[:, 3:4] += column_sums(grad)
        gmods[:, 4:5] += column_sums(grad * rows)
        scaled = grad * (1.0 + scale_two)
        gafter[:, lanes[k]] = scaled
        means.start(k, lanes[k], row_sums(scaled), row_sums(scaled * rows))

    def after_chunk(k):
        total, along = means.end(k, lanes[k])
        scaled = gafter[:, lanes[k]]
        back = inverse[k] * (scaled - total / width - unit_two(k) * (along / width))
        grad = cot_ref[:, lanes[k]].astype(jnp.float32) + back
        gafter[:, lanes[k]] = grad
        gattn[own, lanes[k]] = low(grad * gate_one)
        grad_spread.start(k, lanes[k])
        gmods[:, 2:3] += column_sums(grad * attn[:, lanes[k]])

    def mixed_chunk(k):
        grad_spread.end(k)
        gmix[:, lanes[k]] = mm(out_w_ref[...], gattn[:, lanes[k]], NN)

    def weight_grad(target, columns, left, right, at, pieces):
        rows = target.shape[0] // pieces
        rows = slice(at * rows, (at + 1) * rows)
        target[rows, columns] = low(mm(left[rows, :], right[...], NT))

    def mlp_start(k):
        block = act[:, lanes[k]]
        mlp_sum.start(k, lanes[k], lambda owner: mm(turned[shard(owner, part), :], block, NN))

    def outputs(k):
        mlp = mlp_sum.end(k, lanes[k])
        out_ref[:, lanes[k]] = low(after[:, lanes[k]] + mods_ref[:, 5:6] * mlp)
        gmods[:, 5:6] += column_sums(cot_ref[:, lanes[k]].astype(jnp.float32) * mlp)

    every_column = slice(None)
    attn_start(0)
    attn_start(1)
    attn_sum.relay(0, lanes[0])
    attn_start(2)
    attn_sum.relay(1, lanes[1])
    attn_start(3)
    moves.wait("up")
    turned[...] = jnp.transpose(up[...])
    moves.wait("x")
    attn_end(0)
    attn_sum.relay(2, lanes[2])
    gm_spread.relay(2, lanes[2])
    moves.wait("down")
    moves.wait("normed_out")
    gm_spread.end(0)
    grad_act_chunk(0)
    attn_end(1)
    norm_chunk(0)
    attn_sum.relay(3, lanes[3])
    gm_spread.start(3, lanes[3])
    attn_end(2)
    norm_chunk(1)
    norm_spread.relay(0, lanes[0])
    hidden_chunk(0)
    attn_end(3)
    norm_chunk(2)
    grad_start(0)
    norm_spread.relay(1, lanes[1])
    norm_chunk(3)
    gm_spread.relay(3, lanes[3])
    grad_sum.relay(0, lanes[0])
    gm_spread.end(1)
    grad_act_chunk(1)
    hidden_chunk(1)
    grad_start(1)
    norm_spread.relay(2, lanes[2])
    grad_sum.relay(1, lanes[1])
    gm_spread.end(2)
    grad_act_chunk(2)
    hidden_chunk(2)
    grad_start(2)
    norm_spread.relay(3, lanes[3])
    grad_end(0)
    grad_sum.relay(2, lanes[2])
    gm_spread.end(3)
    grad_act_chunk(3)
    hidden_chunk(3)
    grad_start(3)
    weight_grad(up, every_column, gmlp, act, 0, 2)
    after_chunk(0)
    grad_sum.relay(3, lanes[3])
    weight_grad(up, every_column, gmlp, act, 1, 2)
    begin("down_a", "down_b")
    if not direct:
        moves.start("gdown", up, gdown_out)
    grad_end(1)
    turned[...] = jnp.transpose(down[...])
    grad_spread.relay(0, lanes[0])
    after_chunk(1)
    grad_end(2)
    weight_grad(down, every_column, normed, gup_rows, 0, 2)
    after_chunk(2)
    grad_spread.relay(1, lanes[1])
    mixed_chunk(0)
    grad_end(3)
    weight_grad(down, every_column, normed, gup_rows, 1, 2)
    begin("up_a", "up_b")
    if not direct:
        moves.start("gup", down, gup_out)
    after_chunk(3)
    attn_sum.finish()
    grad_spread.relay(2, lanes[2])
    mixed_chunk(1)
    mlp_start(0)
    mlp_start(1)
    mlp_sum.relay(0, lanes[0])
    mixed_chunk(2)
    mlp_start(2)
    mlp_sum.relay(1, lanes[1])
    grad_spread.relay(3, lanes[3])
    mlp_start(3)
    mlp_sum.relay(2, lanes[2])
    norm_spread.finish()
    moves.start("normed", normed_hbm, normed)
    mixed_chunk(3)
    advance("down_b")
    weight_grad(gup_rows, slice(0, part), gattn, mix_ref, 0, 1)
    begin("out")
    mlp_sum.relay(3, lanes[3])
    moves.start("wback", wback_hbm, turned.at[:, :WIDE_ROWS])
    if not direct:
        moves.start("gout", gup_rows.at[:, : out_a.shape[2]], gout_out)

    conv_backward(gmix, rec, taps, attn, gtaps)
    grad_spread.finish()
    grad_sum.finish()
    advance("down_a", "up_b")
    staged = gact.at[:WIDE_ROWS, :]
    spans_backward(heads, proj, logit_ref, cum_ref, col_ref, states, attn, staged, span_rows, gattn)
    advance("down_a", "up_a")
    gproj = gattn.at[:WIDE_ROWS, :]

    def last_start(k):
        block = gproj[:, lanes[k]]
        last_sum.start(k, lanes[k], lambda owner: mm(turned[shard(owner, part), :WIDE_ROWS], block, NN))

    def unit_one(k):
        return (x_ref[:, lanes[k]].astype(jnp.float32) - stats_ref[0:1, lanes[k]]) * stats_ref[1:2, lanes[k]]

    def last_end(k):
        grad = last_sum.end(k, lanes[k])
        unit = unit_one(k)
        gmods[:, 0:1] += column_sums(grad)
        gmods[:, 1:2] += column_sums(grad * unit)
        scaled = grad * (1.0 + mods_ref[:, 1:2])
        gtokens_ref[:, lanes[k]] = scaled
        last_means.start(k, lanes[k], row_sums(scaled), row_sums(scaled * unit))

    def tokens(k):
        total, along = last_means.end(k, lanes[k])
        back = gtokens_ref[:, lanes[k]] - total / width - unit_one(k) * (along / width)
        gtokens_ref[:, lanes[k]] = gafter[:, lanes[k]] + stats_ref[1:2, lanes[k]] * back

    moves.wait("wback")
    last_start(0)
    last_start(1)
    last_sum.relay(0, lanes[0])
    last_start(2)
    last_sum.relay(1, lanes[1])
    last_start(3)
    last_sum.relay(2, lanes[2])
    moves.wait("normed")
    for piece in range(2):
        weight_grad(act, slice(0, WIDE_ROWS), normed, gproj, piece, 2)
    last_sum.relay(3, lanes[3])
    moves.start("ada_again", ada_hbm.at[:width, :], turned)
    begin("qkv_a", "qkv_b")
    if not direct:
        moves.start("gqkv", act.at[:, :WIDE_ROWS], gqkv_out)
    advance("down_b", "up_b")
    for k in range(chunks):
        outputs(k)
    advance("up_a", "down_a", "out")
    for k in range(chunks):
        last_end(k)
        if k > 0:
            tokens(k - 1)
    advance("down_b", "up_b")

    mod_rows = jnp.transpose(gmods[...])
    low_rows = low(mod_rows)
    row_at = lax.broadcasted_iota(jnp.int32, (8, width), 0)
    moves.wait("ada_again")
    product = jnp.zeros((8, width), jnp.float32)
    for index in range(6):
        piece = turned[index * part : (index + 1) * part, :] if index < 4 else ada_piece(index)
        product = product + jnp.where(row_at == index, mm(low_rows, piece, NN), 0.0)
    silu_rows[me, 0:1, :] = row_sums(product)
    silu_copies = [
        send(silu_rows.at[me], silu_rows.at[me], silu_sems, index, peer) for index, peer in enumerate(where[1:])
    ]
    tap_rows = jnp.transpose(gtaps[...])
    forget = gattn[3 * part : WIDE_ROWS, :].astype(jnp.float32)[:8]
    forget = jnp.transpose(jnp.broadcast_to(column_sums(forget), (8, 128)))[0:1]
    small = jnp.concatenate([mod_rows[:6], tap_rows[:9], jnp.zeros((1, part), jnp.float32)], axis=0)
    mods_out[:, :part] = low(small)
    mods_out[:, part : part + 8] = low(jnp.broadcast_to(forget, (16, 8)))
    mods_in[spot] = mods_out[...]
    dp_copies = []
    for step in range(1, shard_count):
        peer = lax.rem(spot + step, shard_count)
        dp_copies.append(send_dp(mods_out, mods_in.at[spot], dp_sems, step, peer))
    tokens(chunks - 1)
    for copy in silu_copies:
        copy.wait_recv()
    grad_silu = sum(silu_rows[index, 0:1, :] for index in range(4))
    cond = cond_ref[0:1, :]
    sigmoid = 1.0 / (1.0 + jnp.exp(-cond))
    grad_cond = grad_silu * (sigmoid * (1.0 + cond * (1.0 - sigmoid)))
    silu = low(cond * sigmoid).astype(jnp.float32)
    for index in range(shard_count):
        columns = slice(index * own_width, (index + 1) * own_width)
        parcels[index, 0:1, :own_width] = grad_cond[:, columns]
        parcels[index, 1:2, :own_width] = silu[:, columns]
        parcels[index, 2:3, :] = jnp.broadcast_to(label_ref[...], (1, parcels.shape[2]))
    latent_in[spot] = parcels[spot]
    for step in range(1, shard_count):
        peer = lax.rem(spot + step, shard_count)
        dp_copies.append(send_dp(parcels.at[peer], latent_in.at[spot], dp_sems, shard_count + step, peer))
    advance("up_a", "qkv_b", "out", "qkv_a")
    for copy in dp_copies:
        copy.wait_recv()
    small_sum = jnp.zeros(mods_out.shape, jnp.float32)
    for index in range(shard_count):
        arrived = mods_in[index].astype(jnp.float32)
        small_sum = small_sum + arrived
        for row in range(6):
            mods_own[row, index : index + 1, :] = arrived[row : row + 1, :part]
        gcond[index : index + 1, :] = latent_in[index, 0:1, :own_width]
        silu_own[index : index + 1, :] = latent_in[index, 1:2, :own_width]
        label_own[index : index + 1, :] = latent_in[index, 2:3, :128]
    gsmall_ref[...] = small_sum
    class_at = lax.broadcasted_iota(jnp.int32, (shard_count, NCLASS), 1).astype(jnp.float32)
    onehot = jnp.where(label_own[:, 0:1] == class_at, 1.0, 0.0)
    gclass_ref[...] = lax.dot_general(
        gcond[...], onehot, TN, precision=TOP_PRECISION, preferred_element_type=jnp.float32
    )
    for row in range(6):
        gada_ref[row] = mm(low(silu_own[...]), low(mods_own[row]), TN)
    advance("qkv_b", "out", "qkv_a", "qkv_b", "qkv_a")
    if direct:
        for total in totals.values():
            total.finish()
    else:
        for name in ("gdown", "gup", "gqkv", "gout"):
            moves.wait(name)
    for copy in part_copies + dp_copies + silu_copies:
        copy.wait_send()
    for group in (gm_spread, mlp_sum, last_sum, moments, means, last_means):
        group.finish()


def layer(
    x, cot, silu, ada, bias, qkv, gate, gate_bias, conv, out_w, up, down, cond, label, shard_count, heads, direct
):
    part, length = x.shape
    width = 4 * part
    hidden = up.shape[1]
    own = width // shard_count
    chunks = length // CHUNK
    spans = length // SPAN
    padded = part + -part % 128
    own_padded = own + -own % 128
    proj_rows = 3 * heads * HEAD_ROWS
    shape = jax.ShapeDtypeStruct
    vmem = pltpu.VMEM
    bf16, f32 = jnp.bfloat16, jnp.float32
    grad_rows, grad_type, grad_spec = (own, f32, VMEM_SPEC) if direct else (width, bf16, ANY_SPEC)
    arrivals = shard_count if direct else 2
    arrival_rows = width if direct else 32
    cuts = (768, hidden - 768, 640, hidden - 640, 512, WIDE_ROWS - 512, padded)
    return pl.pallas_call(
        functools.partial(layer_kernel, shard_count, heads, direct),
        out_shape=(
            shape((part, length), f32),
            shape((part, length), bf16),
            shape((grad_rows, hidden), grad_type),
            shape((grad_rows, hidden), grad_type),
            shape((grad_rows, WIDE_ROWS), grad_type),
            shape((grad_rows, padded), grad_type),
            shape((own, NCLASS), f32),
            shape((6, own, part), f32),
            shape((16, padded), f32),
            shape((width, length), bf16),
            shape((width, WIDE_ROWS), bf16),
        ),
        in_specs=[
            ANY_SPEC, ANY_SPEC, VMEM_SPEC, ANY_SPEC, VMEM_SPEC, ANY_SPEC, VMEM_SPEC, VMEM_SPEC, VMEM_SPEC, VMEM_SPEC,
            ANY_SPEC, ANY_SPEC, VMEM_SPEC, VMEM_SPEC,
        ],
        out_specs=[VMEM_SPEC, VMEM_SPEC] + [grad_spec] * 4 + [VMEM_SPEC] * 3 + [ANY_SPEC] * 2,
        scratch_shapes=[
            vmem((part, length), bf16),
            vmem((part, length), bf16),
            vmem((width, hidden), bf16),
            vmem((hidden, width), bf16),
            vmem((hidden, width), bf16),
            vmem((width, length), bf16),
            vmem((hidden, CHUNK), f32),
            vmem((width, length), bf16),
            vmem((hidden, length), bf16),
            vmem((hidden, length), bf16),
            vmem((width, length), bf16),
            *[vmem((part, length), f32)] * 3,
            vmem((part, length), bf16),
            *reduce_scratch(part, length),
            *reduce_scratch(part, length),
            vmem((4, 8, padded), f32),
            *[vmem((4, 8, length), f32)] * 3,
            vmem((4, 8, width), f32),
            vmem((proj_rows, length), bf16),
            vmem((part, length), f32),
            vmem((spans, heads, HEAD_ROWS, HEAD_ROWS), f32),
            vmem((8, length), f32),
            vmem((8, length), f32),
            vmem((8, length), f32),
            vmem((length, 8), f32),
            vmem((3, 8, SPAN), f32),
            vmem((part, 16), f32),
            vmem((part, 16), f32),
            vmem((part, 8), f32),
            vmem((part, 8), f32),
            vmem((ada.shape[0] - width, width), bf16),
            vmem((shard_count, 8, own_padded), f32),
            vmem((shard_count, 8, own_padded), f32),
            vmem((16, padded), bf16),
            vmem((shard_count, 16, padded), bf16),
            vmem((shard_count, own), f32),
            vmem((shard_count, own), f32),
            vmem((6, shard_count, part), f32),
            vmem((shard_count, 128), f32),
            *[halving_scratch(arrivals, arrival_rows, cut) for cut in cuts],
            copy_sems(3 * chunks),
            copy_sems(3),
            *[copy_sems(3 * chunks)] * 10,
            copy_sems(3),
            copy_sems(2 * shard_count),
            *[copy_sems(shard_count)] * 7,
            pltpu.SemaphoreType.DMA((20,)),
        ],
        compiler_params=pltpu.CompilerParams(
            collective_id=1, has_side_effects=True, vmem_limit_bytes=VMEM_LIMIT
        ),
        cost_estimate=work_for(180),
        name="layer",
    )(x, cot, silu, ada, bias, qkv, gate, gate_bias, conv, out_w, up, down, cond, label)


def finish_kernel(
    heads, tokens_ref, out_ref, class_ref, ada_ref, down_ref, up_ref, qkv_ref, out_w_ref, small_ref,
    tokens_to, out_to, class_to, ada_to, down_to, up_to, qkv_to, gate_to, out_w_to, ada_b_to, gate_b_to, conv_to,
    sems,
):
    pairs = (
        (tokens_ref, tokens_to), (out_ref, out_to), (class_ref, class_to), (ada_ref, ada_to), (down_ref, down_to),
        (up_ref, up_to),
    )
    moves = Moves(sems)
    for index, (source, target) in enumerate(pairs):
        moves.start(index, source, target)
    part = out_w_to.shape[1]
    for kind in range(3):
        qkv_to[kind] = qkv_ref[:, kind * part : (kind + 1) * part]
    gate_to[...] = jnp.transpose(qkv_ref[:, 3 * part : 3 * part + 8])[:heads]
    out_w_to[...] = out_w_ref[:, :part]
    ada_b_to[...] = small_ref[:6, :part]
    gate_b_to[...] = small_ref[15:16, part : part + heads]
    for row in range(3):
        conv_to[row] = small_ref[6 + 3 * row : 9 + 3 * row, :part]
    for index in range(len(pairs)):
        moves.wait(index)


def finish(heads, part, tokens, out, grad_class, grad_ada, grad_down, grad_up, grad_wide, grad_out_w, small):
    own = grad_wide.shape[0]
    shape = jax.ShapeDtypeStruct
    f32 = jnp.float32
    whole = (tokens, out, grad_class, grad_ada, grad_down, grad_up)
    return pl.pallas_call(
        functools.partial(finish_kernel, heads),
        out_shape=(
            *[shape(array.shape, array.dtype) for array in whole],
            shape((3, own, part), f32),
            shape((heads, own), f32),
            shape((own, part), f32),
            shape((6, part), f32),
            shape((1, heads), f32),
            shape((3, 3, part), f32),
        ),
        in_specs=[ANY_SPEC] * 6 + [VMEM_SPEC] * 3,
        out_specs=[ANY_SPEC] * 6 + [VMEM_SPEC] * 6,
        scratch_shapes=[pltpu.SemaphoreType.DMA((6,))],
        cost_estimate=work_for(5),
        name="finish",
    )(*whole, grad_wide, grad_out_w, small)


def shards(
    latent_tokens,
    timesteps,
    labels,
    class_table,
    ada_weight,
    ada_bias,
    query_key_value_weight,
    gate_weight,
    gate_bias,
    conv_weight,
    out_weight,
    up_weight,
    down_weight,
    cotangent,
):
    part = latent_tokens.shape[2]
    heads = gate_weight.shape[1]
    shard_count = lax.psum(1, "dp")
    own_width = MODEL_DIM // shard_count
    x = latent_tokens[0].T
    cot = cotangent[0].T
    qkv = jnp.transpose(query_key_value_weight, (1, 2, 0)).reshape(3 * part, MODEL_DIM)
    ada = jnp.transpose(ada_weight, (1, 2, 0)).reshape(6 * part, MODEL_DIM)
    cond = lax.dynamic_slice_in_dim(class_table, labels[0], 1, axis=0).astype(jnp.float32) + embed_time(
        timesteps, MODEL_DIM
    )
    silu = jnp.broadcast_to(low(jax.nn.silu(cond)), (8, MODEL_DIM))
    direct = shard_count == 8 and own_width % 16 == 0
    grad_tokens, layer_out, grad_down, grad_up, grad_wide, grad_out_w, grad_class, grad_ada_w, small, _, _ = layer(
        x, cot, silu, ada, ada_bias, qkv, gate_weight.T, gate_bias[None], conv_weight, out_weight, up_weight,
        down_weight, cond, labels.astype(jnp.float32)[None], shard_count, heads, direct,
    )
    if not direct:
        grad_down, grad_up, grad_wide, grad_out_w = (
            lax.psum_scatter(partial, "dp", scatter_dimension=0, tiled=True).astype(jnp.float32)
            for partial in (grad_down, grad_up, grad_wide, grad_out_w)
        )
    (
        grad_tokens, layer_out, grad_class, grad_ada_w, grad_down, grad_up, grad_qkv, grad_gate_w, grad_out_w,
        grad_ada_b, grad_gate_b, grad_conv,
    ) = finish(
        heads, part, grad_tokens, layer_out, grad_class, grad_ada_w, grad_down, grad_up, grad_wide, grad_out_w, small
    )
    return (
        layer_out.T[None],
        grad_tokens.T[None],
        grad_class.T,
        jnp.transpose(grad_ada_w, (1, 0, 2)),
        grad_ada_b,
        jnp.transpose(grad_qkv, (1, 0, 2)),
        grad_gate_w.T,
        grad_gate_b[0],
        grad_conv,
        grad_out_w.T,
        grad_up,
        grad_down.T,
    )


def solution(mesh):
    in_specs = (
        P("dp", None, "tensor"),
        P("dp"),
        P("dp"),
        P(),
        P(None, None, "tensor"),
        P(None, "tensor"),
        P(None, None, "tensor"),
        P(None, "tensor"),
        P("tensor"),
        P(None, None, "tensor"),
        P("tensor", None),
        P(None, "tensor"),
        P("tensor", None),
        P("dp", None, "tensor"),
    )
    out_specs = (
        P("dp", None, "tensor"),
        P("dp", None, "tensor"),
        P(None, "dp"),
        P("dp", None, "tensor"),
        P(None, "tensor"),
        P("dp", None, "tensor"),
        P("dp", "tensor"),
        P("tensor"),
        P(None, None, "tensor"),
        P("tensor", "dp"),
        P("dp", "tensor"),
        P("tensor", "dp"),
    )
    return jax.shard_map(shards, mesh=mesh, in_specs=in_specs, out_specs=out_specs, check_vma=False)
```

```python
import functools
import math

import jax
import jax.numpy as jnp
from jax import lax
from jax.experimental import pallas as pl
from jax.experimental.pallas import tpu as pltpu
from jax.sharding import PartitionSpec as P

MODEL_DIM = 1152
HD = 72
HEAD_ROWS = 80
CONV_ROWS = 144
BACK_ROWS = 96
NCLASS = 1000
GRID = 32


TOP_PRECISION = lax.Precision.HIGHEST
norm_eps = 1e-06


def embed_time(time_steps, model_width):
    half_width = model_width // 2
    frequency = jnp.exp(-math.log(10000.0) * jnp.arange(half_width, dtype=jnp.float32) / half_width)
    angles = time_steps.astype(jnp.float32)[:, None] * frequency[None, :]
    return jnp.concatenate([jnp.cos(angles), jnp.sin(angles)], axis=1)


SPAN = 256

TN = (((0,), (0,)), ((), ()))
NT = (((1,), (1,)), ((), ()))
NN = (((1,), (0,)), ((), ()))


def mm(left, right, form):
    return lax.dot_general(left, right, form, preferred_element_type=jnp.float32)


def low(values):
    return values.astype(jnp.bfloat16)


def shifted(rows, offset):
    length = rows.shape[1]
    return pltpu.roll(rows, (-offset) % length, 1)


def edge_masks(length, begin=0, end=None):
    end = length if end is None else end
    token = lax.broadcasted_iota(jnp.int32, (1, end - begin), 1) + begin
    column = lax.rem(token, GRID)
    return column > 0, column < GRID - 1, token >= GRID, token < length - GRID


def neighbours(rows, masks):
    left_ok, right_ok, _, _ = masks
    return (
        jnp.where(left_ok, shifted(rows, -1), 0.0),
        rows,
        jnp.where(right_ok, shifted(rows, 1), 0.0),
    )


def running_sum(rows, span, reverse=False, exclusive=False):
    length = rows.shape[1]
    place = lax.rem(lax.broadcasted_iota(jnp.int32, (1, length), 1), span)
    total = rows
    step = 1
    if exclusive:
        total = (
            jnp.where(place < span - 1, shifted(total, 1), 0.0)
            if reverse
            else jnp.where(place >= 1, shifted(total, -1), 0.0)
        )
    while step < span:
        if reverse:
            total = total + jnp.where(place < span - step, shifted(total, step), 0.0)
        else:
            total = total + jnp.where(place >= step, shifted(total, -step), 0.0)
        step *= 2
    return total


def log_sigmoid(logit):
    return jnp.minimum(logit, 0.0) - jnp.log(1.0 + jnp.exp(-jnp.abs(logit)))


def conv_rows(rows, taps, masks, adjoint):
    _, _, up_ok, down_ok = masks
    left, middle, right = neighbours(rows, masks)
    parts = []
    for row in range(3):
        if adjoint:
            weights = [taps[:, 3 * (2 - row) + 2 - col : 3 * (2 - row) + 3 - col] for col in range(3)]
        else:
            weights = [taps[:, 3 * row + col : 3 * row + col + 1] for col in range(3)]
        parts.append(left * weights[0] + middle * weights[1] + right * weights[2])
    above = jnp.where(up_ok, shifted(parts[0], -GRID), 0.0)
    below = jnp.where(down_ok, shifted(parts[2], GRID), 0.0)
    return above + parts[1] + below


def decay_block(row, column):
    span = row.shape[1]
    key_at = lax.broadcasted_iota(jnp.int32, (span, span), 0)
    query_at = lax.broadcasted_iota(jnp.int32, (span, span), 1)
    return jnp.where(query_at >= key_at, jnp.exp(jnp.minimum(row - column, 0.0)), 0.0)


MESH = pl.DeviceIdType.MESH
CHUNK = 256
VMEM_LIMIT = 63 * 2**20
VMEM_SPEC = pl.BlockSpec(memory_space=pltpu.VMEM)
ANY_SPEC = pl.BlockSpec(memory_space=pl.ANY)
WIDE_ROWS = 896


def work_for(microseconds):
    return pl.CostEstimate(flops=int(microseconds * 1e9), bytes_accessed=0, transcendentals=0)


def places():
    me = lax.axis_index("tensor")
    across = lax.rem(me + 2, 4)
    beside = me + 1 - 2 * lax.rem(me, 2)
    corner = lax.rem(beside + 2, 4)
    return me, across, beside, corner


def greet(peers):
    barrier = pltpu.get_barrier_semaphore()
    for peer in peers:
        pl.semaphore_signal(barrier, inc=1, device_id={"tensor": peer}, device_id_type=MESH)
    pl.semaphore_wait(barrier, len(peers))


def send(source, target, sems, at, peer):
    copy = pltpu.make_async_remote_copy(
        src_ref=source,
        dst_ref=target,
        send_sem=sems.at[0, at],
        recv_sem=sems.at[1, at],
        device_id={"tensor": peer},
        device_id_type=MESH,
    )
    copy.start()
    return copy


def send_dp(source, target, sems, at, peer):
    copy = pltpu.make_async_remote_copy(
        src_ref=source,
        dst_ref=target,
        send_sem=sems.at[0, at],
        recv_sem=sems.at[1, at],
        device_id={"dp": peer},
        device_id_type=MESH,
    )
    copy.start()
    return copy


class Moves:
    def __init__(self, sems):
        self.sems, self.copies = sems, {}

    def start(self, name, source, target):
        copy = pltpu.make_async_copy(source, target, self.sems.at[len(self.copies)])
        copy.start()
        self.copies[name] = copy

    def wait(self, name):
        self.copies[name].wait()


def shard(at, part):
    return pl.ds(pl.multiple_of(at * part, 32), part)


class Spread:
    def __init__(self, where, buffer, sems, part):
        self.me, self.across, self.beside, _ = where
        self.buffer, self.sems, self.part = buffer, sems, part
        self.far, self.near, self.on = {}, {}, {}

    def view(self, owner, lanes):
        return self.buffer.at[shard(owner, self.part), lanes]

    def start(self, k, lanes, source=None):
        block = self.view(self.me, lanes)
        source = block if source is None else source
        self.far[k] = send(source, block, self.sems, 3 * k, self.across)
        self.near[k] = send(source, block, self.sems, 3 * k + 1, self.beside)

    def relay(self, k, lanes):
        self.far[k].wait_recv()
        block = self.view(self.across, lanes)
        self.on[k] = send(block, block, self.sems, 3 * k + 2, self.beside)

    def end(self, k):
        self.near[k].wait_recv()
        self.on[k].wait_recv()

    def finish(self):
        for copies in (self.far, self.near, self.on):
            for copy in copies.values():
                copy.wait_send()


class Reduce:
    def __init__(self, where, part, bufs, sems):
        self.me, self.across, self.beside, self.corner = where
        self.part = part
        self.pair_out, self.pair_in, self.far_out, self.far_in, self.keep = bufs
        self.sems = sems
        self.pair, self.far = {}, {}

    def start(self, k, lanes, term):
        for index, owner in enumerate((self.corner, self.beside)):
            self.pair_out[index, :, lanes] = low(term(owner))
            self.pair[k, index] = send(
                self.pair_out.at[index, :, lanes],
                self.pair_in.at[index, :, lanes],
                self.sems,
                3 * k + index,
                self.beside,
            )
            self.keep[index, :, lanes] = term((self.across, self.me)[index])

    def relay(self, k, lanes, remote=True):
        self.pair[k, 0].wait_recv()
        block = low(self.keep[0, :, lanes] + self.pair_in[0, :, lanes].astype(jnp.float32))
        self.far_out[:, lanes] = block
        if remote:
            self.far[k] = send(
                self.far_out.at[:, lanes], self.far_in.at[:, lanes], self.sems, 3 * k + 2, self.across
            )

    def near_sum(self, k, lanes):
        self.pair[k, 1].wait_recv()
        return self.keep[1, :, lanes] + self.pair_in[1, :, lanes].astype(jnp.float32)

    def end(self, k, lanes):
        total = self.near_sum(k, lanes)
        self.far[k].wait_recv()
        return total + self.far_in[:, lanes].astype(jnp.float32)

    def finish(self):
        for copies in (self.pair, self.far):
            for copy in copies.values():
                copy.wait_send()


class Rows:
    def __init__(self, where, buffer, sems):
        self.me, self.peers = where[0], where[1:]
        self.buffer, self.sems = buffer, sems
        self.copies = {}

    def start(self, k, lanes, first, second):
        self.buffer[self.me, 0:1, lanes] = first
        self.buffer[self.me, 1:2, lanes] = second
        block = self.buffer.at[self.me, :, lanes]
        self.copies[k] = [
            send(block, block, self.sems, 3 * k + index, peer) for index, peer in enumerate(self.peers)
        ]

    def end(self, k, lanes):
        for copy in self.copies[k]:
            copy.wait_recv()
        total = sum(self.buffer[index, :, lanes] for index in range(4))
        return total[0:1], total[1:2]

    def finish(self):
        for copies in self.copies.values():
            for copy in copies:
                copy.wait_send()


class Halving:
    def __init__(self, count, buffer, lanes, arrivals, sems, order, result):
        self.result = result
        self.count, self.buffer, self.lanes = count, buffer, lanes
        self.arrivals, self.sems, self.order = arrivals, sems, order
        self.own = buffer.shape[0] // count
        self.me = lax.axis_index("dp")
        self.bit = {bit: lax.rem(self.me // 2**bit, 2) for bit in order}
        self.phase, self.slot, self.copies, self.sent = 0, 0, [], []

    def rows(self, block):
        return pl.ds(pl.multiple_of(block * self.own, 16), self.own)

    def blocks(self, side):
        bit = self.order[self.phase]
        found = [self.bit[bit] * (1 - 2 * side) * 2**bit + side * 2**bit]
        for done in self.order[: self.phase]:
            found = [block + self.bit[done] * 2**done for block in found]
        for free in self.order[self.phase + 1 :]:
            found = [block + value * 2**free for block in found for value in range(2)]
        return found

    def start(self):
        bit = self.order[self.phase]
        partner = self.me + 2**bit - 2 * 2**bit * self.bit[bit]
        self.copies = []
        for offset, block in enumerate(self.blocks(1)):
            at = self.slot + offset
            self.copies.append(
                send_dp(self.buffer.at[self.rows(block), self.lanes], self.arrivals.at[at], self.sems, at, partner)
            )
        self.sent += self.copies

    def step(self):
        for offset, block in enumerate(self.blocks(0)):
            self.copies[offset].wait_recv()
            total = self.buffer[self.rows(block), self.lanes].astype(jnp.float32) + self.arrivals[
                self.slot + offset
            ].astype(jnp.float32)
            if self.phase + 1 < len(self.order):
                self.buffer[self.rows(block), self.lanes] = low(total)
            else:
                self.result[:, self.lanes] = total
        self.slot += len(self.copies)
        self.phase += 1
        if self.phase < len(self.order):
            self.start()

    def finish(self):
        for copy in self.sent:
            copy.wait_send()


def halving_scratch(count, rows, columns):
    return pltpu.VMEM((count - 1, rows // count, columns), jnp.bfloat16)


def reduce_scratch(part, length):
    return [
        pltpu.VMEM((2, part, length), jnp.bfloat16),
        pltpu.VMEM((2, part, length), jnp.bfloat16),
        pltpu.VMEM((part, length), jnp.bfloat16),
        pltpu.VMEM((part, length), jnp.bfloat16),
        pltpu.VMEM((2, part, length), jnp.float32),
    ]


def copy_sems(count):
    return pltpu.SemaphoreType.DMA((2, count))


def column_sums(rows):
    return jnp.sum(rows, axis=1, keepdims=True)


def row_sums(rows):
    return jnp.sum(rows, axis=0, keepdims=True)


def span_forward(heads, at, lanes, states, proj, cum_ref, col_ref, rec, states_ref):
    scale = HD ** (-0.5)
    after = []
    for head in range(heads):
        query, key, value = (
            proj[(kind * heads + head) * HEAD_ROWS : (kind * heads + head + 1) * HEAD_ROWS, lanes]
            for kind in range(3)
        )
        row = cum_ref[head : head + 1, lanes]
        column = col_ref[lanes, head : head + 1]
        last = row[:, SPAN - 1 : SPAN]
        state = states[head]
        states_ref[at, head] = state
        weights = decay_block(row, column) * mm(key, query, TN)
        out = mm(value, low(weights), NN)
        out = out + mm(low(state), low(query.astype(jnp.float32) * jnp.exp(row)), NN)
        rec[head * HD : (head + 1) * HD, lanes] = out[:HD] * scale
        carried = low(key.astype(jnp.float32) * jnp.exp(last - row))
        after.append(state * jnp.exp(last) + mm(value, carried, NT))
    return after


def conv_chunk(k, chunks, rec, taps, mixed_ref):
    length = chunks * CHUNK
    begin, end = max(k * CHUNK - 128, 0), min((k + 1) * CHUNK + 128, length)
    window, skip = pl.ds(begin, end - begin), k * CHUNK - begin
    masks = edge_masks(length, begin, end)

    def one_group(at, carry):
        rows = pl.ds(pl.multiple_of(at * CONV_ROWS, CONV_ROWS), CONV_ROWS)
        mixed = conv_rows(rec[rows, window], taps[rows, :], masks, False)
        mixed_ref[rows, k * CHUNK : (k + 1) * CHUNK] = low(mixed[:, skip : skip + CHUNK])
        return carry

    lax.fori_loop(0, rec.shape[0] // CONV_ROWS, one_group, 0)


def conv_backward(grad_ref, rec, taps, grec, gtaps):
    masks = edge_masks(rec.shape[1])
    lane = lax.broadcasted_iota(jnp.int32, (BACK_ROWS, 16), 1)
    scale = HD ** (-0.5)

    def one_group(at, carry):
        rows = pl.ds(pl.multiple_of(at * BACK_ROWS, BACK_ROWS), BACK_ROWS)
        grad = grad_ref[rows, :]
        grec[rows, :] = conv_rows(grad, taps[rows, :], masks, True) * scale
        moved = neighbours(rec[rows, :], masks)
        _, _, up_ok, down_ok = masks
        grads = (
            jnp.where(down_ok, shifted(grad, GRID), 0.0),
            grad,
            jnp.where(up_ok, shifted(grad, -GRID), 0.0),
        )
        result = jnp.zeros((BACK_ROWS, 16), jnp.float32)
        for row in range(3):
            for col in range(3):
                one = jnp.sum(moved[col] * grads[row], axis=1, keepdims=True)
                result = jnp.where(lane == 3 * row + col, one, result)
        gtaps[rows, :] = result
        return carry

    lax.fori_loop(0, rec.shape[0] // BACK_ROWS, one_group, 0)


def spans_backward(heads, proj, logit_ref, cum_ref, col_ref, states, grec, staged, rows_ref, gproj):
    part, length = grec.shape
    spans = length // SPAN
    wide_rows = staged.shape[0]
    rows_ref[...] = jnp.zeros_like(rows_ref)
    staged[3 * part :, :] = jnp.zeros((wide_rows - 3 * part, SPAN), jnp.float32)
    key_at = lax.broadcasted_iota(jnp.int32, (SPAN, SPAN), 0)
    query_at = lax.broadcasted_iota(jnp.int32, (SPAN, SPAN), 1)
    later = low(jnp.where(key_at >= query_at, 1.0, 0.0))
    filler = jnp.zeros((HEAD_ROWS - HD, SPAN), jnp.float32)

    def one_span(step, back_states):
        at = spans - 1 - step
        lanes = pl.ds(pl.multiple_of(at * SPAN, SPAN), SPAN)
        after = []
        for head in range(heads):
            query, key, value = (
                proj[(kind * heads + head) * HEAD_ROWS : (kind * heads + head + 1) * HEAD_ROWS, lanes]
                for kind in range(3)
            )
            grad = low(jnp.concatenate([grec[head * HD : (head + 1) * HD, lanes], filler], axis=0))
            row = cum_ref[head : head + 1, lanes]
            column = col_ref[lanes, head : head + 1]
            last = row[:, SPAN - 1 : SPAN]
            state = states[at, head]
            back = back_states[head]
            decay = decay_block(row, column)
            weights = decay * mm(key, query, TN)
            grad_weights = mm(value, grad, TN)
            product = low(grad_weights * weights)
            grad_score = low(grad_weights * decay)
            in_decay = jnp.exp(row)
            out_decay = jnp.exp(last - row)
            query_in = mm(low(state), grad, TN) * in_decay
            key_out = mm(low(back), value, TN) * out_decay
            query_wide = query.astype(jnp.float32)
            key_wide = key.astype(jnp.float32)
            grad_query = mm(key, grad_score, NN) + query_in
            grad_key = mm(query, grad_score, NT) + key_out
            grad_value = mm(grad, low(weights), NT) + mm(low(back), low(key_wide * out_decay), NN)
            for kind, piece in enumerate((grad_query, grad_key, grad_value)):
                staged[kind * part + head * HD : kind * part + (head + 1) * HD, :] = piece[:HD]
            inside = mm(product, later, NN)
            inside = jnp.sum(jnp.where(key_at < query_at, inside, 0.0), axis=0, keepdims=True)
            span_decay = jnp.exp(last)
            across = jnp.sum(back * state, keepdims=True) * span_decay
            rows_ref[0, head : head + 1, :] = jnp.sum(query_wide * query_in, axis=0, keepdims=True)
            rows_ref[1, head : head + 1, :] = jnp.sum(key_wide * key_out, axis=0, keepdims=True)
            rows_ref[2, head : head + 1, :] = inside + across
            after.append(back * span_decay + mm(grad, low(query_wide * in_decay), NT))
        grad_log = (
            running_sum(rows_ref[0], SPAN, reverse=True)
            + running_sum(rows_ref[1], SPAN, exclusive=True)
            + rows_ref[2]
        )
        grad_forget = grad_log / (1.0 + jnp.exp(logit_ref[:, lanes]))
        staged[3 * part : 3 * part + heads, :] = grad_forget[:heads]
        gproj[:wide_rows, lanes] = low(staged[...])
        return tuple(after)

    lax.fori_loop(
        0, spans, one_span, tuple(jnp.zeros((HEAD_ROWS, HEAD_ROWS), jnp.float32) for _ in range(heads))
    )


GELU_SLOPE = math.sqrt(2.0 / math.pi)
GELU_CUBE = 0.044715
X_FIRST, Z_FIRST = (0, 1, 2), (1, 0, 2)


def layer_kernel(
    shard_count, heads, direct,
    x_hbm, cot_hbm, silu_ref, ada_hbm, bias_ref, qkv_hbm, gate_ref, gate_bias_ref, conv_ref, out_w_ref, up_hbm,
    down_hbm, cond_ref, label_ref,
    gtokens_ref, out_ref, gdown_out, gup_out, gqkv_out, gout_out, gclass_ref, gada_ref, gsmall_ref, normed_hbm,
    wback_hbm,
    x_ref, cot_ref, up, down, turned, gmlp, gact, normed, act, gup_rows, gattn,
    attn, after, gafter, mix_ref,
    a_pair_out, a_pair_in, a_far_out, a_far_in, a_keep,
    g_pair_out, g_pair_in, g_far_out, g_far_in, g_keep,
    mod_parts, first_rows, second_rows, third_rows, silu_rows,
    proj, rec, states, logit_ref, stats_ref, cum_ref, col_ref, span_rows, taps, gtaps, mods_ref, gmods, ada_rest,
    parcels, latent_in, mods_out, mods_in, gcond, silu_own, mods_own, label_own,
    down_a, down_b, up_a, up_b, qkv_a, qkv_b, out_a,
    raw_sems, part_sems, gm_sems, a_sems, n_sems, g_sems, t_sems, m_sems, s_sems, first_sems, second_sems,
    third_sems, silu_sems, dp_sems, down_a_sems, down_b_sems, up_a_sems, up_b_sems, qkv_a_sems, qkv_b_sems,
    out_a_sems, move_sems,
):
    part, length = x_ref.shape
    width = 4 * part
    own_width = width // shard_count
    hidden = up.shape[1]
    chunks = length // CHUNK
    lanes = [pl.ds(k * CHUNK, CHUNK) for k in range(chunks)]
    where = places()
    me, across, beside, _ = where
    spot = lax.axis_index("dp")
    own, other = shard(me, part), shard(across, part)
    projected = qkv_hbm.shape[0]
    raw, wide = act, down.at[:WIDE_ROWS, :]
    moves = Moves(move_sems)
    moves.start("ada", ada_hbm.at[:width, :], up)
    moves.start("ada_rest", ada_hbm.at[width:, :], ada_rest)
    moves.start("raw", x_hbm, raw.at[own, :])
    moves.start("qkv", qkv_hbm, wide.at[:projected, :])
    moves.start("cot", cot_hbm, cot_ref)
    moves.start("x", x_hbm, x_ref)
    for rows in (mod_parts, first_rows, second_rows, third_rows, silu_rows, parcels, mods_out):
        rows[...] = jnp.zeros(rows.shape, rows.dtype)
    barrier = pltpu.get_barrier_semaphore()
    for peer in where[1:]:
        pl.semaphore_signal(barrier, inc=1, device_id={"tensor": peer}, device_id_type=MESH)
    for step in range(1, shard_count):
        pl.semaphore_signal(
            barrier, inc=1, device_id={"dp": lax.rem(spot + step, shard_count)}, device_id_type=MESH
        )
    pl.semaphore_wait(barrier, shard_count + 2)

    spread = Spread(where, raw, raw_sems, part)
    gm_spread = Spread(where, gmlp, gm_sems, part)
    spread.start(0, lanes[0], x_hbm.at[:, lanes[0]])
    part_at = lax.broadcasted_iota(jnp.int32, (8, part), 0)
    bias = bias_ref[...].astype(jnp.float32)
    mod_sum = jnp.concatenate([bias, jnp.zeros((8 - bias.shape[0], part), jnp.float32)], axis=0)
    silu_rows_low = silu_ref[...]

    def ada_piece(index):
        if index < 4:
            return up[index * part : (index + 1) * part, :]
        return ada_rest[(index - 4) * part : (index - 3) * part, :]

    moves.wait("ada")
    moves.wait("ada_rest")
    for index in range(6):
        mod_sum = mod_sum + jnp.where(part_at == index, mm(silu_rows_low, ada_piece(index), NT), 0.0)
    mod_parts[me, :, :part] = mod_sum
    part_copies = [
        send(mod_parts.at[me], mod_parts.at[me], part_sems, index, peer) for index, peer in enumerate(where[1:])
    ]
    for k in range(1, chunks):
        spread.start(k, lanes[k], x_hbm.at[:, lanes[k]])
    moves.start("up", up_hbm, up)
    mods_ref[...] = jnp.transpose(mod_parts[me])[:part]
    moves.wait("cot")
    gmlp[own, :] = low(cot_ref[...].astype(jnp.float32) * mods_ref[:, 5:6])
    gm_spread.start(0, lanes[0])
    moves.wait("qkv")
    gate = gate_ref[...].astype(jnp.float32)
    wide[projected:, :] = low(
        jnp.concatenate([gate, jnp.zeros((WIDE_ROWS - projected - heads, width), jnp.float32)], axis=0)
    )
    gup_rows[:, :WIDE_ROWS] = jnp.transpose(wide[...])
    moves.start("wback_out", gup_rows.at[:, :WIDE_ROWS], wback_hbm)
    gate_at = lax.broadcasted_iota(jnp.int32, (8, 1), 0)
    gate_bias = jnp.zeros((8, 1), jnp.float32)
    for head in range(heads):
        gate_bias = gate_bias + jnp.where(gate_at == head, gate_bias_ref[0:1, head : head + 1].astype(jnp.float32), 0.0)
    conv = [conv_ref[index].astype(jnp.float32) for index in range(3)]
    taps[...] = jnp.transpose(jnp.concatenate(conv + [jnp.zeros((7, part), jnp.float32)], axis=0))
    stats_ref[2:, :] = jnp.zeros((6, length), jnp.float32)
    filler = jnp.zeros((HEAD_ROWS - HD, CHUNK), jnp.float32)
    carried = [jnp.zeros((HEAD_ROWS, HEAD_ROWS), jnp.float32) for _ in range(heads)]

    def project_chunk(k, carried):
        spread.end(k)
        blocks = [raw[index * part : (index + 1) * part, lanes[k]].astype(jnp.float32) for index in range(4)]
        mean = sum(row_sums(block) for block in blocks) / width
        square = sum(row_sums(block * block) for block in blocks) / width
        inv_std = lax.rsqrt(square - mean * mean + norm_eps)
        stats_ref[0:1, lanes[k]] = mean
        stats_ref[1:2, lanes[k]] = inv_std
        for index in range(4):
            unit = (blocks[index] - mean) * inv_std
            value = unit * (1.0 + columns[index][:, 1:2]) + columns[index][:, 0:1]
            gattn[index * part : (index + 1) * part, lanes[k]] = low(value)
        product = mm(wide[...], gattn[:, lanes[k]], NN)
        for index in range(3 * heads):
            piece = jnp.concatenate([product[index * HD : (index + 1) * HD], filler], axis=0)
            proj[index * HEAD_ROWS : (index + 1) * HEAD_ROWS, lanes[k]] = low(piece)
        logit = product[projected : projected + 8] + gate_bias
        logit_ref[:, lanes[k]] = logit
        cum = running_sum(log_sigmoid(logit), SPAN)
        cum_ref[:, lanes[k]] = cum
        col_ref[lanes[k], :] = jnp.transpose(cum)
        return span_forward(heads, k, lanes[k], carried, proj, cum_ref, col_ref, rec, states)

    gate_one, scale_two, shift_two = mods_ref[:, 2:3], mods_ref[:, 4:5], mods_ref[:, 3:4]

    attn_sum = Reduce(where, part, (a_pair_out, a_pair_in, a_far_out, a_far_in, a_keep), a_sems)
    mlp_sum = Reduce(where, part, (a_pair_out, a_pair_in, a_far_out, a_far_in, a_keep), m_sems)
    grad_sum = Reduce(where, part, (g_pair_out, g_pair_in, g_far_out, g_far_in, g_keep), g_sems)
    last_sum = Reduce(where, part, (g_pair_out, g_pair_in, g_far_out, g_far_in, g_keep), s_sems)
    norm_spread = Spread(where, normed, n_sems, part)
    grad_spread = Spread(where, gattn, t_sems, part)
    moments = Rows(where, first_rows, first_sems)
    means = Rows(where, second_rows, second_sems)
    last_means = Rows(where, third_rows, third_sems)
    if direct:
        totals = {}
        for name, buffer, result, (first, second), sems in (
            ("down", up, gdown_out, (down_a, down_b), (down_a_sems, down_b_sems)),
            ("up", down, gup_out, (up_a, up_b), (up_a_sems, up_b_sems)),
            ("qkv", act, gqkv_out, (qkv_a, qkv_b), (qkv_a_sems, qkv_b_sems)),
        ):
            cut = first.shape[2]
            totals[name + "_a"] = Halving(shard_count, buffer, pl.ds(0, cut), first, sems[0], X_FIRST, result)
            totals[name + "_b"] = Halving(
                shard_count, buffer, pl.ds(cut, second.shape[2]), second, sems[1], Z_FIRST, result
            )
        totals["out"] = Halving(
            shard_count, gup_rows, pl.ds(0, out_a.shape[2]), out_a, out_a_sems, X_FIRST, gout_out
        )

    def begin(*names):
        if direct:
            for name in names:
                totals[name].start()

    def advance(*names):
        if direct:
            for name in names:
                totals[name].step()

    gmods[...] = jnp.zeros_like(gmods)
    gmix = gtokens_ref

    def attn_start(k):
        mixed = mix_ref[:, lanes[k]]
        attn_sum.start(k, lanes[k], lambda owner: mm(gup_rows[shard(owner, part), :part], mixed, NN))

    def attn_end(k):
        value = attn_sum.end(k, lanes[k])
        attn[:, lanes[k]] = value
        total = x_ref[:, lanes[k]].astype(jnp.float32) + gate_one * value
        after[:, lanes[k]] = total
        moments.start(k, lanes[k], row_sums(total), row_sums(total * total))

    inverse, average = [None] * chunks, [None] * chunks

    def unit_two(k):
        return (after[:, lanes[k]] - average[k]) * inverse[k]

    def norm_chunk(k):
        total, squares = moments.end(k, lanes[k])
        average[k] = total / width
        inverse[k] = lax.rsqrt(squares / width - average[k] * average[k] + norm_eps)
        normed[own, lanes[k]] = low(unit_two(k) * (1.0 + scale_two) + shift_two)
        norm_spread.start(k, lanes[k])

    def grad_act_chunk(k):
        gact[...] = mm(down[...], gmlp[:, lanes[k]], NN)

    def hidden_chunk(k):
        norm_spread.end(k)
        block = normed[:, lanes[k]]

        def one_block(at, carry):
            rows = pl.ds(pl.multiple_of(at * part, 32), part)
            value = mm(turned[rows, :], block, NN)
            square = value * value
            bend = jnp.tanh(GELU_SLOPE * value * (1.0 + GELU_CUBE * square))
            half = 0.5 * (1.0 + bend)
            act[rows, lanes[k]] = low(value * half)
            slope = half + 0.5 * value * (1.0 - bend * bend) * GELU_SLOPE * (1.0 + 3.0 * GELU_CUBE * square)
            gup_rows[rows, lanes[k]] = low(gact[rows, :] * slope)
            return carry

        lax.fori_loop(0, hidden // part, one_block, 0)

    def grad_start(k):
        block = gup_rows[:, lanes[k]]
        grad_sum.start(k, lanes[k], lambda owner: mm(up[shard(owner, part), :], block, NN))

    def grad_end(k):
        grad = grad_sum.end(k, lanes[k])
        rows = unit_two(k)
        gmods[:, 3:4] += column_sums(grad)
        gmods[:, 4:5] += column_sums(grad * rows)
        scaled = grad * (1.0 + scale_two)
        gafter[:, lanes[k]] = scaled
        means.start(k, lanes[k], row_sums(scaled), row_sums(scaled * rows))

    def after_chunk(k):
        total, along = means.end(k, lanes[k])
        scaled = gafter[:, lanes[k]]
        back = inverse[k] * (scaled - total / width - unit_two(k) * (along / width))
        grad = cot_ref[:, lanes[k]].astype(jnp.float32) + back
        gafter[:, lanes[k]] = grad
        gattn[own, lanes[k]] = low(grad * gate_one)
        grad_spread.start(k, lanes[k])
        gmods[:, 2:3] += column_sums(grad * attn[:, lanes[k]])

    def mixed_chunk(k):
        grad_spread.end(k)
        gmix[:, lanes[k]] = mm(out_w_ref[...], gattn[:, lanes[k]], NN)

    def weight_grad(target, columns, left, right, at, pieces):
        rows = target.shape[0] // pieces
        rows = slice(at * rows, (at + 1) * rows)
        target[rows, columns] = low(mm(left[rows, :], right[...], NT))

    def mlp_start(k):
        block = act[:, lanes[k]]
        mlp_sum.start(k, lanes[k], lambda owner: mm(turned[shard(owner, part), :], block, NN))

    def outputs(k):
        mlp = mlp_sum.end(k, lanes[k])
        out_ref[:, lanes[k]] = low(after[:, lanes[k]] + mods_ref[:, 5:6] * mlp)
        gmods[:, 5:6] += column_sums(cot_ref[:, lanes[k]].astype(jnp.float32) * mlp)

    every_column = slice(None)
    spread.relay(0, lanes[0])
    moves.wait("up")
    turned[...] = jnp.transpose(up[...])
    moves.wait("wback_out")
    gup_rows[:, :part] = jnp.transpose(out_w_ref[...])
    moves.wait("raw")
    for copy in part_copies:
        copy.wait_recv()
    columns = [jnp.transpose(mod_parts[index])[:part] for index in range(4)]
    spread.relay(1, lanes[1])
    carried = project_chunk(0, carried)
    spread.relay(2, lanes[2])
    carried = project_chunk(1, carried)
    conv_chunk(0, chunks, rec, taps, mix_ref)
    attn_start(0)
    spread.relay(3, lanes[3])
    attn_sum.relay(0, lanes[0])
    gm_spread.start(1, lanes[1])
    carried = project_chunk(2, carried)
    conv_chunk(1, chunks, rec, taps, mix_ref)
    attn_start(1)
    moves.wait("x")
    gm_spread.relay(0, lanes[0])
    attn_sum.relay(1, lanes[1])
    gm_spread.start(2, lanes[2])
    attn_end(0)
    project_chunk(3, carried)
    spread.finish()
    moves.start("normed_out", gattn, normed_hbm)
    moves.start("down", down_hbm, down)
    conv_chunk(2, chunks, rec, taps, mix_ref)
    attn_start(2)
    conv_chunk(3, chunks, rec, taps, mix_ref)
    attn_sum.relay(2, lanes[2])
    attn_start(3)
    gm_spread.relay(1, lanes[1])
    moves.wait("down")
    moves.wait("normed_out")
    attn_end(1)
    norm_chunk(0)
    attn_sum.relay(3, lanes[3])
    gm_spread.start(3, lanes[3])
    gm_spread.relay(2, lanes[2])
    gm_spread.end(0)
    grad_act_chunk(0)
    attn_end(2)
    norm_chunk(1)
    norm_spread.relay(0, lanes[0])
    hidden_chunk(0)
    attn_end(3)
    norm_chunk(2)
    grad_start(0)
    norm_spread.relay(1, lanes[1])
    norm_chunk(3)
    gm_spread.relay(3, lanes[3])
    grad_sum.relay(0, lanes[0])
    gm_spread.end(1)
    grad_act_chunk(1)
    hidden_chunk(1)
    grad_start(1)
    norm_spread.relay(2, lanes[2])
    grad_sum.relay(1, lanes[1])
    gm_spread.end(2)
    grad_act_chunk(2)
    hidden_chunk(2)
    grad_start(2)
    norm_spread.relay(3, lanes[3])
    grad_end(0)
    grad_sum.relay(2, lanes[2])
    gm_spread.end(3)
    grad_act_chunk(3)
    hidden_chunk(3)
    grad_start(3)
    weight_grad(up, every_column, gmlp, act, 0, 2)
    after_chunk(0)
    grad_sum.relay(3, lanes[3])
    weight_grad(up, every_column, gmlp, act, 1, 2)
    begin("down_a", "down_b")
    if not direct:
        moves.start("gdown", up, gdown_out)
    grad_end(1)
    turned[...] = jnp.transpose(down[...])
    grad_spread.relay(0, lanes[0])
    after_chunk(1)
    grad_end(2)
    weight_grad(down, every_column, normed, gup_rows, 0, 2)
    after_chunk(2)
    grad_spread.relay(1, lanes[1])
    mixed_chunk(0)
    grad_end(3)
    weight_grad(down, every_column, normed, gup_rows, 1, 2)
    begin("up_a", "up_b")
    if not direct:
        moves.start("gup", down, gup_out)
    after_chunk(3)
    attn_sum.finish()
    grad_spread.relay(2, lanes[2])
    mixed_chunk(1)
    mlp_start(0)
    mlp_start(1)
    mlp_sum.relay(0, lanes[0])
    mixed_chunk(2)
    mlp_start(2)
    mlp_sum.relay(1, lanes[1])
    grad_spread.relay(3, lanes[3])
    mlp_start(3)
    mlp_sum.relay(2, lanes[2])
    norm_spread.finish()
    moves.start("normed", normed_hbm, normed)
    mixed_chunk(3)
    advance("down_b")
    weight_grad(gup_rows, slice(0, part), gattn, mix_ref, 0, 1)
    begin("out")
    mlp_sum.relay(3, lanes[3])
    moves.start("wback", wback_hbm, turned.at[:, :WIDE_ROWS])
    if not direct:
        moves.start("gout", gup_rows.at[:, : out_a.shape[2]], gout_out)

    conv_backward(gmix, rec, taps, attn, gtaps)
    grad_spread.finish()
    grad_sum.finish()
    advance("down_a", "up_b")
    staged = gact.at[:WIDE_ROWS, :]
    spans_backward(heads, proj, logit_ref, cum_ref, col_ref, states, attn, staged, span_rows, gattn)
    advance("up_a")
    gproj = gattn.at[:WIDE_ROWS, :]

    def last_start(k):
        block = gproj[:, lanes[k]]
        last_sum.start(k, lanes[k], lambda owner: mm(turned[shard(owner, part), :WIDE_ROWS], block, NN))

    def unit_one(k):
        return (x_ref[:, lanes[k]].astype(jnp.float32) - stats_ref[0:1, lanes[k]]) * stats_ref[1:2, lanes[k]]

    def last_end(k):
        grad = last_sum.end(k, lanes[k])
        unit = unit_one(k)
        gmods[:, 0:1] += column_sums(grad)
        gmods[:, 1:2] += column_sums(grad * unit)
        scaled = grad * (1.0 + mods_ref[:, 1:2])
        gtokens_ref[:, lanes[k]] = scaled
        last_means.start(k, lanes[k], row_sums(scaled), row_sums(scaled * unit))

    def tokens(k):
        total, along = last_means.end(k, lanes[k])
        back = gtokens_ref[:, lanes[k]] - total / width - unit_one(k) * (along / width)
        gtokens_ref[:, lanes[k]] = gafter[:, lanes[k]] + stats_ref[1:2, lanes[k]] * back

    moves.wait("wback")
    last_start(0)
    last_start(1)
    last_sum.relay(0, lanes[0])
    moves.wait("normed")
    for piece in range(2):
        weight_grad(act, slice(0, WIDE_ROWS), normed, gproj, piece, 2)
    begin("qkv_a", "qkv_b")
    if not direct:
        moves.start("gqkv", act.at[:, :WIDE_ROWS], gqkv_out)
    advance("down_a")
    last_start(2)
    last_sum.relay(1, lanes[1])
    last_start(3)
    last_sum.relay(2, lanes[2])
    moves.start("ada_again", ada_hbm.at[:width, :], turned)
    advance("down_b")
    last_sum.relay(3, lanes[3])
    for k in range(chunks):
        outputs(k)
    advance("up_a", "down_a")
    last_end(0)
    last_end(1)
    tokens(0)
    advance("out")
    last_end(2)
    tokens(1)
    last_end(3)
    advance("up_b", "down_b", "qkv_b")

    mod_rows = jnp.transpose(gmods[...])
    low_rows = low(mod_rows)
    row_at = lax.broadcasted_iota(jnp.int32, (8, width), 0)
    moves.wait("ada_again")
    product = jnp.zeros((8, width), jnp.float32)
    for index in range(6):
        piece = turned[index * part : (index + 1) * part, :] if index < 4 else ada_piece(index)
        product = product + jnp.where(row_at == index, mm(low_rows, piece, NN), 0.0)
    silu_rows[me, 0:1, :] = row_sums(product)
    silu_copies = [
        send(silu_rows.at[me], silu_rows.at[me], silu_sems, index, peer) for index, peer in enumerate(where[1:])
    ]
    tap_rows = jnp.transpose(gtaps[...])
    forget = gattn[3 * part : WIDE_ROWS, :].astype(jnp.float32)[:8]
    forget = jnp.transpose(jnp.broadcast_to(column_sums(forget), (8, 128)))[0:1]
    small = jnp.concatenate([mod_rows[:6], tap_rows[:9], jnp.zeros((1, part), jnp.float32)], axis=0)
    mods_out[:, :part] = low(small)
    mods_out[:, part : part + 8] = low(jnp.broadcast_to(forget, (16, 8)))
    mods_in[spot] = mods_out[...]
    dp_copies = []
    for step in range(1, shard_count):
        peer = lax.rem(spot + step, shard_count)
        dp_copies.append(send_dp(mods_out, mods_in.at[spot], dp_sems, step, peer))
    tokens(2)
    tokens(3)
    advance("up_a", "out")
    for copy in silu_copies:
        copy.wait_recv()
    grad_silu = sum(silu_rows[index, 0:1, :] for index in range(4))
    cond = cond_ref[0:1, :]
    sigmoid = 1.0 / (1.0 + jnp.exp(-cond))
    grad_cond = grad_silu * (sigmoid * (1.0 + cond * (1.0 - sigmoid)))
    silu = low(cond * sigmoid).astype(jnp.float32)
    for index in range(shard_count):
        columns = slice(index * own_width, (index + 1) * own_width)
        parcels[index, 0:1, :own_width] = grad_cond[:, columns]
        parcels[index, 1:2, :own_width] = silu[:, columns]
        parcels[index, 2:3, :] = jnp.broadcast_to(label_ref[...], (1, parcels.shape[2]))
    latent_in[spot] = parcels[spot]
    for step in range(1, shard_count):
        peer = lax.rem(spot + step, shard_count)
        dp_copies.append(send_dp(parcels.at[peer], latent_in.at[spot], dp_sems, shard_count + step, peer))
    advance("qkv_a", "up_b", "out", "qkv_b")
    for copy in dp_copies:
        copy.wait_recv()
    small_sum = jnp.zeros(mods_out.shape, jnp.float32)
    for index in range(shard_count):
        arrived = mods_in[index].astype(jnp.float32)
        small_sum = small_sum + arrived
        for row in range(6):
            mods_own[row, index : index + 1, :] = arrived[row : row + 1, :part]
        gcond[index : index + 1, :] = latent_in[index, 0:1, :own_width]
        silu_own[index : index + 1, :] = latent_in[index, 1:2, :own_width]
        label_own[index : index + 1, :] = latent_in[index, 2:3, :128]
    gsmall_ref[...] = small_sum
    class_at = lax.broadcasted_iota(jnp.int32, (shard_count, NCLASS), 1).astype(jnp.float32)
    onehot = jnp.where(label_own[:, 0:1] == class_at, 1.0, 0.0)
    gclass_ref[...] = lax.dot_general(
        gcond[...], onehot, TN, precision=TOP_PRECISION, preferred_element_type=jnp.float32
    )
    for row in range(6):
        gada_ref[row] = mm(low(silu_own[...]), low(mods_own[row]), TN)
    advance("qkv_a", "qkv_b", "qkv_a")
    if direct:
        for total in totals.values():
            total.finish()
    else:
        for name in ("gdown", "gup", "gqkv", "gout"):
            moves.wait(name)
    for copy in part_copies + dp_copies + silu_copies:
        copy.wait_send()
    for group in (gm_spread, mlp_sum, last_sum, moments, means, last_means):
        group.finish()


def layer(
    x, cot, silu, ada, bias, qkv, gate, gate_bias, conv, out_w, up, down, cond, label, shard_count, heads, direct
):
    part, length = x.shape
    width = 4 * part
    hidden = up.shape[1]
    own = width // shard_count
    chunks = length // CHUNK
    spans = length // SPAN
    padded = part + -part % 128
    own_padded = own + -own % 128
    proj_rows = 3 * heads * HEAD_ROWS
    shape = jax.ShapeDtypeStruct
    vmem = pltpu.VMEM
    bf16, f32 = jnp.bfloat16, jnp.float32
    grad_rows, grad_type, grad_spec = (own, f32, VMEM_SPEC) if direct else (width, bf16, ANY_SPEC)
    arrivals = shard_count if direct else 2
    arrival_rows = width if direct else 32
    cuts = (768, hidden - 768, 768, hidden - 768, 512, WIDE_ROWS - 512, padded)
    return pl.pallas_call(
        functools.partial(layer_kernel, shard_count, heads, direct),
        out_shape=(
            shape((part, length), f32),
            shape((part, length), bf16),
            shape((grad_rows, hidden), grad_type),
            shape((grad_rows, hidden), grad_type),
            shape((grad_rows, WIDE_ROWS), grad_type),
            shape((grad_rows, padded), grad_type),
            shape((own, NCLASS), f32),
            shape((6, own, part), f32),
            shape((16, padded), f32),
            shape((width, length), bf16),
            shape((width, WIDE_ROWS), bf16),
        ),
        in_specs=[
            ANY_SPEC, ANY_SPEC, VMEM_SPEC, ANY_SPEC, VMEM_SPEC, ANY_SPEC, VMEM_SPEC, VMEM_SPEC, VMEM_SPEC, VMEM_SPEC,
            ANY_SPEC, ANY_SPEC, VMEM_SPEC, VMEM_SPEC,
        ],
        out_specs=[VMEM_SPEC, VMEM_SPEC] + [grad_spec] * 4 + [VMEM_SPEC] * 3 + [ANY_SPEC] * 2,
        scratch_shapes=[
            vmem((part, length), bf16),
            vmem((part, length), bf16),
            vmem((width, hidden), bf16),
            vmem((hidden, width), bf16),
            vmem((hidden, width), bf16),
            vmem((width, length), bf16),
            vmem((hidden, CHUNK), f32),
            vmem((width, length), bf16),
            vmem((hidden, length), bf16),
            vmem((hidden, length), bf16),
            vmem((width, length), bf16),
            *[vmem((part, length), f32)] * 3,
            vmem((part, length), bf16),
            *reduce_scratch(part, length),
            *reduce_scratch(part, length),
            vmem((4, 8, padded), f32),
            *[vmem((4, 8, length), f32)] * 3,
            vmem((4, 8, width), f32),
            vmem((proj_rows, length), bf16),
            vmem((part, length), f32),
            vmem((spans, heads, HEAD_ROWS, HEAD_ROWS), f32),
            vmem((8, length), f32),
            vmem((8, length), f32),
            vmem((8, length), f32),
            vmem((length, 8), f32),
            vmem((3, 8, SPAN), f32),
            vmem((part, 16), f32),
            vmem((part, 16), f32),
            vmem((part, 8), f32),
            vmem((part, 8), f32),
            vmem((ada.shape[0] - width, width), bf16),
            vmem((shard_count, 8, own_padded), f32),
            vmem((shard_count, 8, own_padded), f32),
            vmem((16, padded), bf16),
            vmem((shard_count, 16, padded), bf16),
            vmem((shard_count, own), f32),
            vmem((shard_count, own), f32),
            vmem((6, shard_count, part), f32),
            vmem((shard_count, 128), f32),
            *[halving_scratch(arrivals, arrival_rows, cut) for cut in cuts],
            copy_sems(3 * chunks),
            copy_sems(3),
            *[copy_sems(3 * chunks)] * 10,
            copy_sems(3),
            copy_sems(2 * shard_count),
            *[copy_sems(shard_count)] * 7,
            pltpu.SemaphoreType.DMA((20,)),
        ],
        compiler_params=pltpu.CompilerParams(
            collective_id=1, has_side_effects=True, vmem_limit_bytes=VMEM_LIMIT
        ),
        cost_estimate=work_for(180),
        name="layer",
    )(x, cot, silu, ada, bias, qkv, gate, gate_bias, conv, out_w, up, down, cond, label)


def finish_kernel(
    heads, tokens_ref, out_ref, class_ref, ada_ref, down_ref, up_ref, qkv_ref, out_w_ref, small_ref,
    tokens_to, out_to, class_to, ada_to, down_to, up_to, qkv_to, gate_to, out_w_to, ada_b_to, gate_b_to, conv_to,
):
    pairs = (
        (tokens_ref, tokens_to), (out_ref, out_to), (class_ref, class_to), (ada_ref, ada_to), (down_ref, down_to),
        (up_ref, up_to),
    )
    for source, target in pairs:
        target[...] = source[...]
    part = out_w_to.shape[1]
    for kind in range(3):
        qkv_to[kind] = qkv_ref[:, kind * part : (kind + 1) * part]
    gate_to[...] = jnp.transpose(qkv_ref[:, 3 * part : 3 * part + 8])[:heads]
    out_w_to[...] = out_w_ref[:, :part]
    ada_b_to[...] = small_ref[:6, :part]
    gate_b_to[...] = small_ref[15:16, part : part + heads]
    for row in range(3):
        conv_to[row] = small_ref[6 + 3 * row : 9 + 3 * row, :part]


def finish(heads, part, tokens, out, grad_class, grad_ada, grad_down, grad_up, grad_wide, grad_out_w, small):
    own = grad_wide.shape[0]
    shape = jax.ShapeDtypeStruct
    f32 = jnp.float32
    whole = (tokens, out, grad_class, grad_ada, grad_down, grad_up)
    return pl.pallas_call(
        functools.partial(finish_kernel, heads),
        out_shape=(
            *[shape(array.shape, array.dtype) for array in whole],
            shape((3, own, part), f32),
            shape((heads, own), f32),
            shape((own, part), f32),
            shape((6, part), f32),
            shape((1, heads), f32),
            shape((3, 3, part), f32),
        ),
        in_specs=[VMEM_SPEC] * 9,
        out_specs=[VMEM_SPEC] * 12,
        compiler_params=pltpu.CompilerParams(vmem_limit_bytes=VMEM_LIMIT),
        cost_estimate=work_for(5),
        name="finish",
    )(*whole, grad_wide, grad_out_w, small)


def shards(
    latent_tokens,
    timesteps,
    labels,
    class_table,
    ada_weight,
    ada_bias,
    query_key_value_weight,
    gate_weight,
    gate_bias,
    conv_weight,
    out_weight,
    up_weight,
    down_weight,
    cotangent,
):
    part = latent_tokens.shape[2]
    heads = gate_weight.shape[1]
    shard_count = lax.psum(1, "dp")
    own_width = MODEL_DIM // shard_count
    x = latent_tokens[0].T
    cot = cotangent[0].T
    qkv = jnp.transpose(query_key_value_weight, (1, 2, 0)).reshape(3 * part, MODEL_DIM)
    ada = jnp.transpose(ada_weight, (1, 2, 0)).reshape(6 * part, MODEL_DIM)
    cond = lax.dynamic_slice_in_dim(class_table, labels[0], 1, axis=0).astype(jnp.float32) + embed_time(
        timesteps, MODEL_DIM
    )
    silu = jnp.broadcast_to(low(jax.nn.silu(cond)), (8, MODEL_DIM))
    direct = shard_count == 8 and own_width % 16 == 0
    grad_tokens, layer_out, grad_down, grad_up, grad_wide, grad_out_w, grad_class, grad_ada_w, small, _, _ = layer(
        x, cot, silu, ada, ada_bias, qkv, gate_weight.T, gate_bias[None], conv_weight, out_weight, up_weight,
        down_weight, cond, labels.astype(jnp.float32)[None], shard_count, heads, direct,
    )
    if not direct:
        grad_down, grad_up, grad_wide, grad_out_w = (
            lax.psum_scatter(partial, "dp", scatter_dimension=0, tiled=True).astype(jnp.float32)
            for partial in (grad_down, grad_up, grad_wide, grad_out_w)
        )
    (
        grad_tokens, layer_out, grad_class, grad_ada_w, grad_down, grad_up, grad_qkv, grad_gate_w, grad_out_w,
        grad_ada_b, grad_gate_b, grad_conv,
    ) = finish(
        heads, part, grad_tokens, layer_out, grad_class, grad_ada_w, grad_down, grad_up, grad_wide, grad_out_w, small
    )
    return (
        layer_out.T[None],
        grad_tokens.T[None],
        grad_class.T,
        jnp.transpose(grad_ada_w, (1, 0, 2)),
        grad_ada_b,
        jnp.transpose(grad_qkv, (1, 0, 2)),
        grad_gate_w.T,
        grad_gate_b[0],
        grad_conv,
        grad_out_w.T,
        grad_up,
        grad_down.T,
    )


def solution(mesh):
    in_specs = (
        P("dp", None, "tensor"),
        P("dp"),
        P("dp"),
        P(),
        P(None, None, "tensor"),
        P(None, "tensor"),
        P(None, None, "tensor"),
        P(None, "tensor"),
        P("tensor"),
        P(None, None, "tensor"),
        P("tensor", None),
        P(None, "tensor"),
        P("tensor", None),
        P("dp", None, "tensor"),
    )
    out_specs = (
        P("dp", None, "tensor"),
        P("dp", None, "tensor"),
        P(None, "dp"),
        P("dp", None, "tensor"),
        P(None, "tensor"),
        P("dp", None, "tensor"),
        P("dp", "tensor"),
        P("tensor"),
        P(None, None, "tensor"),
        P("tensor", "dp"),
        P("dp", "tensor"),
        P("tensor", "dp"),
    )
    return jax.shard_map(shards, mesh=mesh, in_specs=in_specs, out_specs=out_specs, check_vma=False)
```

```python
import functools
import math

import jax
import jax.numpy as jnp
from jax import lax
from jax.experimental import pallas as pl
from jax.experimental.pallas import tpu as pltpu
from jax.sharding import PartitionSpec as P

MODEL_DIM = 1152
HD = 72
HEAD_ROWS = 80
CONV_ROWS = 144
BACK_ROWS = 96
NCLASS = 1000
GRID = 32


TOP_PRECISION = lax.Precision.HIGHEST
norm_eps = 1e-06


def embed_time(time_steps, model_width):
    half_width = model_width // 2
    frequency = jnp.exp(-math.log(10000.0) * jnp.arange(half_width, dtype=jnp.float32) / half_width)
    angles = time_steps.astype(jnp.float32)[:, None] * frequency[None, :]
    return jnp.concatenate([jnp.cos(angles), jnp.sin(angles)], axis=1)


SPAN = 256

TN = (((0,), (0,)), ((), ()))
NT = (((1,), (1,)), ((), ()))
NN = (((1,), (0,)), ((), ()))


def mm(left, right, form):
    return lax.dot_general(left, right, form, preferred_element_type=jnp.float32)


def low(values):
    return values.astype(jnp.bfloat16)


def shifted(rows, offset):
    length = rows.shape[1]
    return pltpu.roll(rows, (-offset) % length, 1)


def edge_masks(length, begin=0, end=None):
    end = length if end is None else end
    token = lax.broadcasted_iota(jnp.int32, (1, end - begin), 1) + begin
    column = lax.rem(token, GRID)
    return column > 0, column < GRID - 1, token >= GRID, token < length - GRID


def neighbours(rows, masks):
    left_ok, right_ok, _, _ = masks
    return (
        jnp.where(left_ok, shifted(rows, -1), 0.0),
        rows,
        jnp.where(right_ok, shifted(rows, 1), 0.0),
    )


def running_sum(rows, span, reverse=False, exclusive=False):
    length = rows.shape[1]
    place = lax.rem(lax.broadcasted_iota(jnp.int32, (1, length), 1), span)
    total = rows
    step = 1
    if exclusive:
        total = (
            jnp.where(place < span - 1, shifted(total, 1), 0.0)
            if reverse
            else jnp.where(place >= 1, shifted(total, -1), 0.0)
        )
    while step < span:
        if reverse:
            total = total + jnp.where(place < span - step, shifted(total, step), 0.0)
        else:
            total = total + jnp.where(place >= step, shifted(total, -step), 0.0)
        step *= 2
    return total


def log_sigmoid(logit):
    return jnp.minimum(logit, 0.0) - jnp.log(1.0 + jnp.exp(-jnp.abs(logit)))


def conv_rows(rows, taps, masks, adjoint):
    _, _, up_ok, down_ok = masks
    left, middle, right = neighbours(rows, masks)
    parts = []
    for row in range(3):
        if adjoint:
            weights = [taps[:, 3 * (2 - row) + 2 - col : 3 * (2 - row) + 3 - col] for col in range(3)]
        else:
            weights = [taps[:, 3 * row + col : 3 * row + col + 1] for col in range(3)]
        parts.append(left * weights[0] + middle * weights[1] + right * weights[2])
    above = jnp.where(up_ok, shifted(parts[0], -GRID), 0.0)
    below = jnp.where(down_ok, shifted(parts[2], GRID), 0.0)
    return above + parts[1] + below


def decay_block(row, column):
    span = row.shape[1]
    key_at = lax.broadcasted_iota(jnp.int32, (span, span), 0)
    query_at = lax.broadcasted_iota(jnp.int32, (span, span), 1)
    return jnp.where(query_at >= key_at, jnp.exp(jnp.minimum(row - column, 0.0)), 0.0)


MESH = pl.DeviceIdType.MESH
CHUNK = 256
VMEM_LIMIT = 63 * 2**20
VMEM_SPEC = pl.BlockSpec(memory_space=pltpu.VMEM)
ANY_SPEC = pl.BlockSpec(memory_space=pl.ANY)
WIDE_ROWS = 896


def work_for(microseconds):
    return pl.CostEstimate(flops=int(microseconds * 1e9), bytes_accessed=0, transcendentals=0)


def places():
    me = lax.axis_index("tensor")
    across = lax.rem(me + 2, 4)
    beside = me + 1 - 2 * lax.rem(me, 2)
    corner = lax.rem(beside + 2, 4)
    return me, across, beside, corner


def greet(peers):
    barrier = pltpu.get_barrier_semaphore()
    for peer in peers:
        pl.semaphore_signal(barrier, inc=1, device_id={"tensor": peer}, device_id_type=MESH)
    pl.semaphore_wait(barrier, len(peers))


def send(source, target, sems, at, peer):
    copy = pltpu.make_async_remote_copy(
        src_ref=source,
        dst_ref=target,
        send_sem=sems.at[0, at],
        recv_sem=sems.at[1, at],
        device_id={"tensor": peer},
        device_id_type=MESH,
    )
    copy.start()
    return copy


def send_dp(source, target, sems, at, peer):
    copy = pltpu.make_async_remote_copy(
        src_ref=source,
        dst_ref=target,
        send_sem=sems.at[0, at],
        recv_sem=sems.at[1, at],
        device_id={"dp": peer},
        device_id_type=MESH,
    )
    copy.start()
    return copy


class Moves:
    def __init__(self, sems):
        self.sems, self.copies = sems, {}

    def start(self, name, source, target):
        copy = pltpu.make_async_copy(source, target, self.sems.at[len(self.copies)])
        copy.start()
        self.copies[name] = copy

    def wait(self, name):
        self.copies[name].wait()


def shard(at, part):
    return pl.ds(pl.multiple_of(at * part, 32), part)


class Spread:
    def __init__(self, where, buffer, sems, part):
        self.me, self.across, self.beside, _ = where
        self.buffer, self.sems, self.part = buffer, sems, part
        self.far, self.near, self.on = {}, {}, {}

    def view(self, owner, lanes):
        return self.buffer.at[shard(owner, self.part), lanes]

    def start(self, k, lanes, source=None):
        block = self.view(self.me, lanes)
        source = block if source is None else source
        self.far[k] = send(source, block, self.sems, 3 * k, self.across)
        self.near[k] = send(source, block, self.sems, 3 * k + 1, self.beside)

    def relay(self, k, lanes):
        self.far[k].wait_recv()
        block = self.view(self.across, lanes)
        self.on[k] = send(block, block, self.sems, 3 * k + 2, self.beside)

    def end(self, k):
        self.near[k].wait_recv()
        self.on[k].wait_recv()

    def finish(self):
        for copies in (self.far, self.near, self.on):
            for copy in copies.values():
                copy.wait_send()


class Reduce:
    def __init__(self, where, part, bufs, sems):
        self.me, self.across, self.beside, self.corner = where
        self.part = part
        self.pair_out, self.pair_in, self.far_out, self.far_in, self.keep = bufs
        self.sems = sems
        self.pair, self.far = {}, {}

    def start(self, k, lanes, term):
        for index, owner in enumerate((self.corner, self.beside)):
            self.pair_out[index, :, lanes] = low(term(owner))
            self.pair[k, index] = send(
                self.pair_out.at[index, :, lanes],
                self.pair_in.at[index, :, lanes],
                self.sems,
                3 * k + index,
                self.beside,
            )
            self.keep[index, :, lanes] = term((self.across, self.me)[index])

    def relay(self, k, lanes, remote=True):
        self.pair[k, 0].wait_recv()
        block = low(self.keep[0, :, lanes] + self.pair_in[0, :, lanes].astype(jnp.float32))
        self.far_out[:, lanes] = block
        if remote:
            self.far[k] = send(
                self.far_out.at[:, lanes], self.far_in.at[:, lanes], self.sems, 3 * k + 2, self.across
            )

    def near_sum(self, k, lanes):
        self.pair[k, 1].wait_recv()
        return self.keep[1, :, lanes] + self.pair_in[1, :, lanes].astype(jnp.float32)

    def end(self, k, lanes):
        total = self.near_sum(k, lanes)
        self.far[k].wait_recv()
        return total + self.far_in[:, lanes].astype(jnp.float32)

    def finish(self):
        for copies in (self.pair, self.far):
            for copy in copies.values():
                copy.wait_send()


class Rows:
    def __init__(self, where, buffer, sems):
        self.me, self.peers = where[0], where[1:]
        self.buffer, self.sems = buffer, sems
        self.copies = {}

    def start(self, k, lanes, first, second):
        self.buffer[self.me, 0:1, lanes] = first
        self.buffer[self.me, 1:2, lanes] = second
        block = self.buffer.at[self.me, :, lanes]
        self.copies[k] = [
            send(block, block, self.sems, 3 * k + index, peer) for index, peer in enumerate(self.peers)
        ]

    def end(self, k, lanes):
        for copy in self.copies[k]:
            copy.wait_recv()
        total = sum(self.buffer[index, :, lanes] for index in range(4))
        return total[0:1], total[1:2]

    def finish(self):
        for copies in self.copies.values():
            for copy in copies:
                copy.wait_send()


class Halving:
    def __init__(self, count, buffer, lanes, arrivals, transit, sems, order, result):
        self.result, self.transit = result, transit
        self.count, self.buffer, self.lanes = count, buffer, lanes
        self.arrivals, self.sems, self.order = arrivals, sems, order
        self.own = buffer.shape[0] // count
        self.me = lax.axis_index("dp")
        self.bit = {bit: lax.rem(self.me // 2**bit, 2) for bit in order}
        self.phase, self.slot, self.copies, self.sent, self.passing = 0, 0, [], [], False
        self.inner = self.bit[1] + self.bit[2] == 1

    def rows(self, block):
        return pl.ds(pl.multiple_of(block * self.own, 16), self.own)

    def blocks(self, side):
        bit = self.order[self.phase]
        found = [self.bit[bit] * (1 - 2 * side) * 2**bit + side * 2**bit]
        for done in self.order[: self.phase]:
            found = [block + self.bit[done] * 2**done for block in found]
        for free in self.order[self.phase + 1 :]:
            found = [block + value * 2**free for block in found for value in range(2)]
        return found

    def arrival(self, target, at):
        return pltpu.make_async_remote_copy(
            src_ref=target,
            dst_ref=target,
            send_sem=self.sems.at[0, at],
            recv_sem=self.sems.at[1, at],
            device_id={"dp": self.me},
            device_id_type=MESH,
        )

    def forward(self, side):
        return pltpu.make_async_remote_copy(
            src_ref=self.transit.at[side],
            dst_ref=self.arrivals.at[self.slot],
            send_sem=self.sems.at[0, self.count + side],
            recv_sem=self.sems.at[1, self.slot],
            device_id={"dp": self.me + 2 - 4 * side},
            device_id_type=MESH,
        )

    def relay(self):
        @pl.when(self.inner)
        def _():
            for side in range(2):
                self.arrival(self.transit.at[side], self.count + side).wait_recv()
                self.forward(side).start()

    def start_far(self):
        side = self.bit[2]
        copy = pltpu.make_async_remote_copy(
            src_ref=self.buffer.at[self.rows(self.blocks(1)[0]), self.lanes],
            dst_ref=self.transit.at[side],
            send_sem=self.sems.at[0, self.slot],
            recv_sem=self.sems.at[1, self.count + side],
            device_id={"dp": self.me + 2 - 4 * side},
            device_id_type=MESH,
        )
        copy.start()
        self.sent.append(copy)
        self.copies = [self.arrival(self.arrivals.at[self.slot], self.slot)]
        self.passing = True

    def start(self):
        bit = self.order[self.phase]
        if bit == 2:
            self.start_far()
            return
        partner = self.me + 2**bit - 2 * 2**bit * self.bit[bit]
        self.copies = []
        for offset, block in enumerate(self.blocks(1)):
            at = self.slot + offset
            self.copies.append(
                send_dp(self.buffer.at[self.rows(block), self.lanes], self.arrivals.at[at], self.sems, at, partner)
            )
        self.sent += self.copies

    def step(self):
        if self.passing:
            self.passing = False
            self.relay()
            return
        for offset, block in enumerate(self.blocks(0)):
            self.copies[offset].wait_recv()
            total = self.buffer[self.rows(block), self.lanes].astype(jnp.float32) + self.arrivals[
                self.slot + offset
            ].astype(jnp.float32)
            if self.phase + 1 < len(self.order):
                self.buffer[self.rows(block), self.lanes] = low(total)
            else:
                self.result[:, self.lanes] = total
        self.slot += len(self.copies)
        self.phase += 1
        if self.phase < len(self.order):
            self.start()

    def finish(self):
        for copy in self.sent:
            copy.wait_send()
        self.slot -= 1

        @pl.when(self.inner)
        def _():
            for side in range(2):
                self.forward(side).wait_send()


def halving_scratch(count, rows, columns):
    return pltpu.VMEM((count - 1, rows // count, columns), jnp.bfloat16)


def reduce_scratch(part, length):
    return [
        pltpu.VMEM((2, part, length), jnp.bfloat16),
        pltpu.VMEM((2, part, length), jnp.bfloat16),
        pltpu.VMEM((part, length), jnp.bfloat16),
        pltpu.VMEM((part, length), jnp.bfloat16),
        pltpu.VMEM((2, part, length), jnp.float32),
    ]


def copy_sems(count):
    return pltpu.SemaphoreType.DMA((2, count))


def column_sums(rows):
    return jnp.sum(rows, axis=1, keepdims=True)


def row_sums(rows):
    return jnp.sum(rows, axis=0, keepdims=True)


def span_forward(heads, at, lanes, states, proj, cum_ref, col_ref, rec, states_ref):
    scale = HD ** (-0.5)
    after = []
    for head in range(heads):
        query, key, value = (
            proj[(kind * heads + head) * HEAD_ROWS : (kind * heads + head + 1) * HEAD_ROWS, lanes]
            for kind in range(3)
        )
        row = cum_ref[head : head + 1, lanes]
        column = col_ref[lanes, head : head + 1]
        last = row[:, SPAN - 1 : SPAN]
        state = states[head]
        states_ref[at, head] = state
        weights = decay_block(row, column) * mm(key, query, TN)
        out = mm(value, low(weights), NN)
        out = out + mm(low(state), low(query.astype(jnp.float32) * jnp.exp(row)), NN)
        rec[head * HD : (head + 1) * HD, lanes] = out[:HD] * scale
        carried = low(key.astype(jnp.float32) * jnp.exp(last - row))
        after.append(state * jnp.exp(last) + mm(value, carried, NT))
    return after


def conv_chunk(k, chunks, rec, taps, mixed_ref):
    length = chunks * CHUNK
    begin, end = max(k * CHUNK - 128, 0), min((k + 1) * CHUNK + 128, length)
    window, skip = pl.ds(begin, end - begin), k * CHUNK - begin
    masks = edge_masks(length, begin, end)

    def one_group(at, carry):
        rows = pl.ds(pl.multiple_of(at * CONV_ROWS, CONV_ROWS), CONV_ROWS)
        mixed = conv_rows(rec[rows, window], taps[rows, :], masks, False)
        mixed_ref[rows, k * CHUNK : (k + 1) * CHUNK] = low(mixed[:, skip : skip + CHUNK])
        return carry

    lax.fori_loop(0, rec.shape[0] // CONV_ROWS, one_group, 0)


def conv_backward(grad_ref, rec, taps, grec, gtaps):
    masks = edge_masks(rec.shape[1])
    lane = lax.broadcasted_iota(jnp.int32, (BACK_ROWS, 16), 1)
    scale = HD ** (-0.5)

    def one_group(at, carry):
        rows = pl.ds(pl.multiple_of(at * BACK_ROWS, BACK_ROWS), BACK_ROWS)
        grad = grad_ref[rows, :]
        grec[rows, :] = conv_rows(grad, taps[rows, :], masks, True) * scale
        moved = neighbours(rec[rows, :], masks)
        _, _, up_ok, down_ok = masks
        grads = (
            jnp.where(down_ok, shifted(grad, GRID), 0.0),
            grad,
            jnp.where(up_ok, shifted(grad, -GRID), 0.0),
        )
        result = jnp.zeros((BACK_ROWS, 16), jnp.float32)
        for row in range(3):
            for col in range(3):
                one = jnp.sum(moved[col] * grads[row], axis=1, keepdims=True)
                result = jnp.where(lane == 3 * row + col, one, result)
        gtaps[rows, :] = result
        return carry

    lax.fori_loop(0, rec.shape[0] // BACK_ROWS, one_group, 0)


def spans_backward(heads, proj, logit_ref, cum_ref, col_ref, states, grec, staged, rows_ref, gproj):
    part, length = grec.shape
    spans = length // SPAN
    wide_rows = staged.shape[0]
    rows_ref[...] = jnp.zeros_like(rows_ref)
    staged[3 * part :, :] = jnp.zeros((wide_rows - 3 * part, SPAN), jnp.float32)
    key_at = lax.broadcasted_iota(jnp.int32, (SPAN, SPAN), 0)
    query_at = lax.broadcasted_iota(jnp.int32, (SPAN, SPAN), 1)
    later = low(jnp.where(key_at >= query_at, 1.0, 0.0))
    filler = jnp.zeros((HEAD_ROWS - HD, SPAN), jnp.float32)

    def one_span(step, back_states):
        at = spans - 1 - step
        lanes = pl.ds(pl.multiple_of(at * SPAN, SPAN), SPAN)
        after = []
        for head in range(heads):
            query, key, value = (
                proj[(kind * heads + head) * HEAD_ROWS : (kind * heads + head + 1) * HEAD_ROWS, lanes]
                for kind in range(3)
            )
            grad = low(jnp.concatenate([grec[head * HD : (head + 1) * HD, lanes], filler], axis=0))
            row = cum_ref[head : head + 1, lanes]
            column = col_ref[lanes, head : head + 1]
            last = row[:, SPAN - 1 : SPAN]
            state = states[at, head]
            back = back_states[head]
            decay = decay_block(row, column)
            weights = decay * mm(key, query, TN)
            grad_weights = mm(value, grad, TN)
            product = low(grad_weights * weights)
            grad_score = low(grad_weights * decay)
            in_decay = jnp.exp(row)
            out_decay = jnp.exp(last - row)
            query_in = mm(low(state), grad, TN) * in_decay
            key_out = mm(low(back), value, TN) * out_decay
            query_wide = query.astype(jnp.float32)
            key_wide = key.astype(jnp.float32)
            grad_query = mm(key, grad_score, NN) + query_in
            grad_key = mm(query, grad_score, NT) + key_out
            grad_value = mm(grad, low(weights), NT) + mm(low(back), low(key_wide * out_decay), NN)
            for kind, piece in enumerate((grad_query, grad_key, grad_value)):
                staged[kind * part + head * HD : kind * part + (head + 1) * HD, :] = piece[:HD]
            inside = mm(product, later, NN)
            inside = jnp.sum(jnp.where(key_at < query_at, inside, 0.0), axis=0, keepdims=True)
            span_decay = jnp.exp(last)
            across = jnp.sum(back * state, keepdims=True) * span_decay
            rows_ref[0, head : head + 1, :] = jnp.sum(query_wide * query_in, axis=0, keepdims=True)
            rows_ref[1, head : head + 1, :] = jnp.sum(key_wide * key_out, axis=0, keepdims=True)
            rows_ref[2, head : head + 1, :] = inside + across
            after.append(back * span_decay + mm(grad, low(query_wide * in_decay), NT))
        grad_log = (
            running_sum(rows_ref[0], SPAN, reverse=True)
            + running_sum(rows_ref[1], SPAN, exclusive=True)
            + rows_ref[2]
        )
        grad_forget = grad_log / (1.0 + jnp.exp(logit_ref[:, lanes]))
        staged[3 * part : 3 * part + heads, :] = grad_forget[:heads]
        gproj[:wide_rows, lanes] = low(staged[...])
        return tuple(after)

    lax.fori_loop(
        0, spans, one_span, tuple(jnp.zeros((HEAD_ROWS, HEAD_ROWS), jnp.float32) for _ in range(heads))
    )


GELU_SLOPE = math.sqrt(2.0 / math.pi)
GELU_CUBE = 0.044715
X_FIRST, Z_FIRST = (0, 1, 2), (1, 0, 2)


def layer_kernel(
    shard_count, heads, direct,
    x_hbm, cot_hbm, silu_ref, ada_hbm, bias_ref, qkv_hbm, gate_ref, gate_bias_ref, conv_ref, out_w_ref, up_hbm,
    down_hbm, cond_ref, label_ref,
    gtokens_hbm, out_hbm, gdown_hbm, gup_hbm, gqkv_out, gout_out, gclass_ref, gada_ref, gsmall_ref, normed_hbm,
    wback_hbm,
    gtokens_ref, out_ref, gdown_own, gup_own,
    x_ref, cot_ref, up, down, turned, gmlp, gact, normed, act, gup_rows, gattn,
    attn, after, gafter, mix_ref,
    a_pair_out, a_pair_in, a_far_out, a_far_in, a_keep,
    g_pair_out, g_pair_in, g_far_out, g_far_in, g_keep,
    mod_parts, first_rows, second_rows, third_rows, silu_rows,
    proj, rec, states, logit_ref, stats_ref, cum_ref, col_ref, span_rows, taps, gtaps, mods_ref, gmods, ada_rest,
    parcels, latent_in, mods_out, mods_in, gcond, silu_own, mods_own, label_own,
    down_a, down_b, down_c, up_a, up_b, up_c, qkv_a, qkv_b, out_a, *rest
):
    transits = rest[:9]
    (
        raw_sems, part_sems, gm_sems, a_sems, n_sems, g_sems, t_sems, m_sems, s_sems, first_sems, second_sems,
        third_sems, silu_sems, dp_sems, down_a_sems, down_b_sems, down_c_sems, up_a_sems, up_b_sems, up_c_sems,
        qkv_a_sems, qkv_b_sems, out_a_sems, move_sems,
    ) = rest[9:]
    part, length = x_ref.shape
    width = 4 * part
    own_width = width // shard_count
    hidden = up.shape[1]
    chunks = length // CHUNK
    lanes = [pl.ds(k * CHUNK, CHUNK) for k in range(chunks)]
    where = places()
    me, across, beside, _ = where
    spot = lax.axis_index("dp")
    own, other = shard(me, part), shard(across, part)
    projected = qkv_hbm.shape[0]
    raw, wide = act, down.at[:WIDE_ROWS, :]
    moves = Moves(move_sems)
    moves.start("ada", ada_hbm.at[:width, :], up)
    moves.start("ada_rest", ada_hbm.at[width:, :], ada_rest)
    moves.start("raw", x_hbm, raw.at[own, :])
    moves.start("qkv", qkv_hbm, wide.at[:projected, :])
    moves.start("cot", cot_hbm, cot_ref)
    moves.start("x", x_hbm, x_ref)
    for rows in (mod_parts, first_rows, second_rows, third_rows, silu_rows, parcels, mods_out):
        rows[...] = jnp.zeros(rows.shape, rows.dtype)
    barrier = pltpu.get_barrier_semaphore()
    for peer in where[1:]:
        pl.semaphore_signal(barrier, inc=1, device_id={"tensor": peer}, device_id_type=MESH)
    for step in range(1, shard_count):
        pl.semaphore_signal(
            barrier, inc=1, device_id={"dp": lax.rem(spot + step, shard_count)}, device_id_type=MESH
        )
    pl.semaphore_wait(barrier, shard_count + 2)

    spread = Spread(where, raw, raw_sems, part)
    gm_spread = Spread(where, gmlp, gm_sems, part)
    spread.start(0, lanes[0], x_hbm.at[:, lanes[0]])
    part_at = lax.broadcasted_iota(jnp.int32, (8, part), 0)
    bias = bias_ref[...].astype(jnp.float32)
    mod_sum = jnp.concatenate([bias, jnp.zeros((8 - bias.shape[0], part), jnp.float32)], axis=0)
    silu_rows_low = silu_ref[...]

    def ada_piece(index):
        if index < 4:
            return up[index * part : (index + 1) * part, :]
        return ada_rest[(index - 4) * part : (index - 3) * part, :]

    moves.wait("ada")
    moves.wait("ada_rest")
    for index in range(6):
        mod_sum = mod_sum + jnp.where(part_at == index, mm(silu_rows_low, ada_piece(index), NT), 0.0)
    mod_parts[me, :, :part] = mod_sum
    part_copies = [
        send(mod_parts.at[me], mod_parts.at[me], part_sems, index, peer) for index, peer in enumerate(where[1:])
    ]
    for k in range(1, chunks):
        spread.start(k, lanes[k], x_hbm.at[:, lanes[k]])
    moves.start("up", up_hbm, up)
    mods_ref[...] = jnp.transpose(mod_parts[me])[:part]
    moves.wait("cot")
    gmlp[own, :] = low(cot_ref[...].astype(jnp.float32) * mods_ref[:, 5:6])
    gm_spread.start(0, lanes[0])
    moves.wait("qkv")
    gate = gate_ref[...].astype(jnp.float32)
    wide[projected:, :] = low(
        jnp.concatenate([gate, jnp.zeros((WIDE_ROWS - projected - heads, width), jnp.float32)], axis=0)
    )
    gup_rows[:, :WIDE_ROWS] = jnp.transpose(wide[...])
    moves.start("wback_out", gup_rows.at[:, :WIDE_ROWS], wback_hbm)
    gate_at = lax.broadcasted_iota(jnp.int32, (8, 1), 0)
    gate_bias = jnp.zeros((8, 1), jnp.float32)
    for head in range(heads):
        gate_bias = gate_bias + jnp.where(gate_at == head, gate_bias_ref[0:1, head : head + 1].astype(jnp.float32), 0.0)
    conv = [conv_ref[index].astype(jnp.float32) for index in range(3)]
    taps[...] = jnp.transpose(jnp.concatenate(conv + [jnp.zeros((7, part), jnp.float32)], axis=0))
    stats_ref[2:, :] = jnp.zeros((6, length), jnp.float32)
    filler = jnp.zeros((HEAD_ROWS - HD, CHUNK), jnp.float32)
    carried = [jnp.zeros((HEAD_ROWS, HEAD_ROWS), jnp.float32) for _ in range(heads)]

    def project_chunk(k, carried):
        spread.end(k)
        blocks = [raw[index * part : (index + 1) * part, lanes[k]].astype(jnp.float32) for index in range(4)]
        mean = sum(row_sums(block) for block in blocks) / width
        square = sum(row_sums(block * block) for block in blocks) / width
        inv_std = lax.rsqrt(square - mean * mean + norm_eps)
        stats_ref[0:1, lanes[k]] = mean
        stats_ref[1:2, lanes[k]] = inv_std
        for index in range(4):
            unit = (blocks[index] - mean) * inv_std
            value = unit * (1.0 + columns[index][:, 1:2]) + columns[index][:, 0:1]
            gattn[index * part : (index + 1) * part, lanes[k]] = low(value)
        product = mm(wide[...], gattn[:, lanes[k]], NN)
        for index in range(3 * heads):
            piece = jnp.concatenate([product[index * HD : (index + 1) * HD], filler], axis=0)
            proj[index * HEAD_ROWS : (index + 1) * HEAD_ROWS, lanes[k]] = low(piece)
        logit = product[projected : projected + 8] + gate_bias
        logit_ref[:, lanes[k]] = logit
        cum = running_sum(log_sigmoid(logit), SPAN)
        cum_ref[:, lanes[k]] = cum
        col_ref[lanes[k], :] = jnp.transpose(cum)
        return span_forward(heads, k, lanes[k], carried, proj, cum_ref, col_ref, rec, states)

    gate_one, scale_two, shift_two = mods_ref[:, 2:3], mods_ref[:, 4:5], mods_ref[:, 3:4]

    attn_sum = Reduce(where, part, (a_pair_out, a_pair_in, a_far_out, a_far_in, a_keep), a_sems)
    mlp_sum = Reduce(where, part, (a_pair_out, a_pair_in, a_far_out, a_far_in, a_keep), m_sems)
    grad_sum = Reduce(where, part, (g_pair_out, g_pair_in, g_far_out, g_far_in, g_keep), g_sems)
    last_sum = Reduce(where, part, (g_pair_out, g_pair_in, g_far_out, g_far_in, g_keep), s_sems)
    norm_spread = Spread(where, normed, n_sems, part)
    grad_spread = Spread(where, gattn, t_sems, part)
    moments = Rows(where, first_rows, first_sems)
    means = Rows(where, second_rows, second_sems)
    last_means = Rows(where, third_rows, third_sems)
    if direct:
        totals = {}
        for name, buffer, result, parts in (
            (
                "down", up, gdown_own,
                ((down_a, down_a_sems, X_FIRST), (down_b, down_b_sems, X_FIRST), (down_c, down_c_sems, Z_FIRST)),
            ),
            ("up", down, gup_own, ((up_a, up_a_sems, X_FIRST), (up_b, up_b_sems, X_FIRST), (up_c, up_c_sems, Z_FIRST))),
            ("qkv", act, gqkv_out, ((qkv_a, qkv_a_sems, X_FIRST), (qkv_b, qkv_b_sems, Z_FIRST))),
            ("out", gup_rows, gout_out, ((out_a, out_a_sems, Z_FIRST),)),
        ):
            column = 0
            for letter, (arrivals, sems, order) in zip("abc", parts):
                columns = arrivals.shape[2]
                totals[name + "_" + letter] = Halving(
                    shard_count, buffer, pl.ds(column, columns), arrivals, transits[len(totals)], sems, order, result
                )
                column += columns

    def begin(*names):
        if direct:
            for name in names:
                totals[name].start()

    def advance(*names):
        if direct:
            for name in names:
                totals[name].step()

    gmods[...] = jnp.zeros_like(gmods)
    gmix = gtokens_ref

    def attn_start(k):
        mixed = mix_ref[:, lanes[k]]
        attn_sum.start(k, lanes[k], lambda owner: mm(gup_rows[shard(owner, part), :part], mixed, NN))

    def attn_end(k):
        value = attn_sum.end(k, lanes[k])
        attn[:, lanes[k]] = value
        total = x_ref[:, lanes[k]].astype(jnp.float32) + gate_one * value
        after[:, lanes[k]] = total
        moments.start(k, lanes[k], row_sums(total), row_sums(total * total))

    inverse, average = [None] * chunks, [None] * chunks

    def unit_two(k):
        return (after[:, lanes[k]] - average[k]) * inverse[k]

    def norm_chunk(k):
        total, squares = moments.end(k, lanes[k])
        average[k] = total / width
        inverse[k] = lax.rsqrt(squares / width - average[k] * average[k] + norm_eps)
        normed[own, lanes[k]] = low(unit_two(k) * (1.0 + scale_two) + shift_two)
        norm_spread.start(k, lanes[k])

    def grad_act_chunk(k):
        gact[...] = mm(down[...], gmlp[:, lanes[k]], NN)

    def hidden_chunk(k):
        norm_spread.end(k)
        block = normed[:, lanes[k]]

        def one_block(at, carry):
            rows = pl.ds(pl.multiple_of(at * part, 32), part)
            value = mm(turned[rows, :], block, NN)
            square = value * value
            bend = jnp.tanh(GELU_SLOPE * value * (1.0 + GELU_CUBE * square))
            half = 0.5 * (1.0 + bend)
            act[rows, lanes[k]] = low(value * half)
            slope = half + 0.5 * value * (1.0 - bend * bend) * GELU_SLOPE * (1.0 + 3.0 * GELU_CUBE * square)
            gup_rows[rows, lanes[k]] = low(gact[rows, :] * slope)
            return carry

        lax.fori_loop(0, hidden // part, one_block, 0)

    def grad_start(k):
        block = gup_rows[:, lanes[k]]
        grad_sum.start(k, lanes[k], lambda owner: mm(up[shard(owner, part), :], block, NN))

    def grad_end(k):
        grad = grad_sum.end(k, lanes[k])
        rows = unit_two(k)
        gmods[:, 3:4] += column_sums(grad)
        gmods[:, 4:5] += column_sums(grad * rows)
        scaled = grad * (1.0 + scale_two)
        gafter[:, lanes[k]] = scaled
        means.start(k, lanes[k], row_sums(scaled), row_sums(scaled * rows))

    def after_chunk(k):
        total, along = means.end(k, lanes[k])
        scaled = gafter[:, lanes[k]]
        back = inverse[k] * (scaled - total / width - unit_two(k) * (along / width))
        grad = cot_ref[:, lanes[k]].astype(jnp.float32) + back
        gafter[:, lanes[k]] = grad
        gattn[own, lanes[k]] = low(grad * gate_one)
        grad_spread.start(k, lanes[k])
        gmods[:, 2:3] += column_sums(grad * attn[:, lanes[k]])

    def mixed_chunk(k):
        grad_spread.end(k)
        gmix[:, lanes[k]] = mm(out_w_ref[...], gattn[:, lanes[k]], NN)

    def weight_grad(target, columns, left, right, at, pieces):
        rows = target.shape[0] // pieces
        rows = slice(at * rows, (at + 1) * rows)
        target[rows, columns] = low(mm(left[rows, :], right[...], NT))

    def mlp_start(k):
        block = act[:, lanes[k]]
        mlp_sum.start(k, lanes[k], lambda owner: mm(turned[shard(owner, part), :], block, NN))

    def outputs(k):
        mlp = mlp_sum.end(k, lanes[k])
        out_ref[:, lanes[k]] = low(after[:, lanes[k]] + mods_ref[:, 5:6] * mlp)
        gmods[:, 5:6] += column_sums(cot_ref[:, lanes[k]].astype(jnp.float32) * mlp)

    every_column = slice(None)
    spread.relay(0, lanes[0])
    moves.wait("up")
    turned[...] = jnp.transpose(up[...])
    moves.wait("wback_out")
    gup_rows[:, :part] = jnp.transpose(out_w_ref[...])
    moves.wait("raw")
    for copy in part_copies:
        copy.wait_recv()
    columns = [jnp.transpose(mod_parts[index])[:part] for index in range(4)]
    spread.relay(1, lanes[1])
    carried = project_chunk(0, carried)
    spread.relay(2, lanes[2])
    carried = project_chunk(1, carried)
    conv_chunk(0, chunks, rec, taps, mix_ref)
    attn_start(0)
    spread.relay(3, lanes[3])
    attn_sum.relay(0, lanes[0])
    carried = project_chunk(2, carried)
    conv_chunk(1, chunks, rec, taps, mix_ref)
    attn_start(1)
    moves.wait("x")
    gm_spread.relay(0, lanes[0])
    attn_sum.relay(1, lanes[1])
    attn_end(0)
    gm_spread.start(1, lanes[1])
    project_chunk(3, carried)
    spread.finish()
    moves.start("normed_out", gattn, normed_hbm)
    moves.start("down", down_hbm, down)
    conv_chunk(2, chunks, rec, taps, mix_ref)
    attn_start(2)
    conv_chunk(3, chunks, rec, taps, mix_ref)
    attn_sum.relay(2, lanes[2])
    attn_end(1)
    norm_chunk(0)
    attn_start(3)
    gm_spread.relay(1, lanes[1])
    attn_sum.relay(3, lanes[3])
    moves.wait("down")
    moves.wait("normed_out")
    gm_spread.end(0)
    grad_act_chunk(0)
    attn_end(2)
    norm_chunk(1)
    gm_spread.start(2, lanes[2])
    norm_spread.relay(0, lanes[0])
    hidden_chunk(0)
    attn_end(3)
    norm_chunk(2)
    gm_spread.start(3, lanes[3])
    grad_start(0)
    norm_spread.relay(1, lanes[1])
    norm_chunk(3)
    gm_spread.relay(2, lanes[2])
    grad_sum.relay(0, lanes[0])
    gm_spread.end(1)
    grad_act_chunk(1)
    hidden_chunk(1)
    grad_start(1)
    norm_spread.relay(2, lanes[2])
    gm_spread.relay(3, lanes[3])
    grad_sum.relay(1, lanes[1])
    gm_spread.end(2)
    grad_act_chunk(2)
    hidden_chunk(2)
    grad_start(2)
    gm_spread.end(3)
    grad_act_chunk(3)
    norm_spread.relay(3, lanes[3])
    grad_end(0)
    grad_sum.relay(2, lanes[2])
    hidden_chunk(3)
    grad_start(3)
    weight_grad(up, every_column, gmlp, act, 0, 2)
    weight_grad(up, every_column, gmlp, act, 1, 2)
    begin("down_a", "down_c", "down_b")
    if not direct:
        moves.start("gdown", up, gdown_hbm)
    grad_sum.relay(3, lanes[3])
    after_chunk(0)
    grad_end(1)
    turned[...] = jnp.transpose(down[...])
    weight_grad(down, every_column, normed, gup_rows, 0, 2)
    grad_spread.relay(0, lanes[0])
    after_chunk(1)
    grad_end(2)
    weight_grad(down, every_column, normed, gup_rows, 1, 2)
    begin("up_c", "up_a")
    if not direct:
        moves.start("gup", down, gup_hbm)
    after_chunk(2)
    advance("down_a", "down_c")
    begin("up_b")
    grad_spread.relay(1, lanes[1])
    mixed_chunk(0)
    grad_end(3)
    after_chunk(3)
    attn_sum.finish()
    grad_spread.relay(2, lanes[2])
    mixed_chunk(1)
    mlp_start(0)
    mlp_start(1)
    mlp_sum.relay(0, lanes[0])
    mixed_chunk(2)
    mlp_start(2)
    mlp_sum.relay(1, lanes[1])
    grad_spread.relay(3, lanes[3])
    mlp_start(3)
    mlp_sum.relay(2, lanes[2])
    norm_spread.finish()
    moves.start("normed", normed_hbm, normed)
    advance("down_b", "up_c")
    mixed_chunk(3)
    weight_grad(gup_rows, slice(0, part), gattn, mix_ref, 0, 1)
    mlp_sum.relay(3, lanes[3])
    moves.start("wback", wback_hbm, turned.at[:, :WIDE_ROWS])
    if not direct:
        moves.start("gout", gup_rows.at[:, : out_a.shape[2]], gout_out)

    advance("down_a")
    conv_backward(gmix, rec, taps, attn, gtaps)
    advance("down_a", "up_a", "down_b", "down_c")
    begin("out_a")
    grad_spread.finish()
    grad_sum.finish()
    staged = gact.at[:WIDE_ROWS, :]
    spans_backward(heads, proj, logit_ref, cum_ref, col_ref, states, attn, staged, span_rows, gattn)
    advance("down_b", "down_c", "up_b", "up_a", "down_a")
    gproj = gattn.at[:WIDE_ROWS, :]

    def last_start(k):
        block = gproj[:, lanes[k]]
        last_sum.start(k, lanes[k], lambda owner: mm(turned[shard(owner, part), :WIDE_ROWS], block, NN))

    def unit_one(k):
        return (x_ref[:, lanes[k]].astype(jnp.float32) - stats_ref[0:1, lanes[k]]) * stats_ref[1:2, lanes[k]]

    def last_end(k):
        grad = last_sum.end(k, lanes[k])
        unit = unit_one(k)
        gmods[:, 0:1] += column_sums(grad)
        gmods[:, 1:2] += column_sums(grad * unit)
        scaled = grad * (1.0 + mods_ref[:, 1:2])
        gtokens_ref[:, lanes[k]] = scaled
        last_means.start(k, lanes[k], row_sums(scaled), row_sums(scaled * unit))

    def tokens(k):
        total, along = last_means.end(k, lanes[k])
        back = gtokens_ref[:, lanes[k]] - total / width - unit_one(k) * (along / width)
        gtokens_ref[:, lanes[k]] = gafter[:, lanes[k]] + stats_ref[1:2, lanes[k]] * back

    moves.wait("wback")
    last_start(0)
    last_start(1)
    last_sum.relay(0, lanes[0])
    moves.wait("normed")
    for piece in range(2):
        weight_grad(act, slice(0, WIDE_ROWS), normed, gproj, piece, 2)
    begin("qkv_a", "qkv_b")
    if not direct:
        moves.start("gqkv", act.at[:, :WIDE_ROWS], gqkv_out)
    last_start(2)
    last_sum.relay(1, lanes[1])
    last_start(3)
    last_sum.relay(2, lanes[2])
    moves.start("ada_again", ada_hbm.at[:width, :], turned)
    last_sum.relay(3, lanes[3])
    for k in range(chunks):
        outputs(k)
    moves.start("out", out_ref, out_hbm)
    advance("out_a", "up_c")
    last_end(0)
    last_end(1)
    tokens(0)
    advance("up_a", "down_b", "down_c")
    if direct:
        moves.start("gdown", gdown_own, gdown_hbm)
    last_end(2)
    tokens(1)
    last_end(3)
    advance("up_b")

    mod_rows = jnp.transpose(gmods[...])
    low_rows = low(mod_rows)
    row_at = lax.broadcasted_iota(jnp.int32, (8, width), 0)
    moves.wait("ada_again")
    product = jnp.zeros((8, width), jnp.float32)
    for index in range(6):
        piece = turned[index * part : (index + 1) * part, :] if index < 4 else ada_piece(index)
        product = product + jnp.where(row_at == index, mm(low_rows, piece, NN), 0.0)
    silu_rows[me, 0:1, :] = row_sums(product)
    silu_copies = [
        send(silu_rows.at[me], silu_rows.at[me], silu_sems, index, peer) for index, peer in enumerate(where[1:])
    ]
    tap_rows = jnp.transpose(gtaps[...])
    forget = gattn[3 * part : WIDE_ROWS, :].astype(jnp.float32)[:8]
    forget = jnp.transpose(jnp.broadcast_to(column_sums(forget), (8, 128)))[0:1]
    small = jnp.concatenate([mod_rows[:6], tap_rows[:9], jnp.zeros((1, part), jnp.float32)], axis=0)
    mods_out[:, :part] = low(small)
    mods_out[:, part : part + 8] = low(jnp.broadcast_to(forget, (16, 8)))
    mods_in[spot] = mods_out[...]
    dp_copies = []
    for step in range(1, shard_count):
        peer = lax.rem(spot + step, shard_count)
        dp_copies.append(send_dp(mods_out, mods_in.at[spot], dp_sems, step, peer))
    tokens(2)
    tokens(3)
    moves.start("gtokens", gtokens_ref, gtokens_hbm)
    advance("qkv_a", "qkv_b", "up_c", "up_a")
    for copy in silu_copies:
        copy.wait_recv()
    grad_silu = sum(silu_rows[index, 0:1, :] for index in range(4))
    cond = cond_ref[0:1, :]
    sigmoid = 1.0 / (1.0 + jnp.exp(-cond))
    grad_cond = grad_silu * (sigmoid * (1.0 + cond * (1.0 - sigmoid)))
    silu = low(cond * sigmoid).astype(jnp.float32)
    for index in range(shard_count):
        columns = slice(index * own_width, (index + 1) * own_width)
        parcels[index, 0:1, :own_width] = grad_cond[:, columns]
        parcels[index, 1:2, :own_width] = silu[:, columns]
        parcels[index, 2:3, :] = jnp.broadcast_to(label_ref[...], (1, parcels.shape[2]))
    latent_in[spot] = parcels[spot]
    for step in range(1, shard_count):
        peer = lax.rem(spot + step, shard_count)
        dp_copies.append(send_dp(parcels.at[peer], latent_in.at[spot], dp_sems, shard_count + step, peer))
    advance("out_a", "up_b", "qkv_b", "up_c", "up_b")
    if direct:
        moves.start("gup", gup_own, gup_hbm)
    advance("qkv_a", "out_a", "qkv_b")
    for copy in dp_copies:
        copy.wait_recv()
    small_sum = jnp.zeros(mods_out.shape, jnp.float32)
    for index in range(shard_count):
        arrived = mods_in[index].astype(jnp.float32)
        small_sum = small_sum + arrived
        for row in range(6):
            mods_own[row, index : index + 1, :] = arrived[row : row + 1, :part]
        gcond[index : index + 1, :] = latent_in[index, 0:1, :own_width]
        silu_own[index : index + 1, :] = latent_in[index, 1:2, :own_width]
        label_own[index : index + 1, :] = latent_in[index, 2:3, :128]
    gsmall_ref[...] = small_sum
    class_at = lax.broadcasted_iota(jnp.int32, (shard_count, NCLASS), 1).astype(jnp.float32)
    onehot = jnp.where(label_own[:, 0:1] == class_at, 1.0, 0.0)
    gclass_ref[...] = lax.dot_general(
        gcond[...], onehot, TN, precision=TOP_PRECISION, preferred_element_type=jnp.float32
    )
    for row in range(6):
        gada_ref[row] = mm(low(silu_own[...]), low(mods_own[row]), TN)
    advance("qkv_a", "out_a", "qkv_b", "qkv_a")
    if direct:
        for total in totals.values():
            total.finish()
    else:
        moves.wait("gqkv")
        moves.wait("gout")
    for name in ("gdown", "gup", "out", "gtokens"):
        moves.wait(name)
    for copy in part_copies + dp_copies + silu_copies:
        copy.wait_send()
    for group in (gm_spread, mlp_sum, last_sum, moments, means, last_means):
        group.finish()


def layer(
    x, cot, silu, ada, bias, qkv, gate, gate_bias, conv, out_w, up, down, cond, label, shard_count, heads, direct
):
    part, length = x.shape
    width = 4 * part
    hidden = up.shape[1]
    own = width // shard_count
    chunks = length // CHUNK
    spans = length // SPAN
    padded = part + -part % 128
    own_padded = own + -own % 128
    proj_rows = 3 * heads * HEAD_ROWS
    shape = jax.ShapeDtypeStruct
    vmem = pltpu.VMEM
    bf16, f32 = jnp.bfloat16, jnp.float32
    grad_rows, grad_type, grad_spec = (own, f32, VMEM_SPEC) if direct else (width, bf16, ANY_SPEC)
    arrivals = shard_count if direct else 2
    arrival_rows = width if direct else 32
    cuts = (*[hidden // 3] * 6, 640, WIDE_ROWS - 640, padded)
    return pl.pallas_call(
        functools.partial(layer_kernel, shard_count, heads, direct),
        out_shape=(
            shape((part, length), f32),
            shape((part, length), bf16),
            shape((grad_rows, hidden), grad_type),
            shape((grad_rows, hidden), grad_type),
            shape((grad_rows, WIDE_ROWS), grad_type),
            shape((grad_rows, padded), grad_type),
            shape((own, NCLASS), f32),
            shape((6, own, part), f32),
            shape((16, padded), f32),
            shape((width, length), bf16),
            shape((width, WIDE_ROWS), bf16),
        ),
        in_specs=[
            ANY_SPEC, ANY_SPEC, VMEM_SPEC, ANY_SPEC, VMEM_SPEC, ANY_SPEC, VMEM_SPEC, VMEM_SPEC, VMEM_SPEC, VMEM_SPEC,
            ANY_SPEC, ANY_SPEC, VMEM_SPEC, VMEM_SPEC,
        ],
        out_specs=[ANY_SPEC] * 4 + [grad_spec] * 2 + [VMEM_SPEC] * 3 + [ANY_SPEC] * 2,
        scratch_shapes=[
            vmem((part, length), f32),
            vmem((part, length), bf16),
            *[vmem((own if direct else 8, hidden), f32)] * 2,
            vmem((part, length), bf16),
            vmem((part, length), bf16),
            vmem((width, hidden), bf16),
            vmem((hidden, width), bf16),
            vmem((hidden, width), bf16),
            vmem((width, length), bf16),
            vmem((hidden, CHUNK), f32),
            vmem((width, length), bf16),
            vmem((hidden, length), bf16),
            vmem((hidden, length), bf16),
            vmem((width, length), bf16),
            *[vmem((part, length), f32)] * 3,
            vmem((part, length), bf16),
            *reduce_scratch(part, length),
            *reduce_scratch(part, length),
            vmem((4, 8, padded), f32),
            *[vmem((4, 8, length), f32)] * 3,
            vmem((4, 8, width), f32),
            vmem((proj_rows, length), bf16),
            vmem((part, length), f32),
            vmem((spans, heads, HEAD_ROWS, HEAD_ROWS), f32),
            vmem((8, length), f32),
            vmem((8, length), f32),
            vmem((8, length), f32),
            vmem((length, 8), f32),
            vmem((3, 8, SPAN), f32),
            vmem((part, 16), f32),
            vmem((part, 16), f32),
            vmem((part, 8), f32),
            vmem((part, 8), f32),
            vmem((ada.shape[0] - width, width), bf16),
            vmem((shard_count, 8, own_padded), f32),
            vmem((shard_count, 8, own_padded), f32),
            vmem((16, padded), bf16),
            vmem((shard_count, 16, padded), bf16),
            vmem((shard_count, own), f32),
            vmem((shard_count, own), f32),
            vmem((6, shard_count, part), f32),
            vmem((shard_count, 128), f32),
            *[halving_scratch(arrivals, arrival_rows, cut) for cut in cuts],
            *[vmem((2, own if direct else 16, cut), bf16) for cut in cuts],
            copy_sems(3 * chunks),
            copy_sems(3),
            *[copy_sems(3 * chunks)] * 10,
            copy_sems(3),
            copy_sems(2 * shard_count),
            *[copy_sems(shard_count + 2)] * 9,
            pltpu.SemaphoreType.DMA((20,)),
        ],
        compiler_params=pltpu.CompilerParams(
            collective_id=1, has_side_effects=True, vmem_limit_bytes=VMEM_LIMIT
        ),
        cost_estimate=work_for(180),
        name="layer",
    )(x, cot, silu, ada, bias, qkv, gate, gate_bias, conv, out_w, up, down, cond, label)


def finish_kernel(
    heads, tokens_ref, out_ref, class_ref, ada_ref, down_ref, up_ref, qkv_ref, out_w_ref, small_ref,
    tokens_to, out_to, class_to, ada_to, down_to, up_to, qkv_to, gate_to, out_w_to, ada_b_to, gate_b_to, conv_to,
):
    pairs = (
        (tokens_ref, tokens_to), (out_ref, out_to), (class_ref, class_to), (ada_ref, ada_to), (down_ref, down_to),
        (up_ref, up_to),
    )
    for source, target in pairs:
        target[...] = source[...]
    part = out_w_to.shape[1]
    for kind in range(3):
        qkv_to[kind] = qkv_ref[:, kind * part : (kind + 1) * part]
    gate_to[...] = jnp.transpose(qkv_ref[:, 3 * part : 3 * part + 8])[:heads]
    out_w_to[...] = out_w_ref[:, :part]
    ada_b_to[...] = small_ref[:6, :part]
    gate_b_to[...] = small_ref[15:16, part : part + heads]
    for row in range(3):
        conv_to[row] = small_ref[6 + 3 * row : 9 + 3 * row, :part]


def finish(heads, part, tokens, out, grad_class, grad_ada, grad_down, grad_up, grad_wide, grad_out_w, small):
    own = grad_wide.shape[0]
    shape = jax.ShapeDtypeStruct
    f32 = jnp.float32
    whole = (tokens, out, grad_class, grad_ada, grad_down, grad_up)
    return pl.pallas_call(
        functools.partial(finish_kernel, heads),
        out_shape=(
            *[shape(array.shape, array.dtype) for array in whole],
            shape((3, own, part), f32),
            shape((heads, own), f32),
            shape((own, part), f32),
            shape((6, part), f32),
            shape((1, heads), f32),
            shape((3, 3, part), f32),
        ),
        in_specs=[VMEM_SPEC] * 9,
        out_specs=[VMEM_SPEC] * 12,
        compiler_params=pltpu.CompilerParams(vmem_limit_bytes=VMEM_LIMIT),
        cost_estimate=work_for(5),
        name="finish",
    )(*whole, grad_wide, grad_out_w, small)


def shards(
    latent_tokens,
    timesteps,
    labels,
    class_table,
    ada_weight,
    ada_bias,
    query_key_value_weight,
    gate_weight,
    gate_bias,
    conv_weight,
    out_weight,
    up_weight,
    down_weight,
    cotangent,
):
    part = latent_tokens.shape[2]
    heads = gate_weight.shape[1]
    shard_count = lax.psum(1, "dp")
    own_width = MODEL_DIM // shard_count
    x = latent_tokens[0].T
    cot = cotangent[0].T
    qkv = jnp.transpose(query_key_value_weight, (1, 2, 0)).reshape(3 * part, MODEL_DIM)
    ada = jnp.transpose(ada_weight, (1, 2, 0)).reshape(6 * part, MODEL_DIM)
    cond = lax.dynamic_slice_in_dim(class_table, labels[0], 1, axis=0).astype(jnp.float32) + embed_time(
        timesteps, MODEL_DIM
    )
    silu = jnp.broadcast_to(low(jax.nn.silu(cond)), (8, MODEL_DIM))
    direct = shard_count == 8 and own_width % 16 == 0
    grad_tokens, layer_out, grad_down, grad_up, grad_wide, grad_out_w, grad_class, grad_ada_w, small, _, _ = layer(
        x, cot, silu, ada, ada_bias, qkv, gate_weight.T, gate_bias[None], conv_weight, out_weight, up_weight,
        down_weight, cond, labels.astype(jnp.float32)[None], shard_count, heads, direct,
    )
    if not direct:
        grad_down, grad_up, grad_wide, grad_out_w = (
            lax.psum_scatter(partial, "dp", scatter_dimension=0, tiled=True).astype(jnp.float32)
            for partial in (grad_down, grad_up, grad_wide, grad_out_w)
        )
    (
        grad_tokens, layer_out, grad_class, grad_ada_w, grad_down, grad_up, grad_qkv, grad_gate_w, grad_out_w,
        grad_ada_b, grad_gate_b, grad_conv,
    ) = finish(
        heads, part, grad_tokens, layer_out, grad_class, grad_ada_w, grad_down, grad_up, grad_wide, grad_out_w, small
    )
    return (
        layer_out.T[None],
        grad_tokens.T[None],
        grad_class.T,
        jnp.transpose(grad_ada_w, (1, 0, 2)),
        grad_ada_b,
        jnp.transpose(grad_qkv, (1, 0, 2)),
        grad_gate_w.T,
        grad_gate_b[0],
        grad_conv,
        grad_out_w.T,
        grad_up,
        grad_down.T,
    )


def solution(mesh):
    in_specs = (
        P("dp", None, "tensor"),
        P("dp"),
        P("dp"),
        P(),
        P(None, None, "tensor"),
        P(None, "tensor"),
        P(None, None, "tensor"),
        P(None, "tensor"),
        P("tensor"),
        P(None, None, "tensor"),
        P("tensor", None),
        P(None, "tensor"),
        P("tensor", None),
        P("dp", None, "tensor"),
    )
    out_specs = (
        P("dp", None, "tensor"),
        P("dp", None, "tensor"),
        P(None, "dp"),
        P("dp", None, "tensor"),
        P(None, "tensor"),
        P("dp", None, "tensor"),
        P("dp", "tensor"),
        P("tensor"),
        P(None, None, "tensor"),
        P("tensor", "dp"),
        P("dp", "tensor"),
        P("tensor", "dp"),
    )
    return jax.shard_map(shards, mesh=mesh, in_specs=in_specs, out_specs=out_specs, check_vma=False)
```
